512 devices in a mesh: region: 16 (over z, core), row: 32 (over x, y).
Axes of the slice: x: 4, y: 8, z: 8, core: 2. Of those that a mesh axis runs over, the one named last changes fastest.
Arguments:
- queries: float32 [64, 512], P('row'), may hold values from -6 to 6
- descriptors: float32 [131072, 512], P(('region', 'row')), may hold values from -6 to 6
- candidates: int32 [64, 64], replicated, may hold values from 0 to 1023
- cluster_perm: int32 [16, 8192], P('region', 'row'), may hold values from 0 to 8191, each once within a row
- tile_vals: float32 [6144, 128, 128], P(('region', 'row')), may hold values from 0 to 1, as said below
- tile_row: int32 [6144], P(('region', 'row')), may hold values from 0 to 1, as said below
- tile_col: int32 [6144], P(('region', 'row')), may hold values from 0 to 67, as said below
Outputs:
- diffused: float32 [64, 131072], P(None, ('region', 'row'))
- residual: float32 [64, 131072], P(None, ('region', 'row'))
The draws below stay inside these ranges and needn't reach their ends.
Inputs may be any that keep to these rules, and one draw needn't show every extreme that they name: Each row of cluster_perm names every storage position of its region once. tile_row is a row tile of the owning device. In device (region r, row index i) the first 2 tiles are its diagonal tiles in order; the intra-region column tiles lie on row indices i, i + 1, i - 1, i + 3, i - 3, i + 8, i - 8 and i + 32 // 2 (modulo 32). `tile_col`: every device holds tiles with column slots in both neighbouring regions. `tile_vals`: S is symmetric with nonnegative entries and every row of S sums to at most 1.
All inputs are finite; a program needn't handle non-finite values.
Results may differ from the reference program's by a relative error of at most 0.0003.
Values sent between devices are 32-bit elements; how exact they have to be, the bound alone decides.
No kernel may reach another device: no remote copies, remote signals or barrier semaphores. Data moves between devices by JAX's collectives and lax.ppermute only.
A program may use at most 64 MiB of HBM per device.

```python
import jax
import jax.numpy as jnp
from jax import lax

D = 512
Q = 64
K = 64
TILE = 128
ITERS = 3
ROWS_DEV = 256
TILES_DEV = 12
REG_ROWS = 8192
ROWS_ALL = 131072
BLOCKS = 1024
TILES_ALL = 6144
N_REGION = 16
N_ROW = 32


def tile_layout(key):
    per_device = ROWS_DEV // TILE
    hop_list = [1, 3, N_ROW // 4, N_ROW // 2]
    fore_rows = jax.random.randint(jax.random.fold_in(key, 101), (N_REGION, N_ROW, 4), 0, per_device, dtype=jnp.int32)
    fore_cols = jax.random.randint(jax.random.fold_in(key, 102), (N_REGION, N_ROW, 4), 0, per_device, dtype=jnp.int32)
    cross_rows = jax.random.randint(jax.random.fold_in(key, 103), (N_REGION, N_ROW), 0, per_device, dtype=jnp.int32)
    cross_cols = jax.random.randint(jax.random.fold_in(key, 104), (N_REGION, N_ROW), 0, per_device, dtype=jnp.int32)
    region_ids = jnp.arange(N_REGION, dtype=jnp.int32)[:, None]
    device_ids = jnp.arange(N_ROW, dtype=jnp.int32)[None, :]
    region_span = N_ROW * per_device
    row_list = []
    col_list = []
    for diag_slot in range(per_device):
        row_list.append(jnp.full((N_REGION, N_ROW), diag_slot, jnp.int32))
        col_list.append(jnp.broadcast_to(device_ids * per_device + diag_slot, (N_REGION, N_ROW)).astype(jnp.int32))
    for slot_m, hop_size in enumerate(hop_list):
        row_list.append(fore_rows[:, :, slot_m])
        col_list.append((device_ids + hop_size) % N_ROW * per_device + fore_cols[:, :, slot_m])
        source = (device_ids - hop_size) % N_ROW
        row_list.append(fore_cols[region_ids, source, slot_m])
        col_list.append(source * per_device + fore_rows[region_ids, source, slot_m])
    row_list.append(cross_rows)
    col_list.append(region_span + per_device + cross_cols)
    region_below = (region_ids - 1) % N_REGION
    row_list.append(cross_cols[region_below, device_ids])
    col_list.append(region_span + cross_rows[region_below, device_ids])
    rows_out = jnp.stack(row_list, axis=2).reshape(-1).astype(jnp.int32)
    cols_out = jnp.stack(col_list, axis=2).reshape(-1).astype(jnp.int32)
    return (rows_out, cols_out)


def draw_tile_row(key, part):
    return tile_layout(key)[0]


def draw_tile_col(key, part):
    return tile_layout(key)[1]


def draw_tile_vals(key, part):
    per_device = ROWS_DEV // TILE
    hop_list = [1, 3, N_ROW // 4, N_ROW // 2]
    limit = 1.0 / (TILES_DEV * TILE)

    def entries(index, shape):
        values = jax.random.uniform(jax.random.fold_in(key, index), shape, jnp.float32)
        return values * limit
    diag_raw = entries(201, (N_REGION, N_ROW, per_device, TILE, TILE))
    diag_sym = 0.5 * (diag_raw + jnp.swapaxes(diag_raw, -1, -2))
    fore_vals = entries(202, (N_REGION, N_ROW, 4, TILE, TILE))
    cross_vals = entries(203, (N_REGION, N_ROW, TILE, TILE))
    region_ids = jnp.arange(N_REGION, dtype=jnp.int32)[:, None]
    device_ids = jnp.arange(N_ROW, dtype=jnp.int32)[None, :]
    tile_list = []
    for diag_slot in range(per_device):
        tile_list.append(diag_sym[:, :, diag_slot])
    for slot_m, hop_size in enumerate(hop_list):
        tile_list.append(fore_vals[:, :, slot_m])
        source = (device_ids - hop_size) % N_ROW
        tile_list.append(jnp.swapaxes(fore_vals[region_ids, source, slot_m], -1, -2))
    tile_list.append(cross_vals)
    region_below = (region_ids - 1) % N_REGION
    tile_list.append(jnp.swapaxes(cross_vals[region_below, device_ids], -1, -2))
    return jnp.stack(tile_list, axis=2).reshape(-1, TILE, TILE).astype(jnp.float32)


def set_ends(drawn, stream_key, least, top_value):
    index_at = [jax.random.randint(jax.random.fold_in(stream_key, axis), (), 0, length) for axis, length in enumerate(drawn.shape)]
    main_axis = drawn.shape.index(max(drawn.shape))
    beside = index_at[:main_axis] + [(index_at[main_axis] + 1) % drawn.shape[main_axis]] + index_at[main_axis + 1:]
    return drawn.at[tuple(index_at)].set(least).at[tuple(beside)].set(top_value)


def steps_of(stream_key, dims, pieces, low, top_value):
    factor_of = 1.0
    for position, shards_of in pieces:
        steps = jax.random.uniform(jax.random.fold_in(jax.random.fold_in(stream_key, 6), position), (shards_of,), jnp.float32, low / len(pieces), top_value / len(pieces))
        factor_of = factor_of * jnp.repeat(jnp.exp(steps), dims[position] // shards_of).reshape((-1,) + (1,) * (len(dims) - 1 - position))
    return factor_of


def scatter_about(own_key, dims, deviation, most, cuts=(), held_as=jnp.bfloat16):
    result = deviation * jax.random.normal(own_key, dims, jnp.float32)
    if cuts:
        result = result * steps_of(own_key, dims, cuts, -0.22, 0.18)
    return jnp.clip(result, -most, most).astype(held_as)


def setup_inputs(seed: int = 0) -> dict:
    key_list = jax.random.split(jax.random.key(seed), 8)
    queries = scatter_about(key_list[0], (Q, D), 1.0, 6.0, ((0, 32),), jnp.float32)
    descriptors = scatter_about(key_list[1], (ROWS_ALL, D), 1.0, 6.0, ((0, 512),), jnp.float32)
    candidates = set_ends(jax.random.randint(key_list[2], (Q, K), 0, BLOCKS), jax.random.fold_in(key_list[2], 1), 0, BLOCKS - 1).astype(jnp.int32)
    cluster_perm = jax.vmap(lambda own: jax.random.permutation(own, REG_ROWS))(jax.random.split(key_list[3], N_REGION)).reshape((N_REGION, REG_ROWS)).astype(jnp.int32)
    tile_vals = draw_tile_vals(jax.random.fold_in(key_list[7], 71), 0)
    tile_row = draw_tile_row(jax.random.fold_in(key_list[7], 71), 0)
    tile_col = draw_tile_col(jax.random.fold_in(key_list[7], 71), 0)
    return {"queries": queries, "descriptors": descriptors, "candidates": candidates, "cluster_perm": cluster_perm, "tile_vals": tile_vals, "tile_row": tile_row, "tile_col": tile_col}


def apply_operator(field, tile_vals, global_rows, global_cols):
    blocked = field.reshape(Q, BLOCKS, TILE)
    picked = blocked[:, global_cols, :]
    products = jnp.einsum('qtc,trc->tqr', picked, tile_vals, precision=lax.Precision.HIGHEST)
    summed = jax.ops.segment_sum(products, global_rows, num_segments=BLOCKS)
    return field - 0.9 * summed.transpose(1, 0, 2).reshape(Q, ROWS_ALL)

def reference(queries, descriptors, candidates, cluster_perm, tile_vals, tile_row, tile_col):
    scores = lax.dot_general(queries, descriptors, (((1,), (1,)), ((), ())), precision=lax.Precision.HIGHEST, preferred_element_type=jnp.float32) * (1.0 / jnp.sqrt(jnp.float32(D)))
    block_ids = jnp.arange(BLOCKS, dtype=jnp.int32)
    member = jnp.any(candidates[:, :, None] == block_ids[None, None, :], axis=1)
    member_rows = jnp.repeat(member, TILE, axis=1)
    stored = jnp.where(member_rows, jnp.exp(scores), jnp.float32(0.0))
    by_region = stored.reshape(Q, N_REGION, REG_ROWS)
    seeds = jnp.take_along_axis(by_region, cluster_perm[None, :, :], axis=2).reshape(Q, ROWS_ALL)
    per_device = ROWS_DEV // TILE
    region_span = N_ROW * per_device
    entry = jnp.arange(TILES_ALL, dtype=jnp.int32)
    device_id = entry // TILES_DEV
    region_id = device_id // N_ROW
    row_index = device_id % N_ROW
    base_low = ((region_id - 1) % N_REGION * N_ROW + row_index) * per_device
    base_up = ((region_id + 1) % N_REGION * N_ROW + row_index) * per_device
    global_cols = jnp.where(tile_col < region_span, region_id * region_span + tile_col, jnp.where(tile_col < region_span + per_device, base_low + tile_col - region_span, base_up + tile_col - region_span - per_device)).astype(jnp.int32)
    global_rows = (device_id * per_device + tile_row).astype(jnp.int32)
    diffused = jnp.zeros_like(seeds)
    residual = seeds
    direction = seeds
    norm_now = lax.optimization_barrier(jnp.sum(residual * residual, axis=1))
    for step in range(ITERS):
        image = apply_operator(direction, tile_vals, global_rows, global_cols)
        alpha = norm_now / lax.optimization_barrier(jnp.sum(direction * image, axis=1))
        diffused = diffused + alpha[:, None] * direction
        residual = residual - alpha[:, None] * image
        norm_next = lax.optimization_barrier(jnp.sum(residual * residual, axis=1))
        direction = residual + (norm_next / norm_now)[:, None] * direction
        norm_now = norm_next
    return (diffused, residual)
```

```python
import functools

import jax
import jax.numpy as jnp
from jax import lax
from jax.experimental import pallas as pl
from jax.experimental.pallas import tpu as pltpu
from jax.sharding import PartitionSpec as P

Q = 64
D = 512
TILE = 128
HALF = 2
ROWS = TILE * HALF
N_ROW = 32
N_REGION = 16
QS = Q // N_ROW
HOPS = (0, 1, -1, 3, -3, 8, -8, 16)
SLOTS = len(HOPS) + 2
HIGHEST = lax.Precision.HIGHEST
F32 = jnp.float32
TAU = 1.0 / 0.9


def ring(count, hop):
    return [(i, (i + hop) % count) for i in range(count)]


def scores_kernel(dev_ref, queries_ref, desc_ref, cand_ref, out_ref):
    scores = lax.dot_general(
        queries_ref[...], desc_ref[...], (((1,), (1,)), ((), ())),
        precision=HIGHEST, preferred_element_type=F32,
    ) * (1.0 / (D ** 0.5))
    stored = jnp.exp(scores)
    cand = cand_ref[...]
    for h in range(HALF):
        hit = jnp.where(cand == dev_ref[0] * HALF + h, 1.0, 0.0)
        member = jnp.max(hit, axis=1, keepdims=True) > 0.5
        out_ref[:, h * TILE:(h + 1) * TILE] = jnp.where(member, stored[:, h * TILE:(h + 1) * TILE], 0.0)


def permute_kernel(table_ref, perm_ref, out_ref, graph_ref):
    rows = N_ROW * HALF
    perm = perm_ref[...].astype(jnp.int32)
    groups = rows // 8
    low = [perm[g * 8:(g + 1) * 8] & (TILE - 1) for g in range(groups)]
    high = [perm[g * 8:(g + 1) * 8] >> 7 for g in range(groups)]

    def body(sender, acc):
        block = table_ref[sender]
        acc = [list(a) for a in acc]
        for h in range(HALF):
            hits = [high[g] == sender * HALF + h for g in range(groups)]
            for q in range(QS):
                line = jnp.broadcast_to(block[q * HALF + h][None, :], (8, TILE))
                for g in range(groups):
                    got = jnp.take_along_axis(line, low[g], axis=1)
                    acc[q][g] = jnp.where(hits[g], got, acc[q][g])
        return tuple(tuple(a) for a in acc)

    zero = tuple(tuple(jnp.zeros((8, TILE), F32) for _ in range(groups)) for _ in range(QS))
    acc = lax.fori_loop(0, N_ROW, body, zero)
    for q in range(QS):
        for g in range(groups):
            graph_ref[q, g * 8:(g + 1) * 8, :] = acc[q][g]
    width = len(HOPS) * QS * HALF
    for q in range(QS):
        for h in range(HALF):
            mine = graph_ref[q, pl.ds(h, N_ROW, stride=HALF), :]
            for k, hop in enumerate(HOPS):
                hop = hop % N_ROW
                rolled = mine if hop == 0 else jnp.concatenate([mine[hop:], mine[:hop]], axis=0)
                out_ref[pl.ds((k * QS + q) * HALF + h, N_ROW, stride=width), :] = rolled


def tile_slot(col, row_index):
    owner = col >> 1
    hop = (owner - row_index) & (N_ROW - 1)
    slot = jnp.int32(0)
    for k, h in enumerate(HOPS):
        slot = jnp.where(hop == h % N_ROW, k, slot)
    slot = slot * HALF + (col & 1)
    return jnp.where(col >= N_ROW * HALF, col - N_ROW * HALF + len(HOPS) * HALF, slot)


def multiply(place_ref, row_ref, col_ref, tiles_ref, slots_ref, acc_ref):
    acc_ref[...] = jnp.zeros_like(acc_ref)
    for t in range(tiles_ref.shape[0]):
        slot = tile_slot(col_ref[t], place_ref[0])
        part = lax.dot_general(
            slots_ref[slot], tiles_ref[t], (((1,), (1,)), ((), ())),
            precision=HIGHEST, preferred_element_type=F32,
        )
        acc_ref[row_ref[t]] += part


def spread(slots_ref, k, block_ref):
    for h in range(HALF):
        slots_ref[k * HALF + h] = block_ref[:, h * TILE:(h + 1) * TILE]


def first_kernel(place_ref, row_ref, col_ref, near_ref, low_ref, high_ref, tiles_ref, out_ref, slots_ref, acc_ref):
    width = len(HOPS) * QS * HALF
    for k in range(len(HOPS)):
        for h in range(HALF):
            for q in range(QS):
                slots_ref[k * HALF + h, q * N_ROW:(q + 1) * N_ROW, :] = near_ref[
                    pl.ds((k * QS + q) * HALF + h, N_ROW, stride=width), :]
    spread(slots_ref, len(HOPS), low_ref)
    spread(slots_ref, len(HOPS) + 1, high_ref)
    multiply(place_ref, row_ref, col_ref, tiles_ref, slots_ref, acc_ref)
    for h in range(HALF):
        out_ref[:, h * TILE:(h + 1) * TILE] = acc_ref[h]


def next_kernel(place_ref, row_ref, col_ref, *refs):
    blocks, (tiles_ref, out_ref, slots_ref, acc_ref) = refs[:SLOTS], refs[SLOTS:]
    for k, block in enumerate(blocks):
        spread(slots_ref, k, block)
    multiply(place_ref, row_ref, col_ref, tiles_ref, slots_ref, acc_ref)
    for h in range(HALF):
        out_ref[:, h * TILE:(h + 1) * TILE] = acc_ref[h]


def last_kernel(place_ref, row_ref, col_ref, *refs):
    blocks = refs[:SLOTS]
    v0_ref, v1_ref, tiles_ref, out_ref, moments_ref, slots_ref, acc_ref = refs[SLOTS:]
    next_kernel(place_ref, row_ref, col_ref, *blocks, tiles_ref, out_ref, slots_ref, acc_ref)
    vs = [v0_ref[...], v1_ref[...], blocks[0][...], out_ref[...]]
    lane = lax.broadcasted_iota(jnp.int32, (Q, TILE), 1)
    packed = [jnp.zeros((Q, TILE), F32), jnp.zeros((Q, TILE), F32)]
    for m in range(6):
        prod = vs[m // 2] * vs[(m + 1) // 2]
        total = jnp.sum(prod[:, :TILE] + prod[:, TILE:], axis=1, keepdims=True)
        packed[m % 2] = jnp.where(lane == m // 2, total, packed[m % 2])
    moments_ref[...] = jnp.concatenate(packed, axis=0).T[:4]


def finish_kernel(moments_ref, v0_ref, v1_ref, v2_ref, v3_ref, diffused_ref, residual_ref):
    parts = [moments_ref[r] for r in range(N_REGION)]
    while len(parts) > 1:
        parts = [a + b for a, b in zip(parts[::2], parts[1::2])]
    square = jnp.concatenate([parts[0], jnp.zeros((TILE - 4, TILE), F32)], axis=0).T
    m = [square[(k % 2) * Q:(k % 2 + 1) * Q, k // 2:k // 2 + 1] for k in range(6)]
    g = [None] + [x / m[0] for x in m[1:]]
    d11 = g[2] - g[1] * g[1]
    d12 = g[3] - g[1] * g[2]
    d22 = g[4] - g[2] * g[2]
    f1 = g[4] - g[1] * g[3]
    f2 = g[5] - g[2] * g[3]
    ratio = d12 / d11
    c2 = -(f2 - ratio * f1) / (d22 - ratio * d12)
    c1 = -(f1 + d12 * c2) / d11
    c0 = -(g[3] + g[1] * c1 + g[2] * c2)
    e1 = TAU + c2
    e0 = e1 * TAU + c1
    scale = 1.0 / (e0 * TAU + c0)
    v0, v1, v2 = v0_ref[...], v1_ref[...], v2_ref[...]
    diffused_ref[...] = (TAU * scale) * (v2 + e1 * v1 + e0 * v0)
    residual_ref[...] = scale * (v3_ref[...] + c2 * v2 + c1 * v1 + c0 * v0)


SMEM = pl.BlockSpec(memory_space=pltpu.SMEM)
VMEM = pl.BlockSpec(memory_space=pltpu.VMEM)
PARAMS = pltpu.CompilerParams(vmem_limit_bytes=32 * 1024 * 1024)


def shape(*dims):
    return jax.ShapeDtypeStruct(dims, F32)


def local(queries, descriptors, candidates, cluster_perm, tile_vals, tile_row, tile_col):
    row_index = lax.axis_index("row").astype(jnp.int32)
    place = row_index[None]
    device = (lax.axis_index("region").astype(jnp.int32) * N_ROW + row_index)[None]

    own = jnp.concatenate([queries, cluster_perm.reshape(HALF, TILE).astype(F32)], axis=1)
    all_own = lax.all_to_all(jnp.broadcast_to(own[None], (N_ROW,) + own.shape), "row", 0, 0, tiled=True)
    all_own = all_own.reshape(Q, D + TILE)
    stored = pl.pallas_call(
        scores_kernel, out_shape=shape(Q, ROWS), in_specs=[SMEM, VMEM, VMEM, VMEM], out_specs=VMEM,
        compiler_params=PARAMS, name="scores",
    )(device, all_own[:, :D], descriptors, candidates)
    by_query = stored.reshape(QS, N_ROW, HALF, TILE).transpose(1, 0, 2, 3).reshape(N_ROW, QS * HALF, TILE)
    table = lax.all_to_all(by_query, "row", 0, 0, tiled=True)
    width = len(HOPS) * QS * HALF
    near = pl.pallas_call(
        permute_kernel, out_shape=shape(N_ROW * width, TILE), in_specs=[VMEM, VMEM], out_specs=VMEM,
        scratch_shapes=[pltpu.VMEM((QS, N_ROW * HALF, TILE), F32)],
        compiler_params=PARAMS, name="permute",
    )(table, all_own[:, D:])
    near = lax.all_to_all(near.reshape(N_ROW, width, TILE), "row", 0, 0, tiled=True)
    v0 = near[:, :QS * HALF].reshape(N_ROW, QS, HALF, TILE).transpose(1, 0, 2, 3).reshape(Q, ROWS)

    def region_pair(v):
        return (lax.ppermute(v, "region", ring(N_REGION, 1)), lax.ppermute(v, "region", ring(N_REGION, -1)))

    def exchange(v):
        low, high = region_pair(v)
        return [v] + [lax.ppermute(v, "row", ring(N_ROW, -hop)) for hop in HOPS[1:]] + [low, high]

    scratch = [pltpu.VMEM((SLOTS * HALF, Q, TILE), F32), pltpu.VMEM((HALF, Q, TILE), F32)]
    low, high = region_pair(v0)
    v1 = pl.pallas_call(
        first_kernel, out_shape=shape(Q, ROWS), in_specs=[SMEM] * 3 + [VMEM] * 4, out_specs=VMEM,
        scratch_shapes=scratch, compiler_params=PARAMS, name="first",
    )(place, tile_row, tile_col, near.reshape(N_ROW * width, TILE), low, high, tile_vals)
    v2 = pl.pallas_call(
        next_kernel, out_shape=shape(Q, ROWS), in_specs=[SMEM] * 3 + [VMEM] * (SLOTS + 1), out_specs=VMEM,
        scratch_shapes=scratch, compiler_params=PARAMS, name="second",
    )(place, tile_row, tile_col, *exchange(v1), tile_vals)
    v3, moments = pl.pallas_call(
        last_kernel, out_shape=(shape(Q, ROWS), shape(4, TILE)),
        in_specs=[SMEM] * 3 + [VMEM] * (SLOTS + 3), out_specs=(VMEM, VMEM),
        scratch_shapes=scratch, compiler_params=PARAMS, name="third",
    )(place, tile_row, tile_col, *exchange(v2), v0, v1, tile_vals)

    moments = lax.all_to_all(jnp.broadcast_to(moments[None], (N_ROW, 4, TILE)), "row", 0, 0, tiled=True)
    moments = jnp.sum(moments.reshape(2, 2, 2, 2, 2, 4, TILE).sum(0).sum(0).sum(0).sum(0), axis=0)
    moments = lax.all_to_all(jnp.broadcast_to(moments[None], (N_REGION, 4, TILE)), "region", 0, 0, tiled=True)
    diffused, residual = pl.pallas_call(
        finish_kernel, out_shape=(shape(Q, ROWS), shape(Q, ROWS)), in_specs=[VMEM] * 5, out_specs=(VMEM, VMEM),
        compiler_params=PARAMS, name="finish",
    )(moments, v0, v1, v2, v3)
    return (diffused, residual)


def solution(mesh):
    in_specs = (
        P("row", None),
        P(("region", "row"), None),
        P(),
        P("region", "row"),
        P(("region", "row"), None, None),
        P(("region", "row")),
        P(("region", "row")),
    )
    out_specs = (P(None, ("region", "row")), P(None, ("region", "row")))
    return jax.shard_map(local, mesh=mesh, in_specs=in_specs, out_specs=out_specs, check_vma=False)
```

```python
import jax
import jax.numpy as jnp
from jax import lax
from jax.experimental import pallas as pl
from jax.experimental.pallas import tpu as pltpu
from jax.sharding import PartitionSpec as P

Q = 64
D = 512
TILE = 128
HALF = 2
ROWS = TILE * HALF
N_ROW = 32
N_REGION = 16
QS = Q // N_ROW
HOPS = (0, 3, 8, 1, -3, -8, -1, 16)
SLOTS = len(HOPS) + 2
HIGHEST = lax.Precision.HIGHEST
F32 = jnp.float32
TAU = 1.0 / 0.9


def ring(count, hop):
    return [(i, (i + hop) % count) for i in range(count)]


def pack_kernel(queries_ref, perm_ref, out_ref):
    perm = perm_ref[...].astype(F32)
    out_ref[:, :, :D] = jnp.broadcast_to(queries_ref[...][None], (N_ROW, QS, D))
    for h in range(HALF):
        out_ref[:, h:h + 1, D:] = jnp.broadcast_to(perm[:, h * TILE:(h + 1) * TILE][None], (N_ROW, 1, TILE))


def scores_kernel(dev_ref, packed_ref, desc_ref, cand_ref, out_ref):
    scores = lax.dot_general(
        packed_ref[:, :D], desc_ref[...], (((1,), (1,)), ((), ())),
        precision=HIGHEST, preferred_element_type=F32,
    ) * (1.0 / (D ** 0.5))
    stored = jnp.exp(scores)
    cand = cand_ref[...]
    for h in range(HALF):
        hit = jnp.where(cand == dev_ref[0] * HALF + h, 1.0, 0.0)
        member = jnp.max(hit, axis=1, keepdims=True) > 0.5
        kept = jnp.where(member, stored[:, h * TILE:(h + 1) * TILE], 0.0)
        for q in range(QS):
            out_ref[pl.ds(q * HALF + h, N_ROW, stride=QS * HALF), :] = kept[q * N_ROW:(q + 1) * N_ROW]


def permute_kernel(table_ref, packed_ref, out_ref, graph_ref):
    rows = N_ROW * HALF
    perm = packed_ref[:, D:].astype(jnp.int32)
    groups = rows // 8
    low = [perm[g * 8:(g + 1) * 8] & (TILE - 1) for g in range(groups)]
    high = [perm[g * 8:(g + 1) * 8] >> 7 for g in range(groups)]

    def body(sender, acc):
        acc = [list(a) for a in acc]
        for h in range(HALF):
            hits = [high[g] == sender * HALF + h for g in range(groups)]
            for q in range(QS):
                line = jnp.broadcast_to(table_ref[pl.ds(sender * (QS * HALF) + q * HALF + h, 1), :], (8, TILE))
                for g in range(groups):
                    got = jnp.take_along_axis(line, low[g], axis=1)
                    acc[q][g] = jnp.where(hits[g], got, acc[q][g])
        return tuple(tuple(a) for a in acc)

    zero = tuple(tuple(jnp.zeros((8, TILE), F32) for _ in range(groups)) for _ in range(QS))
    acc = lax.fori_loop(0, N_ROW, body, zero)
    for q in range(QS):
        for g in range(groups):
            graph_ref[q, g * 8:(g + 1) * 8, :] = acc[q][g]
    width = len(HOPS) * QS * HALF
    for q in range(QS):
        for h in range(HALF):
            mine = graph_ref[q, pl.ds(h, N_ROW, stride=HALF), :]
            for k, hop in enumerate(HOPS):
                hop = hop % N_ROW
                rolled = mine if hop == 0 else jnp.concatenate([mine[hop:], mine[:hop]], axis=0)
                out_ref[pl.ds((k * QS + q) * HALF + h, N_ROW, stride=width), :] = rolled


def tile_slot(col, place_ref):
    hop = (((col >> 1) - place_ref[0]) * place_ref[1]) & (N_ROW - 1)
    slot = jnp.int32(0)
    for k, h in enumerate(HOPS):
        slot = jnp.where(hop == h % N_ROW, k, slot)
    slot = slot * HALF + (col & 1)
    return jnp.where(col >= N_ROW * HALF, col - N_ROW * HALF + len(HOPS) * HALF, slot)


def product(slots_ref, slot, tiles_ref, t):
    return lax.dot_general(
        slots_ref[slot], tiles_ref[t], (((1,), (1,)), ((), ())), precision=HIGHEST, preferred_element_type=F32,
    )


def spread(slots_ref, k, block):
    for h in range(HALF):
        slots_ref[k * HALF + h] = block[:, h * TILE:(h + 1) * TILE]


def inner_kernel(place_ref, row_ref, col_ref, near_ref, tiles_ref, out_ref, slots_ref):
    width = len(HOPS) * QS * HALF
    for k in range(len(HOPS)):
        for h in range(HALF):
            for q in range(QS):
                slots_ref[k * HALF + h, q * N_ROW:(q + 1) * N_ROW, :] = near_ref[
                    pl.ds((k * QS + q) * HALF + h, N_ROW, stride=width), :]
    out_ref[...] = jnp.zeros_like(out_ref)
    for t in range(tiles_ref.shape[0]):
        @pl.when(col_ref[t] < N_ROW * HALF)
        def _():
            out_ref[row_ref[t]] += product(slots_ref, tile_slot(col_ref[t], place_ref), tiles_ref, t)


def outer_kernel(row_ref, col_ref, inner_ref, low_ref, high_ref, tiles_ref, out_ref, slots_ref, acc_ref):
    spread(slots_ref, 0, low_ref[...])
    spread(slots_ref, 1, high_ref[...])
    acc_ref[...] = inner_ref[...]
    for t in range(tiles_ref.shape[0]):
        @pl.when(col_ref[t] >= N_ROW * HALF)
        def _():
            acc_ref[row_ref[t]] += product(slots_ref, col_ref[t] - N_ROW * HALF, tiles_ref, t)
    for h in range(HALF):
        out_ref[:, h * TILE:(h + 1) * TILE] = acc_ref[h]


N_BLOCKS = 8


def next_kernel(place_ref, row_ref, col_ref, *refs):
    own, a_ref, b_ref, c_ref, swapped_ref, far_ref, low_ref, high_ref = refs[:N_BLOCKS]
    tiles_ref, out_ref, slots_ref, acc_ref = refs[N_BLOCKS:]
    blocks = [own[...], a_ref[0], b_ref[0], c_ref[0], swapped_ref[0], swapped_ref[1], swapped_ref[2],
              far_ref[...], low_ref[...], high_ref[...]]
    for k, block in enumerate(blocks):
        spread(slots_ref, k, block)
    acc_ref[...] = jnp.zeros_like(acc_ref)
    for t in range(tiles_ref.shape[0]):
        acc_ref[row_ref[t]] += product(slots_ref, tile_slot(col_ref[t], place_ref), tiles_ref, t)
    for h in range(HALF):
        out_ref[:, h * TILE:(h + 1) * TILE] = acc_ref[h]


def last_kernel(place_ref, row_ref, col_ref, *refs):
    blocks = refs[:N_BLOCKS]
    v0_ref, v1_ref, tiles_ref, out_ref, moments_ref, slots_ref, acc_ref = refs[N_BLOCKS:]
    next_kernel(place_ref, row_ref, col_ref, *blocks, tiles_ref, out_ref, slots_ref, acc_ref)
    vs = [v0_ref[...], v1_ref[...], blocks[0][...], out_ref[...]]
    lane = lax.broadcasted_iota(jnp.int32, (Q, TILE), 1)
    packed = [jnp.zeros((Q, TILE), F32), jnp.zeros((Q, TILE), F32)]
    for m in range(6):
        prod = vs[m // 2] * vs[(m + 1) // 2]
        total = jnp.sum(prod[:, :TILE] + prod[:, TILE:], axis=1, keepdims=True)
        packed[m % 2] = jnp.where(lane == m // 2, total, packed[m % 2])
    moments_ref[...] = jnp.concatenate(packed, axis=0).T[:4]


def finish_kernel(moments_ref, v0_ref, v1_ref, v2_ref, v3_ref, diffused_ref, residual_ref):
    parts = [moments_ref[r] for r in range(N_REGION)]
    while len(parts) > 1:
        parts = [a + b for a, b in zip(parts[::2], parts[1::2])]
    square = jnp.concatenate([parts[0], jnp.zeros((TILE - 4, TILE), F32)], axis=0).T
    m = [square[(k % 2) * Q:(k % 2 + 1) * Q, k // 2:k // 2 + 1] for k in range(6)]
    g = [None] + [x / m[0] for x in m[1:]]
    d11 = g[2] - g[1] * g[1]
    d12 = g[3] - g[1] * g[2]
    d22 = g[4] - g[2] * g[2]
    f1 = g[4] - g[1] * g[3]
    f2 = g[5] - g[2] * g[3]
    ratio = d12 / d11
    c2 = -(f2 - ratio * f1) / (d22 - ratio * d12)
    c1 = -(f1 + d12 * c2) / d11
    c0 = -(g[3] + g[1] * c1 + g[2] * c2)
    e1 = TAU + c2
    e0 = e1 * TAU + c1
    scale = 1.0 / (e0 * TAU + c0)
    v0, v1, v2 = v0_ref[...], v1_ref[...], v2_ref[...]
    diffused_ref[...] = (TAU * scale) * (v2 + e1 * v1 + e0 * v0)
    residual_ref[...] = scale * (v3_ref[...] + c2 * v2 + c1 * v1 + c0 * v0)


SMEM = pl.BlockSpec(memory_space=pltpu.SMEM)
VMEM = pl.BlockSpec(memory_space=pltpu.VMEM)
PARAMS = pltpu.CompilerParams(vmem_limit_bytes=32 * 1024 * 1024)


def shape(*dims):
    return jax.ShapeDtypeStruct(dims, F32)


def local(queries, descriptors, candidates, cluster_perm, tile_vals, tile_row, tile_col):
    row_index = lax.axis_index("row").astype(jnp.int32)
    region = lax.axis_index("region").astype(jnp.int32)
    core = region & 1
    device = (region * N_ROW + row_index)[None]
    place = jnp.stack([row_index, 1 - 2 * core])
    upward = jnp.stack([row_index, jnp.int32(1)])

    packed = pl.pallas_call(
        pack_kernel, out_shape=shape(N_ROW, QS, D + TILE), in_specs=[VMEM, VMEM], out_specs=VMEM,
        compiler_params=PARAMS, name="pack",
    )(queries, cluster_perm)
    packed = lax.all_to_all(packed, "row", 0, 0, tiled=True).reshape(Q, D + TILE)
    by_query = pl.pallas_call(
        scores_kernel, out_shape=shape(N_ROW * QS * HALF, TILE), in_specs=[SMEM, VMEM, VMEM, VMEM], out_specs=VMEM,
        compiler_params=PARAMS, name="scores",
    )(device, packed, descriptors, candidates)
    table = lax.all_to_all(by_query.reshape(N_ROW, QS * HALF, TILE), "row", 0, 0, tiled=True)
    width = len(HOPS) * QS * HALF
    near = pl.pallas_call(
        permute_kernel, out_shape=shape(N_ROW * width, TILE), in_specs=[VMEM, VMEM], out_specs=VMEM,
        scratch_shapes=[pltpu.VMEM((QS, N_ROW * HALF, TILE), F32)],
        compiler_params=PARAMS, name="permute",
    )(table.reshape(N_ROW * QS * HALF, TILE), packed)
    near = lax.all_to_all(near.reshape(N_ROW, width, TILE), "row", 0, 0, tiled=True)
    v0 = near[:, :QS * HALF].reshape(N_ROW, QS, HALF, TILE).transpose(1, 0, 2, 3).reshape(Q, ROWS)

    def region_pair(v):
        return (lax.ppermute(v, "region", ring(N_REGION, 1)), lax.ppermute(v, "region", ring(N_REGION, -1)))

    def exchange(v):
        low, high = region_pair(v)
        far = lax.ppermute(v, "row", ring(N_ROW, 16))
        both = jnp.stack([v, jnp.where(core == 0, high, low)])
        got = []
        for hop in HOPS[1:4]:
            pairs = [(r * N_ROW + i, r * N_ROW + (i - (hop if r % 2 == 0 else -hop)) % N_ROW)
                     for r in range(N_REGION) for i in range(N_ROW)]
            got.append(lax.ppermute(both, ("region", "row"), pairs))
        swapped = lax.ppermute(jnp.stack([g[1] for g in got]), "region", [(r, r ^ 1) for r in range(N_REGION)])
        return [v] + got + [swapped, far, low, high]

    slots = pltpu.VMEM((SLOTS * HALF, Q, TILE), F32)
    acc = pltpu.VMEM((HALF, Q, TILE), F32)
    low, high = region_pair(v0)
    inner = pl.pallas_call(
        inner_kernel, out_shape=shape(HALF, Q, TILE), in_specs=[SMEM] * 3 + [VMEM] * 2, out_specs=VMEM,
        scratch_shapes=[pltpu.VMEM((len(HOPS) * HALF, Q, TILE), F32)],
        cost_estimate=pl.CostEstimate(flops=2 * 12 * Q * TILE * TILE, bytes_accessed=2000000, transcendentals=0),
        compiler_params=PARAMS, name="first_inner",
    )(upward, tile_row, tile_col, near.reshape(N_ROW * width, TILE), tile_vals)
    v1 = pl.pallas_call(
        outer_kernel, out_shape=shape(Q, ROWS), in_specs=[SMEM] * 2 + [VMEM] * 4, out_specs=VMEM,
        scratch_shapes=[pltpu.VMEM((2 * HALF, Q, TILE), F32), acc], compiler_params=PARAMS, name="first_outer",
    )(tile_row, tile_col, inner, low, high, tile_vals)
    v2 = pl.pallas_call(
        next_kernel, out_shape=shape(Q, ROWS), in_specs=[SMEM] * 3 + [VMEM] * (N_BLOCKS + 1), out_specs=VMEM,
        scratch_shapes=[slots, acc], compiler_params=PARAMS, name="second",
    )(place, tile_row, tile_col, *exchange(v1), tile_vals)
    v3, moments = pl.pallas_call(
        last_kernel, out_shape=(shape(Q, ROWS), shape(4, TILE)),
        in_specs=[SMEM] * 3 + [VMEM] * (N_BLOCKS + 3), out_specs=(VMEM, VMEM),
        scratch_shapes=[slots, acc], compiler_params=PARAMS, name="third",
    )(place, tile_row, tile_col, *exchange(v2), v0, v1, tile_vals)

    moments = lax.all_to_all(jnp.broadcast_to(moments[None], (N_ROW, 4, TILE)), "row", 0, 0, tiled=True)
    moments = jnp.sum(moments.reshape(2, 2, 2, 2, 2, 4, TILE).sum(0).sum(0).sum(0).sum(0), axis=0)
    moments = lax.all_to_all(jnp.broadcast_to(moments[None], (N_REGION, 4, TILE)), "region", 0, 0, tiled=True)
    diffused, residual = pl.pallas_call(
        finish_kernel, out_shape=(shape(Q, ROWS), shape(Q, ROWS)), in_specs=[VMEM] * 5, out_specs=(VMEM, VMEM),
        compiler_params=PARAMS, name="finish",
    )(moments, v0, v1, v2, v3)
    return (diffused, residual)


def solution(mesh):
    in_specs = (
        P("row", None),
        P(("region", "row"), None),
        P(),
        P("region", "row"),
        P(("region", "row"), None, None),
        P(("region", "row")),
        P(("region", "row")),
    )
    out_specs = (P(None, ("region", "row")), P(None, ("region", "row")))
    return jax.shard_map(local, mesh=mesh, in_specs=in_specs, out_specs=out_specs, check_vma=False)
```

```python
import jax
import jax.numpy as jnp
from jax import lax
from jax.experimental import pallas as pl
from jax.experimental.pallas import tpu as pltpu
from jax.sharding import PartitionSpec as P

Q = 64
D = 512
TILE = 128
HALF = 2
ROWS = TILE * HALF
N_ROW = 32
N_REGION = 16
QS = Q // N_ROW
HOPS = (0, 1, 8, 3, -1, -8, -3, 16)
SLOTS = len(HOPS) + 2
HIGHEST = lax.Precision.HIGHEST
F32 = jnp.float32
TAU = 1.0 / 0.9


def ring(count, hop):
    return [(i, (i + hop) % count) for i in range(count)]


def pack_kernel(queries_hbm, perm_hbm, row_hbm, col_hbm, out_ref, row_ref, col_ref, queries_ref, perm_ref, sems):
    pairs = ((queries_hbm, queries_ref), (perm_hbm, perm_ref), (row_hbm, row_ref), (col_hbm, col_ref))
    copies = [pltpu.make_async_copy(src, dst, sems.at[n]) for n, (src, dst) in enumerate(pairs)]
    for copy in copies:
        copy.start()
    for copy in copies:
        copy.wait()
    perm = perm_ref[...].astype(F32)
    out_ref[:, :, :D] = jnp.broadcast_to(queries_ref[...][None], (N_ROW, QS, D))
    for h in range(HALF):
        out_ref[:, h:h + 1, D:] = jnp.broadcast_to(perm[:, h * TILE:(h + 1) * TILE][None], (N_ROW, 1, TILE))


def scores_kernel(dev_ref, packed_ref, desc_ref, cand_ref, out_ref):
    scores = lax.dot_general(
        packed_ref[:, :D], desc_ref[...], (((1,), (1,)), ((), ())),
        precision=HIGHEST, preferred_element_type=F32,
    ) * (1.0 / (D ** 0.5))
    stored = jnp.exp(scores)
    cand = cand_ref[...]
    for h in range(HALF):
        hit = jnp.where(cand == dev_ref[0] * HALF + h, 1.0, 0.0)
        member = jnp.max(hit, axis=1, keepdims=True) > 0.5
        kept = jnp.where(member, stored[:, h * TILE:(h + 1) * TILE], 0.0)
        for q in range(QS):
            out_ref[pl.ds(q * HALF + h, N_ROW, stride=QS * HALF), :] = kept[q * N_ROW:(q + 1) * N_ROW]


GROUPS = 2


def permute_kernel(table_ref, packed_ref, out_ref, graph_ref):
    rows = N_ROW * HALF
    perm = packed_ref[:, D:].astype(jnp.int32)
    for first in range(0, rows, 8 * GROUPS):
        spans = [slice(first + 8 * g, first + 8 * g + 8) for g in range(GROUPS)]
        low = [perm[span] & (TILE - 1) for span in spans]
        high = [perm[span] >> 7 for span in spans]
        acc = [[jnp.zeros((8, TILE), F32) for _ in spans] for _ in range(QS)]
        for sender in range(N_ROW):
            for h in range(HALF):
                hits = [x == sender * HALF + h for x in high]
                for q in range(QS):
                    line = table_ref[(sender * QS + q) * HALF + h:(sender * QS + q) * HALF + h + 1, :]
                    line = jnp.broadcast_to(line, (8, TILE))
                    for g in range(GROUPS):
                        acc[q][g] = jnp.where(hits[g], jnp.take_along_axis(line, low[g], axis=1), acc[q][g])
        for q in range(QS):
            for g, span in enumerate(spans):
                graph_ref[q, span, :] = acc[q][g]
    width = len(HOPS) * QS * HALF
    for q in range(QS):
        for h in range(HALF):
            mine = graph_ref[q, pl.ds(h, N_ROW, stride=HALF), :]
            for k, hop in enumerate(HOPS):
                hop = hop % N_ROW
                rolled = mine if hop == 0 else jnp.concatenate([mine[hop:], mine[:hop]], axis=0)
                out_ref[pl.ds((k * QS + q) * HALF + h, N_ROW, stride=width), :] = rolled


def tile_slot(col, place_ref):
    hop = (((col >> 1) - place_ref[0]) * place_ref[1]) & (N_ROW - 1)
    slot = jnp.int32(0)
    for k, h in enumerate(HOPS):
        slot = jnp.where(hop == h % N_ROW, k, slot)
    slot = slot * HALF + (col & 1)
    return jnp.where(col >= N_ROW * HALF, col - N_ROW * HALF + len(HOPS) * HALF, slot)


def split(x):
    high = x.astype(jnp.bfloat16)
    return high, (x - high.astype(F32)).astype(jnp.bfloat16)


def product(slots_ref, slot, tiles_ref, t):
    high, low = split(slots_ref[slot])
    tile_high, tile_low = split(tiles_ref[t])
    contract = (((1,), (1,)), ((), ()))
    both = lax.dot_general(jnp.concatenate([high, low], axis=0), tile_high, contract, preferred_element_type=F32)
    return both[:Q] + both[Q:] + lax.dot_general(high, tile_low, contract, preferred_element_type=F32)


def spread(slots_ref, k, block):
    for h in range(HALF):
        slots_ref[k * HALF + h] = block[:, h * TILE:(h + 1) * TILE]


def inner_kernel(place_ref, row_ref, col_ref, near_ref, tiles_ref, out_ref, slots_ref):
    width = len(HOPS) * QS * HALF
    for k in range(len(HOPS)):
        for h in range(HALF):
            for q in range(QS):
                slots_ref[k * HALF + h, q * N_ROW:(q + 1) * N_ROW, :] = near_ref[
                    pl.ds((k * QS + q) * HALF + h, N_ROW, stride=width), :]
    out_ref[...] = jnp.zeros_like(out_ref)
    for t in range(tiles_ref.shape[0]):
        inside = col_ref[t] < N_ROW * HALF
        slot = jnp.where(inside, tile_slot(col_ref[t], place_ref), 0)
        out_ref[row_ref[t]] += jnp.where(inside, product(slots_ref, slot, tiles_ref, t), 0.0)


def outer_kernel(row_ref, col_ref, inner_ref, low_ref, high_ref, tiles_ref, out_ref, slots_ref, acc_ref):
    spread(slots_ref, 0, low_ref[...])
    spread(slots_ref, 1, high_ref[...])
    acc_ref[...] = inner_ref[...]
    for t in range(tiles_ref.shape[0]):
        @pl.when(col_ref[t] >= N_ROW * HALF)
        def _():
            acc_ref[row_ref[t]] += product(slots_ref, col_ref[t] - N_ROW * HALF, tiles_ref, t)
    for h in range(HALF):
        out_ref[:, h * TILE:(h + 1) * TILE] = acc_ref[h]


def pair_kernel(core_ref, own_ref, low_ref, high_ref, out_ref):
    out_ref[0] = own_ref[...]
    out_ref[1] = jnp.where(core_ref[0] == 0, high_ref[...], low_ref[...])


def swap_kernel(a_ref, b_ref, c_ref, out_ref):
    for k, ref in enumerate((a_ref, b_ref, c_ref)):
        out_ref[k] = ref[1]


N_BLOCKS = 8


def next_kernel(place_ref, row_ref, col_ref, *refs):
    own, a_ref, b_ref, c_ref, swapped_ref, far_ref, low_ref, high_ref = refs[:N_BLOCKS]
    tiles_ref, out_ref, slots_ref, acc_ref = refs[N_BLOCKS:]
    blocks = [own[...], a_ref[0], b_ref[0], c_ref[0], swapped_ref[0], swapped_ref[1], swapped_ref[2],
              far_ref[...], low_ref[...], high_ref[...]]
    for k, block in enumerate(blocks):
        spread(slots_ref, k, block)
    acc_ref[...] = jnp.zeros_like(acc_ref)
    for t in range(tiles_ref.shape[0]):
        acc_ref[row_ref[t]] += product(slots_ref, tile_slot(col_ref[t], place_ref), tiles_ref, t)
    for h in range(HALF):
        out_ref[:, h * TILE:(h + 1) * TILE] = acc_ref[h]


def last_kernel(place_ref, row_ref, col_ref, *refs):
    blocks = refs[:N_BLOCKS]
    v0_ref, v1_ref, tiles_ref, out_ref, moments_ref, *scratch = refs[N_BLOCKS:]
    next_kernel(place_ref, row_ref, col_ref, *blocks, tiles_ref, out_ref, *scratch)
    vs = [v0_ref[...], v1_ref[...], blocks[0][...], out_ref[...]]
    lane = lax.broadcasted_iota(jnp.int32, (Q, TILE), 1)
    packed = [jnp.zeros((Q, TILE), F32), jnp.zeros((Q, TILE), F32)]
    for m in range(6):
        prod = vs[m // 2] * vs[(m + 1) // 2]
        total = jnp.sum(prod[:, :TILE] + prod[:, TILE:], axis=1, keepdims=True)
        packed[m % 2] = jnp.where(lane == m // 2, total, packed[m % 2])
    moments_ref[...] = jnp.concatenate(packed, axis=0).T[:4]


def finish_kernel(moments_ref, v0_ref, v1_ref, v2_ref, v3_ref, diffused_ref, residual_ref):
    parts = [moments_ref[r] for r in range(N_REGION)]
    while len(parts) > 1:
        parts = [a + b for a, b in zip(parts[::2], parts[1::2])]
    square = jnp.concatenate([parts[0], jnp.zeros((TILE - 4, TILE), F32)], axis=0).T
    m = [square[(k % 2) * Q:(k % 2 + 1) * Q, k // 2:k // 2 + 1] for k in range(6)]
    g = [None] + [x / m[0] for x in m[1:]]
    d11 = g[2] - g[1] * g[1]
    d12 = g[3] - g[1] * g[2]
    d22 = g[4] - g[2] * g[2]
    f1 = g[4] - g[1] * g[3]
    f2 = g[5] - g[2] * g[3]
    ratio = d12 / d11
    c2 = -(f2 - ratio * f1) / (d22 - ratio * d12)
    c1 = -(f1 + d12 * c2) / d11
    c0 = -(g[3] + g[1] * c1 + g[2] * c2)
    e1 = TAU + c2
    e0 = e1 * TAU + c1
    scale = 1.0 / (e0 * TAU + c0)
    v0, v1, v2 = v0_ref[...], v1_ref[...], v2_ref[...]
    diffused_ref[...] = (TAU * scale) * (v2 + e1 * v1 + e0 * v0)
    residual_ref[...] = scale * (v3_ref[...] + c2 * v2 + c1 * v1 + c0 * v0)


SMEM = pl.BlockSpec(memory_space=pltpu.SMEM)
VMEM = pl.BlockSpec(memory_space=pltpu.VMEM)
HBM = pl.BlockSpec(memory_space=pltpu.MemorySpace.HBM)
PARAMS = pltpu.CompilerParams(vmem_limit_bytes=32 * 1024 * 1024)


def shape(*dims):
    return jax.ShapeDtypeStruct(dims, F32)


def local(queries, descriptors, candidates, cluster_perm, tile_vals, tile_row, tile_col):
    row_index = lax.axis_index("row").astype(jnp.int32)
    region = lax.axis_index("region").astype(jnp.int32)
    core = region & 1
    device = (region * N_ROW + row_index)[None]
    place = jnp.stack([row_index, 1 - 2 * core])
    upward = jnp.stack([row_index, jnp.int32(1)])

    index = jax.ShapeDtypeStruct(tile_row.shape, jnp.int32)
    packed, tile_row, tile_col = pl.pallas_call(
        pack_kernel, out_shape=(shape(N_ROW, QS, D + TILE), index, index), in_specs=[HBM] * 4, out_specs=(VMEM, SMEM, SMEM),
        scratch_shapes=[pltpu.VMEM(queries.shape, F32), pltpu.VMEM(cluster_perm.shape, jnp.int32),
                        pltpu.SemaphoreType.DMA((4,))],
        compiler_params=pltpu.CompilerParams(vmem_limit_bytes=64 * 1024 * 1024), name="pack",
    )(queries, cluster_perm, tile_row, tile_col)
    packed = lax.all_to_all(packed, "row", 0, 0, tiled=True).reshape(Q, D + TILE)
    by_query = pl.pallas_call(
        scores_kernel, out_shape=shape(N_ROW * QS * HALF, TILE), in_specs=[SMEM, VMEM, VMEM, VMEM], out_specs=VMEM,
        compiler_params=PARAMS, name="scores",
    )(device, packed, descriptors, candidates)
    table = lax.all_to_all(by_query.reshape(N_ROW, QS * HALF, TILE), "row", 0, 0, tiled=True)
    width = len(HOPS) * QS * HALF
    near = pl.pallas_call(
        permute_kernel, out_shape=shape(N_ROW * width, TILE), in_specs=[VMEM, VMEM], out_specs=VMEM,
        scratch_shapes=[pltpu.VMEM((QS, N_ROW * HALF, TILE), F32)],
        compiler_params=PARAMS, name="permute",
    )(table.reshape(N_ROW * QS * HALF, TILE), packed)
    near = lax.all_to_all(near.reshape(N_ROW, width, TILE), "row", 0, 0, tiled=True)
    v0 = near[:, :QS * HALF].reshape(N_ROW, QS, HALF, TILE).transpose(1, 0, 2, 3).reshape(Q, ROWS)

    def region_pair(v):
        return (lax.ppermute(v, "region", ring(N_REGION, 1)), lax.ppermute(v, "region", ring(N_REGION, -1)))

    def exchange(v):
        far, low, high = lax.optimization_barrier((lax.ppermute(v, "row", ring(N_ROW, 16)), *region_pair(v)))
        both = pl.pallas_call(
            pair_kernel, out_shape=shape(2, Q, ROWS), in_specs=[SMEM] + [VMEM] * 3, out_specs=VMEM,
            compiler_params=PARAMS, name="pair",
        )(core[None], v, low, high)
        got = []
        for hop in HOPS[1:4]:
            pairs = [(r * N_ROW + i, r * N_ROW + (i - (hop if r % 2 == 0 else -hop)) % N_ROW)
                     for r in range(N_REGION) for i in range(N_ROW)]
            got.append(lax.ppermute(both, ("region", "row"), pairs))
        swapped = pl.pallas_call(
            swap_kernel, out_shape=shape(len(got), Q, ROWS), in_specs=[VMEM] * len(got), out_specs=VMEM,
            compiler_params=PARAMS, name="swap",
        )(*got)
        swapped = lax.ppermute(swapped, "region", [(r, r ^ 1) for r in range(N_REGION)])
        return [v] + got + [swapped, far, low, high]

    slots = pltpu.VMEM((SLOTS * HALF, Q, TILE), F32)
    acc = pltpu.VMEM((HALF, Q, TILE), F32)
    low, high = region_pair(v0)
    inner = pl.pallas_call(
        inner_kernel, out_shape=shape(HALF, Q, TILE), in_specs=[SMEM] * 3 + [VMEM] * 2, out_specs=VMEM,
        scratch_shapes=[pltpu.VMEM((len(HOPS) * HALF, Q, TILE), F32)],
        cost_estimate=pl.CostEstimate(flops=2 * 12 * Q * TILE * TILE, bytes_accessed=2000000, transcendentals=0),
        compiler_params=PARAMS, name="first_inner",
    )(upward, tile_row, tile_col, near.reshape(N_ROW * width, TILE), tile_vals)
    v1 = pl.pallas_call(
        outer_kernel, out_shape=shape(Q, ROWS), in_specs=[SMEM] * 2 + [VMEM] * 4, out_specs=VMEM,
        scratch_shapes=[pltpu.VMEM((2 * HALF, Q, TILE), F32), acc], compiler_params=PARAMS, name="first_outer",
    )(tile_row, tile_col, inner, low, high, tile_vals)
    v2 = pl.pallas_call(
        next_kernel, out_shape=shape(Q, ROWS), in_specs=[SMEM] * 3 + [VMEM] * (N_BLOCKS + 1), out_specs=VMEM,
        scratch_shapes=[slots, acc], compiler_params=PARAMS, name="second",
    )(place, tile_row, tile_col, *exchange(v1), tile_vals)
    v3, moments = pl.pallas_call(
        last_kernel, out_shape=(shape(Q, ROWS), shape(4, TILE)),
        in_specs=[SMEM] * 3 + [VMEM] * (N_BLOCKS + 3), out_specs=(VMEM, VMEM),
        scratch_shapes=[slots, acc], compiler_params=PARAMS, name="third",
    )(place, tile_row, tile_col, *exchange(v2), v0, v1, tile_vals)

    moments = lax.all_to_all(jnp.broadcast_to(moments[None], (N_ROW, 4, TILE)), "row", 0, 0, tiled=True)
    moments = jnp.sum(moments.reshape(2, 2, 2, 2, 2, 4, TILE).sum(0).sum(0).sum(0).sum(0), axis=0)
    moments = lax.all_to_all(jnp.broadcast_to(moments[None], (N_REGION, 4, TILE)), "region", 0, 0, tiled=True)
    diffused, residual = pl.pallas_call(
        finish_kernel, out_shape=(shape(Q, ROWS), shape(Q, ROWS)), in_specs=[VMEM] * 5, out_specs=(VMEM, VMEM),
        compiler_params=PARAMS, name="finish",
    )(moments, v0, v1, v2, v3)
    return (diffused, residual)


def solution(mesh):
    in_specs = (
        P("row", None),
        P(("region", "row"), None),
        P(),
        P("region", "row"),
        P(("region", "row"), None, None),
        P(("region", "row")),
        P(("region", "row")),
    )
    out_specs = (P(None, ("region", "row")), P(None, ("region", "row")))
    return jax.shard_map(local, mesh=mesh, in_specs=in_specs, out_specs=out_specs, check_vma=False)
```

```python
import jax
import jax.numpy as jnp
from jax import lax
from jax.experimental import pallas as pl
from jax.experimental.pallas import tpu as pltpu
from jax.sharding import PartitionSpec as P

Q = 64
D = 512
TILE = 128
HALF = 2
ROWS = TILE * HALF
N_ROW = 32
N_REGION = 16
QS = Q // N_ROW
HOPS = (0, 1, -1, 3, -3, 8, -8, 16)
N_X = 4
N_Y = 8
SHARED = (1, 3)
SLOTS = len(HOPS) + 2
HIGHEST = lax.Precision.HIGHEST
F32 = jnp.float32
TAU = 1.0 / 0.9


def ring(count, hop):
    return [(i, (i + hop) % count) for i in range(count)]


def pack_kernel(queries_hbm, perm_hbm, row_hbm, col_hbm, out_ref, row_ref, col_ref, queries_ref, perm_ref, sems):
    pairs = ((queries_hbm, queries_ref), (perm_hbm, perm_ref), (row_hbm, row_ref), (col_hbm, col_ref))
    copies = [pltpu.make_async_copy(src, dst, sems.at[n]) for n, (src, dst) in enumerate(pairs)]
    for copy in copies:
        copy.start()
    for copy in copies:
        copy.wait()
    perm = perm_ref[...].astype(F32)
    out_ref[:, :, :D] = jnp.broadcast_to(queries_ref[...][None], (N_ROW, QS, D))
    for h in range(HALF):
        out_ref[:, h:h + 1, D:] = jnp.broadcast_to(perm[:, h * TILE:(h + 1) * TILE][None], (N_ROW, 1, TILE))


def scores_kernel(dev_ref, packed_ref, desc_ref, cand_ref, out_ref):
    scores = lax.dot_general(
        packed_ref[:, :D], desc_ref[...], (((1,), (1,)), ((), ())),
        precision=HIGHEST, preferred_element_type=F32,
    ) * (1.0 / (D ** 0.5))
    stored = jnp.exp(scores)
    cand = cand_ref[...]
    for h in range(HALF):
        hit = jnp.where(cand == dev_ref[0] * HALF + h, 1.0, 0.0)
        member = jnp.max(hit, axis=1, keepdims=True) > 0.5
        kept = jnp.where(member, stored[:, h * TILE:(h + 1) * TILE], 0.0)
        for q in range(QS):
            out_ref[pl.ds(q * HALF + h, N_ROW, stride=QS * HALF), :] = kept[q * N_ROW:(q + 1) * N_ROW]


GROUPS = 2


def permute_kernel(table_ref, packed_ref, out_ref, graph_ref):
    rows = N_ROW * HALF
    perm = packed_ref[:, D:].astype(jnp.int32)
    for first in range(0, rows, 8 * GROUPS):
        spans = [slice(first + 8 * g, first + 8 * g + 8) for g in range(GROUPS)]
        low = [perm[span] & (TILE - 1) for span in spans]
        high = [perm[span] >> 7 for span in spans]
        acc = [[jnp.zeros((8, TILE), F32) for _ in spans] for _ in range(QS)]
        for sender in range(N_ROW):
            for h in range(HALF):
                hits = [x == sender * HALF + h for x in high]
                for q in range(QS):
                    line = table_ref[(sender * QS + q) * HALF + h:(sender * QS + q) * HALF + h + 1, :]
                    line = jnp.broadcast_to(line, (8, TILE))
                    for g in range(GROUPS):
                        acc[q][g] = jnp.where(hits[g], jnp.take_along_axis(line, low[g], axis=1), acc[q][g])
        for q in range(QS):
            for g, span in enumerate(spans):
                graph_ref[q, span, :] = acc[q][g]
    width = len(HOPS) * QS * HALF
    for q in range(QS):
        for h in range(HALF):
            mine = graph_ref[q, pl.ds(h, N_ROW, stride=HALF), :]
            for k, hop in enumerate(HOPS):
                hop = hop % N_ROW
                rolled = mine if hop == 0 else jnp.concatenate([mine[hop:], mine[:hop]], axis=0)
                out_ref[pl.ds((k * QS + q) * HALF + h, N_ROW, stride=width), :] = rolled


def near_slot(col, place_ref):
    hop = ((col >> 1) - place_ref[0]) & (N_ROW - 1)
    slot = jnp.int32(0)
    for k, h in enumerate(HOPS):
        slot = jnp.where(hop == h % N_ROW, k, slot)
    return slot * HALF + (col & 1)


def any_slot(col, place_ref):
    owner = col >> 1
    hop = owner - place_ref[0]
    slot = owner >> 3
    for k, h in enumerate(SHARED + tuple(-h for h in SHARED)):
        slot = jnp.where(((hop * place_ref[1]) & (N_ROW - 1)) == h % N_ROW, N_X + k, slot)
    slot = slot * HALF + (col & 1)
    return jnp.where(col >= N_ROW * HALF, col - N_ROW * HALF + (N_X + 2 * len(SHARED)) * HALF, slot)


def split(x):
    high = x.astype(jnp.bfloat16)
    return high, (x - high.astype(F32)).astype(jnp.bfloat16)


def product(slots_ref, slot, tiles_ref, t):
    high, low = split(slots_ref[slot])
    tile_high, tile_low = split(tiles_ref[t])
    contract = (((1,), (1,)), ((), ()))
    both = lax.dot_general(jnp.concatenate([high, low], axis=0), tile_high, contract, preferred_element_type=F32)
    return both[:Q] + both[Q:] + lax.dot_general(high, tile_low, contract, preferred_element_type=F32)


def spread(slots_ref, k, block):
    for h in range(HALF):
        slots_ref[k * HALF + h] = block[:, h * TILE:(h + 1) * TILE]


def inner_kernel(place_ref, row_ref, col_ref, near_ref, tiles_ref, out_ref, slots_ref):
    width = len(HOPS) * QS * HALF
    for k in range(len(HOPS)):
        for h in range(HALF):
            for q in range(QS):
                slots_ref[k * HALF + h, q * N_ROW:(q + 1) * N_ROW, :] = near_ref[
                    pl.ds((k * QS + q) * HALF + h, N_ROW, stride=width), :]
    out_ref[...] = jnp.zeros_like(out_ref)
    for t in range(tiles_ref.shape[0]):
        inside = col_ref[t] < N_ROW * HALF
        slot = jnp.where(inside, near_slot(col_ref[t], place_ref), 0)
        out_ref[row_ref[t]] += jnp.where(inside, product(slots_ref, slot, tiles_ref, t), 0.0)


def outer_kernel(row_ref, col_ref, inner_ref, low_ref, high_ref, tiles_ref, out_ref, slots_ref, acc_ref):
    spread(slots_ref, 0, low_ref[...])
    spread(slots_ref, 1, high_ref[...])
    acc_ref[...] = inner_ref[...]
    for t in range(tiles_ref.shape[0]):
        @pl.when(col_ref[t] >= N_ROW * HALF)
        def _():
            acc_ref[row_ref[t]] += product(slots_ref, col_ref[t] - N_ROW * HALF, tiles_ref, t)
    for h in range(HALF):
        out_ref[:, h * TILE:(h + 1) * TILE] = acc_ref[h]


def pair_kernel(core_ref, own_ref, low_ref, high_ref, out_ref):
    out_ref[0] = own_ref[...]
    out_ref[1] = jnp.where(core_ref[0] == 0, high_ref[...], low_ref[...])


def swap_kernel(*refs):
    *got, out_ref = refs
    for k, ref in enumerate(got):
        out_ref[k] = ref[1]


N_BLOCKS = 7


def next_kernel(place_ref, row_ref, col_ref, *refs):
    _, line_ref, a_ref, b_ref, swapped_ref, low_ref, high_ref = refs[:N_BLOCKS]
    tiles_ref, out_ref, slots_ref, acc_ref = refs[N_BLOCKS:]
    blocks = [line_ref[x] for x in range(N_X)] + [
        a_ref[0], b_ref[0], swapped_ref[0], swapped_ref[1], low_ref[...], high_ref[...]]
    for k, block in enumerate(blocks):
        spread(slots_ref, k, block)
    acc_ref[...] = jnp.zeros_like(acc_ref)
    for t in range(tiles_ref.shape[0]):
        acc_ref[row_ref[t]] += product(slots_ref, any_slot(col_ref[t], place_ref), tiles_ref, t)
    for h in range(HALF):
        out_ref[:, h * TILE:(h + 1) * TILE] = acc_ref[h]


def last_kernel(place_ref, row_ref, col_ref, *refs):
    blocks = refs[:N_BLOCKS]
    v0_ref, v1_ref, tiles_ref, out_ref, moments_ref, *scratch = refs[N_BLOCKS:]
    next_kernel(place_ref, row_ref, col_ref, *blocks, tiles_ref, out_ref, *scratch)
    vs = [v0_ref[...], v1_ref[...], blocks[0][...], out_ref[...]]
    lane = lax.broadcasted_iota(jnp.int32, (Q, TILE), 1)
    packed = [jnp.zeros((Q, TILE), F32), jnp.zeros((Q, TILE), F32)]
    for m in range(6):
        prod = vs[m // 2] * vs[(m + 1) // 2]
        total = jnp.sum(prod[:, :TILE] + prod[:, TILE:], axis=1, keepdims=True)
        packed[m % 2] = jnp.where(lane == m // 2, total, packed[m % 2])
    moments_ref[...] = jnp.concatenate(packed, axis=0).T[:4]


def finish_kernel(moments_ref, v0_ref, v1_ref, v2_ref, v3_ref, diffused_ref, residual_ref):
    parts = [moments_ref[r] for r in range(N_REGION)]
    while len(parts) > 1:
        parts = [a + b for a, b in zip(parts[::2], parts[1::2])]
    square = jnp.concatenate([parts[0], jnp.zeros((TILE - 4, TILE), F32)], axis=0).T
    m = [square[(k % 2) * Q:(k % 2 + 1) * Q, k // 2:k // 2 + 1] for k in range(6)]
    g = [None] + [x / m[0] for x in m[1:]]
    d11 = g[2] - g[1] * g[1]
    d12 = g[3] - g[1] * g[2]
    d22 = g[4] - g[2] * g[2]
    f1 = g[4] - g[1] * g[3]
    f2 = g[5] - g[2] * g[3]
    ratio = d12 / d11
    c2 = -(f2 - ratio * f1) / (d22 - ratio * d12)
    c1 = -(f1 + d12 * c2) / d11
    c0 = -(g[3] + g[1] * c1 + g[2] * c2)
    e1 = TAU + c2
    e0 = e1 * TAU + c1
    scale = 1.0 / (e0 * TAU + c0)
    v0, v1, v2 = v0_ref[...], v1_ref[...], v2_ref[...]
    diffused_ref[...] = (TAU * scale) * (v2 + e1 * v1 + e0 * v0)
    residual_ref[...] = scale * (v3_ref[...] + c2 * v2 + c1 * v1 + c0 * v0)


SMEM = pl.BlockSpec(memory_space=pltpu.SMEM)
VMEM = pl.BlockSpec(memory_space=pltpu.VMEM)
HBM = pl.BlockSpec(memory_space=pltpu.MemorySpace.HBM)
PARAMS = pltpu.CompilerParams(vmem_limit_bytes=32 * 1024 * 1024)


def shape(*dims):
    return jax.ShapeDtypeStruct(dims, F32)


def local(queries, descriptors, candidates, cluster_perm, tile_vals, tile_row, tile_col):
    row_index = lax.axis_index("row").astype(jnp.int32)
    region = lax.axis_index("region").astype(jnp.int32)
    core = region & 1
    device = (region * N_ROW + row_index)[None]
    place = jnp.stack([row_index, 1 - 2 * core])

    index = jax.ShapeDtypeStruct(tile_row.shape, jnp.int32)
    packed, tile_row, tile_col = pl.pallas_call(
        pack_kernel, out_shape=(shape(N_ROW, QS, D + TILE), index, index), in_specs=[HBM] * 4, out_specs=(VMEM, SMEM, SMEM),
        scratch_shapes=[pltpu.VMEM(queries.shape, F32), pltpu.VMEM(cluster_perm.shape, jnp.int32),
                        pltpu.SemaphoreType.DMA((4,))],
        compiler_params=pltpu.CompilerParams(vmem_limit_bytes=64 * 1024 * 1024), name="pack",
    )(queries, cluster_perm, tile_row, tile_col)
    packed = lax.all_to_all(packed, "row", 0, 0, tiled=True).reshape(Q, D + TILE)
    by_query = pl.pallas_call(
        scores_kernel, out_shape=shape(N_ROW * QS * HALF, TILE), in_specs=[SMEM, VMEM, VMEM, VMEM], out_specs=VMEM,
        compiler_params=PARAMS, name="scores",
    )(device, packed, descriptors, candidates)
    table = lax.all_to_all(by_query.reshape(N_ROW, QS * HALF, TILE), "row", 0, 0, tiled=True)
    width = len(HOPS) * QS * HALF
    near = pl.pallas_call(
        permute_kernel, out_shape=shape(N_ROW * width, TILE), in_specs=[VMEM, VMEM], out_specs=VMEM,
        scratch_shapes=[pltpu.VMEM((QS, N_ROW * HALF, TILE), F32)],
        compiler_params=PARAMS, name="permute",
    )(table.reshape(N_ROW * QS * HALF, TILE), packed)
    near = lax.all_to_all(near.reshape(N_ROW, width, TILE), "row", 0, 0, tiled=True)
    v0 = near[:, :QS * HALF].reshape(N_ROW, QS, HALF, TILE).transpose(1, 0, 2, 3).reshape(Q, ROWS)

    def region_pair(v):
        return (lax.ppermute(v, "region", ring(N_REGION, 1)), lax.ppermute(v, "region", ring(N_REGION, -1)))

    def exchange(v):
        low, high = region_pair(v)
        line = lax.all_to_all(
            jnp.broadcast_to(v[None], (N_X,) + v.shape), "row", 0, 0, tiled=True,
            axis_index_groups=[[x * N_Y + y for x in range(N_X)] for y in range(N_Y)])
        both = pl.pallas_call(
            pair_kernel, out_shape=shape(2, Q, ROWS), in_specs=[SMEM] + [VMEM] * 3, out_specs=VMEM,
            compiler_params=PARAMS, name="pair",
        )(core[None], v, low, high)
        got = []
        for hop in SHARED:
            pairs = [(r * N_ROW + i, r * N_ROW + (i - (hop if r % 2 == 0 else -hop)) % N_ROW)
                     for r in range(N_REGION) for i in range(N_ROW)]
            got.append(lax.ppermute(both, ("region", "row"), pairs))
        swapped = pl.pallas_call(
            swap_kernel, out_shape=shape(len(got), Q, ROWS), in_specs=[VMEM] * len(got), out_specs=VMEM,
            compiler_params=PARAMS, name="swap",
        )(*got)
        swapped = lax.ppermute(swapped, "region", [(r, r ^ 1) for r in range(N_REGION)])
        return [v, line] + got + [swapped, low, high]

    slots = pltpu.VMEM((SLOTS * HALF, Q, TILE), F32)
    acc = pltpu.VMEM((HALF, Q, TILE), F32)
    low, high = region_pair(v0)
    inner = pl.pallas_call(
        inner_kernel, out_shape=shape(HALF, Q, TILE), in_specs=[SMEM] * 3 + [VMEM] * 2, out_specs=VMEM,
        scratch_shapes=[pltpu.VMEM((len(HOPS) * HALF, Q, TILE), F32)],
        cost_estimate=pl.CostEstimate(flops=2 * 12 * Q * TILE * TILE, bytes_accessed=2000000, transcendentals=0),
        compiler_params=PARAMS, name="first_inner",
    )(place, tile_row, tile_col, near.reshape(N_ROW * width, TILE), tile_vals)
    v1 = pl.pallas_call(
        outer_kernel, out_shape=shape(Q, ROWS), in_specs=[SMEM] * 2 + [VMEM] * 4, out_specs=VMEM,
        scratch_shapes=[pltpu.VMEM((2 * HALF, Q, TILE), F32), acc], compiler_params=PARAMS, name="first_outer",
    )(tile_row, tile_col, inner, low, high, tile_vals)
    v2 = pl.pallas_call(
        next_kernel, out_shape=shape(Q, ROWS), in_specs=[SMEM] * 3 + [VMEM] * (N_BLOCKS + 1), out_specs=VMEM,
        scratch_shapes=[slots, acc], compiler_params=PARAMS, name="second",
    )(place, tile_row, tile_col, *exchange(v1), tile_vals)
    v3, moments = pl.pallas_call(
        last_kernel, out_shape=(shape(Q, ROWS), shape(4, TILE)),
        in_specs=[SMEM] * 3 + [VMEM] * (N_BLOCKS + 3), out_specs=(VMEM, VMEM),
        scratch_shapes=[slots, acc], compiler_params=PARAMS, name="third",
    )(place, tile_row, tile_col, *exchange(v2), v0, v1, tile_vals)

    moments = lax.all_to_all(jnp.broadcast_to(moments[None], (N_ROW, 4, TILE)), "row", 0, 0, tiled=True)
    moments = jnp.sum(moments.reshape(2, 2, 2, 2, 2, 4, TILE).sum(0).sum(0).sum(0).sum(0), axis=0)
    moments = lax.all_to_all(jnp.broadcast_to(moments[None], (N_REGION, 4, TILE)), "region", 0, 0, tiled=True)
    diffused, residual = pl.pallas_call(
        finish_kernel, out_shape=(shape(Q, ROWS), shape(Q, ROWS)), in_specs=[VMEM] * 5, out_specs=(VMEM, VMEM),
        compiler_params=PARAMS, name="finish",
    )(moments, v0, v1, v2, v3)
    return (diffused, residual)


def solution(mesh):
    in_specs = (
        P("row", None),
        P(("region", "row"), None),
        P(),
        P("region", "row"),
        P(("region", "row"), None, None),
        P(("region", "row")),
        P(("region", "row")),
    )
    out_specs = (P(None, ("region", "row")), P(None, ("region", "row")))
    return jax.shard_map(local, mesh=mesh, in_specs=in_specs, out_specs=out_specs, check_vma=False)
```

```python
import jax
import jax.numpy as jnp
from jax import lax
from jax.experimental import pallas as pl
from jax.experimental.pallas import tpu as pltpu
from jax.sharding import PartitionSpec as P

Q = 64
D = 512
TILE = 128
HALF = 2
ROWS = TILE * HALF
N_ROW = 32
N_REGION = 16
QS = Q // N_ROW
HOPS = (0, 1, -1, 3, -3, 8, -8, 16)
N_X = 4
N_Y = 8
SHARED = (1, 3)
SLOTS = len(HOPS) + 2
HIGHEST = lax.Precision.HIGHEST
F32 = jnp.float32
TAU = 1.0 / 0.9


def ring(count, hop):
    return [(i, (i + hop) % count) for i in range(count)]


def pack_kernel(queries_hbm, perm_hbm, row_hbm, col_hbm, out_ref, row_ref, col_ref, queries_ref, perm_ref, sems):
    pairs = ((queries_hbm, queries_ref), (perm_hbm, perm_ref), (row_hbm, row_ref), (col_hbm, col_ref))
    copies = [pltpu.make_async_copy(src, dst, sems.at[n]) for n, (src, dst) in enumerate(pairs)]
    for copy in copies:
        copy.start()
    for copy in copies:
        copy.wait()
    perm = perm_ref[...].astype(F32)
    out_ref[:, :, :D] = jnp.broadcast_to(queries_ref[...][None], (N_ROW, QS, D))
    for h in range(HALF):
        out_ref[:, h:h + 1, D:] = jnp.broadcast_to(perm[:, h * TILE:(h + 1) * TILE][None], (N_ROW, 1, TILE))


def scores_kernel(dev_ref, packed_ref, desc_ref, cand_ref, out_ref):
    scores = lax.dot_general(
        packed_ref[:, :D], desc_ref[...], (((1,), (1,)), ((), ())),
        precision=HIGHEST, preferred_element_type=F32,
    ) * (1.0 / (D ** 0.5))
    stored = jnp.exp(scores)
    cand = cand_ref[...]
    for h in range(HALF):
        hit = jnp.where(cand == dev_ref[0] * HALF + h, 1.0, 0.0)
        member = jnp.max(hit, axis=1, keepdims=True) > 0.5
        kept = jnp.where(member, stored[:, h * TILE:(h + 1) * TILE], 0.0)
        for q in range(QS):
            out_ref[pl.ds(q * HALF + h, N_ROW, stride=QS * HALF), :] = kept[q * N_ROW:(q + 1) * N_ROW]


GROUPS = 2


def permute_kernel(table_ref, packed_ref, out_ref, graph_ref):
    rows = N_ROW * HALF
    perm = packed_ref[:, D:].astype(jnp.int32)
    for first in range(0, rows, 8 * GROUPS):
        spans = [slice(first + 8 * g, first + 8 * g + 8) for g in range(GROUPS)]
        low = [perm[span] & (TILE - 1) for span in spans]
        high = [perm[span] >> 7 for span in spans]
        acc = [[jnp.zeros((8, TILE), F32) for _ in spans] for _ in range(QS)]
        for sender in range(N_ROW):
            for h in range(HALF):
                hits = [x == sender * HALF + h for x in high]
                for q in range(QS):
                    line = table_ref[(sender * QS + q) * HALF + h:(sender * QS + q) * HALF + h + 1, :]
                    line = jnp.broadcast_to(line, (8, TILE))
                    for g in range(GROUPS):
                        acc[q][g] = jnp.where(hits[g], jnp.take_along_axis(line, low[g], axis=1), acc[q][g])
        for q in range(QS):
            for g, span in enumerate(spans):
                graph_ref[q, span, :] = acc[q][g]
    width = len(HOPS) * QS * HALF
    for q in range(QS):
        for h in range(HALF):
            mine = graph_ref[q, pl.ds(h, N_ROW, stride=HALF), :]
            for k, hop in enumerate(HOPS):
                hop = hop % N_ROW
                rolled = mine if hop == 0 else jnp.concatenate([mine[hop:], mine[:hop]], axis=0)
                out_ref[pl.ds((k * QS + q) * HALF + h, N_ROW, stride=width), :] = rolled


def near_slot(col, place_ref):
    hop = ((col >> 1) - place_ref[0]) & (N_ROW - 1)
    slot = jnp.int32(0)
    for k, h in enumerate(HOPS):
        slot = jnp.where(hop == h % N_ROW, k, slot)
    return slot * HALF + (col & 1)


def any_slot(col, place_ref):
    owner = col >> 1
    hop = owner - place_ref[0]
    slot = owner >> 3
    for k, h in enumerate(SHARED + tuple(-h for h in SHARED)):
        slot = jnp.where(((hop * place_ref[1]) & (N_ROW - 1)) == h % N_ROW, N_X + k, slot)
    slot = slot * HALF + (col & 1)
    return jnp.where(col >= N_ROW * HALF, col - N_ROW * HALF + (N_X + 2 * len(SHARED)) * HALF, slot)


def split(x):
    high = x.astype(jnp.bfloat16)
    return high, (x - high.astype(F32)).astype(jnp.bfloat16)


def product(slots_ref, slot, tiles_ref, t):
    high, low = split(slots_ref[slot])
    tile_high, tile_low = split(tiles_ref[t])
    contract = (((1,), (1,)), ((), ()))
    both = lax.dot_general(jnp.concatenate([high, low], axis=0), tile_high, contract, preferred_element_type=F32)
    return both[:Q] + both[Q:] + lax.dot_general(high, tile_low, contract, preferred_element_type=F32)


def spread(slots_ref, k, block):
    for h in range(HALF):
        slots_ref[k * HALF + h] = block[:, h * TILE:(h + 1) * TILE]


def store(acc_ref, out_ref, copies_ref=None):
    for h in range(HALF):
        cols = slice(h * TILE, (h + 1) * TILE)
        out_ref[:, cols] = acc_ref[h]
        if copies_ref is not None:
            for x in range(N_X):
                copies_ref[x, :, cols] = acc_ref[h]


def inner_kernel(place_ref, row_ref, col_ref, near_ref, tiles_ref, out_ref, slots_ref):
    width = len(HOPS) * QS * HALF
    for k in range(len(HOPS)):
        for h in range(HALF):
            for q in range(QS):
                slots_ref[k * HALF + h, q * N_ROW:(q + 1) * N_ROW, :] = near_ref[
                    pl.ds((k * QS + q) * HALF + h, N_ROW, stride=width), :]
    out_ref[...] = jnp.zeros_like(out_ref)
    for t in range(tiles_ref.shape[0]):
        inside = col_ref[t] < N_ROW * HALF
        slot = jnp.where(inside, near_slot(col_ref[t], place_ref), 0)
        out_ref[row_ref[t]] += jnp.where(inside, product(slots_ref, slot, tiles_ref, t), 0.0)


def outer_kernel(row_ref, col_ref, inner_ref, low_ref, high_ref, tiles_ref, out_ref, copies_ref, slots_ref, acc_ref):
    spread(slots_ref, 0, low_ref[...])
    spread(slots_ref, 1, high_ref[...])
    acc_ref[...] = inner_ref[...]
    for t in range(tiles_ref.shape[0]):
        @pl.when(col_ref[t] >= N_ROW * HALF)
        def _():
            acc_ref[row_ref[t]] += product(slots_ref, col_ref[t] - N_ROW * HALF, tiles_ref, t)
    store(acc_ref, out_ref, copies_ref)


def pair_kernel(core_ref, own_ref, low_ref, high_ref, out_ref):
    out_ref[0] = own_ref[...]
    out_ref[1] = jnp.where(core_ref[0] == 0, high_ref[...], low_ref[...])


def swap_kernel(*refs):
    *got, out_ref = refs
    for k, ref in enumerate(got):
        out_ref[k] = ref[1]


N_BLOCKS = 7


def times_s(place_ref, row_ref, col_ref, blocks, tiles_ref, slots_ref, acc_ref):
    _, line_ref, a_ref, b_ref, swapped_ref, low_ref, high_ref = blocks
    blocks = [line_ref[x] for x in range(N_X)] + [
        a_ref[0], b_ref[0], swapped_ref[0], swapped_ref[1], low_ref[...], high_ref[...]]
    for k, block in enumerate(blocks):
        spread(slots_ref, k, block)
    acc_ref[...] = jnp.zeros_like(acc_ref)
    for t in range(tiles_ref.shape[0]):
        acc_ref[row_ref[t]] += product(slots_ref, any_slot(col_ref[t], place_ref), tiles_ref, t)


def next_kernel(place_ref, row_ref, col_ref, *refs):
    tiles_ref, out_ref, copies_ref, slots_ref, acc_ref = refs[N_BLOCKS:]
    times_s(place_ref, row_ref, col_ref, refs[:N_BLOCKS], tiles_ref, slots_ref, acc_ref)
    store(acc_ref, out_ref, copies_ref)


def last_kernel(place_ref, row_ref, col_ref, *refs):
    blocks = refs[:N_BLOCKS]
    v0_ref, v1_ref, tiles_ref, out_ref, moments_ref, slots_ref, acc_ref = refs[N_BLOCKS:]
    times_s(place_ref, row_ref, col_ref, blocks, tiles_ref, slots_ref, acc_ref)
    store(acc_ref, out_ref)
    vs = [v0_ref[...], v1_ref[...], blocks[0][...], out_ref[...]]
    lane = lax.broadcasted_iota(jnp.int32, (Q, TILE), 1)
    packed = [jnp.zeros((Q, TILE), F32), jnp.zeros((Q, TILE), F32)]
    for m in range(6):
        prod = vs[m // 2] * vs[(m + 1) // 2]
        total = jnp.sum(prod[:, :TILE] + prod[:, TILE:], axis=1, keepdims=True)
        packed[m % 2] = jnp.where(lane == m // 2, total, packed[m % 2])
    moments_ref[...] = jnp.concatenate(packed, axis=0).T[:4]


def finish_kernel(moments_ref, v0_ref, v1_ref, v2_ref, v3_ref, diffused_ref, residual_ref):
    parts = [moments_ref[r] for r in range(N_REGION)]
    while len(parts) > 1:
        parts = [a + b for a, b in zip(parts[::2], parts[1::2])]
    square = jnp.concatenate([parts[0], jnp.zeros((TILE - 4, TILE), F32)], axis=0).T
    m = [square[(k % 2) * Q:(k % 2 + 1) * Q, k // 2:k // 2 + 1] for k in range(6)]
    g = [None] + [x / m[0] for x in m[1:]]
    d11 = g[2] - g[1] * g[1]
    d12 = g[3] - g[1] * g[2]
    d22 = g[4] - g[2] * g[2]
    f1 = g[4] - g[1] * g[3]
    f2 = g[5] - g[2] * g[3]
    ratio = d12 / d11
    c2 = -(f2 - ratio * f1) / (d22 - ratio * d12)
    c1 = -(f1 + d12 * c2) / d11
    c0 = -(g[3] + g[1] * c1 + g[2] * c2)
    e1 = TAU + c2
    e0 = e1 * TAU + c1
    scale = 1.0 / (e0 * TAU + c0)
    v0, v1, v2 = v0_ref[...], v1_ref[...], v2_ref[...]
    diffused_ref[...] = (TAU * scale) * (v2 + e1 * v1 + e0 * v0)
    residual_ref[...] = scale * (v3_ref[...] + c2 * v2 + c1 * v1 + c0 * v0)


SMEM = pl.BlockSpec(memory_space=pltpu.SMEM)
VMEM = pl.BlockSpec(memory_space=pltpu.VMEM)
HBM = pl.BlockSpec(memory_space=pltpu.MemorySpace.HBM)
PARAMS = pltpu.CompilerParams(vmem_limit_bytes=32 * 1024 * 1024)


def shape(*dims):
    return jax.ShapeDtypeStruct(dims, F32)


def local(queries, descriptors, candidates, cluster_perm, tile_vals, tile_row, tile_col):
    row_index = lax.axis_index("row").astype(jnp.int32)
    region = lax.axis_index("region").astype(jnp.int32)
    core = region & 1
    device = (region * N_ROW + row_index)[None]
    place = jnp.stack([row_index, 1 - 2 * core])

    index = jax.ShapeDtypeStruct(tile_row.shape, jnp.int32)
    packed, tile_row, tile_col = pl.pallas_call(
        pack_kernel, out_shape=(shape(N_ROW, QS, D + TILE), index, index), in_specs=[HBM] * 4, out_specs=(VMEM, SMEM, SMEM),
        scratch_shapes=[pltpu.VMEM(queries.shape, F32), pltpu.VMEM(cluster_perm.shape, jnp.int32),
                        pltpu.SemaphoreType.DMA((4,))],
        compiler_params=pltpu.CompilerParams(vmem_limit_bytes=64 * 1024 * 1024), name="pack",
    )(queries, cluster_perm, tile_row, tile_col)
    packed = lax.all_to_all(packed, "row", 0, 0, tiled=True).reshape(Q, D + TILE)
    by_query = pl.pallas_call(
        scores_kernel, out_shape=shape(N_ROW * QS * HALF, TILE), in_specs=[SMEM, VMEM, VMEM, VMEM], out_specs=VMEM,
        compiler_params=PARAMS, name="scores",
    )(device, packed, descriptors, candidates)
    table = lax.all_to_all(by_query.reshape(N_ROW, QS * HALF, TILE), "row", 0, 0, tiled=True)
    width = len(HOPS) * QS * HALF
    near = pl.pallas_call(
        permute_kernel, out_shape=shape(N_ROW * width, TILE), in_specs=[VMEM, VMEM], out_specs=VMEM,
        scratch_shapes=[pltpu.VMEM((QS, N_ROW * HALF, TILE), F32)],
        compiler_params=PARAMS, name="permute",
    )(table.reshape(N_ROW * QS * HALF, TILE), packed)
    near = lax.all_to_all(near.reshape(N_ROW, width, TILE), "row", 0, 0, tiled=True)
    v0 = near[:, :QS * HALF].reshape(N_ROW, QS, HALF, TILE).transpose(1, 0, 2, 3).reshape(Q, ROWS)

    def region_pair(v):
        return (lax.ppermute(v, "region", ring(N_REGION, 1)), lax.ppermute(v, "region", ring(N_REGION, -1)))

    def exchange(v, copies):
        low, high = region_pair(v)
        line = lax.all_to_all(
            copies, "row", 0, 0, tiled=True,
            axis_index_groups=[[x * N_Y + y for x in range(N_X)] for y in range(N_Y)])
        both = pl.pallas_call(
            pair_kernel, out_shape=shape(2, Q, ROWS), in_specs=[SMEM] + [VMEM] * 3, out_specs=VMEM,
            compiler_params=PARAMS, name="pair",
        )(core[None], v, low, high)
        got = []
        for hop in SHARED:
            pairs = [(r * N_ROW + i, r * N_ROW + (i - (hop if r % 2 == 0 else -hop)) % N_ROW)
                     for r in range(N_REGION) for i in range(N_ROW)]
            got.append(lax.ppermute(both, ("region", "row"), pairs))
        *got, line = lax.optimization_barrier((*got, line))
        swapped = pl.pallas_call(
            swap_kernel, out_shape=shape(len(got), Q, ROWS), in_specs=[VMEM] * len(got), out_specs=VMEM,
            compiler_params=PARAMS, name="swap",
        )(*got)
        swapped = lax.ppermute(swapped, "region", [(r, r ^ 1) for r in range(N_REGION)])
        return [v, line] + got + [swapped, low, high]

    slots = pltpu.VMEM((SLOTS * HALF, Q, TILE), F32)
    acc = pltpu.VMEM((HALF, Q, TILE), F32)
    low, high = region_pair(v0)
    inner = pl.pallas_call(
        inner_kernel, out_shape=shape(HALF, Q, TILE), in_specs=[SMEM] * 3 + [VMEM] * 2, out_specs=VMEM,
        scratch_shapes=[pltpu.VMEM((len(HOPS) * HALF, Q, TILE), F32)],
        cost_estimate=pl.CostEstimate(flops=2 * 12 * Q * TILE * TILE, bytes_accessed=2000000, transcendentals=0),
        compiler_params=PARAMS, name="first_inner",
    )(place, tile_row, tile_col, near.reshape(N_ROW * width, TILE), tile_vals)
    with_copies = (shape(Q, ROWS), shape(N_X, Q, ROWS))
    v1, copies = pl.pallas_call(
        outer_kernel, out_shape=with_copies, in_specs=[SMEM] * 2 + [VMEM] * 4, out_specs=(VMEM, VMEM),
        scratch_shapes=[pltpu.VMEM((2 * HALF, Q, TILE), F32), acc], compiler_params=PARAMS, name="first_outer",
    )(tile_row, tile_col, inner, low, high, tile_vals)
    v2, copies = pl.pallas_call(
        next_kernel, out_shape=with_copies, in_specs=[SMEM] * 3 + [VMEM] * (N_BLOCKS + 1), out_specs=(VMEM, VMEM),
        scratch_shapes=[slots, acc], compiler_params=PARAMS, name="second",
    )(place, tile_row, tile_col, *exchange(v1, copies), tile_vals)
    v3, moments = pl.pallas_call(
        last_kernel, out_shape=(shape(Q, ROWS), shape(4, TILE)),
        in_specs=[SMEM] * 3 + [VMEM] * (N_BLOCKS + 3), out_specs=(VMEM, VMEM),
        scratch_shapes=[slots, acc], compiler_params=PARAMS, name="third",
    )(place, tile_row, tile_col, *exchange(v2, copies), v0, v1, tile_vals)

    moments = lax.all_to_all(jnp.broadcast_to(moments[None], (N_ROW, 4, TILE)), "row", 0, 0, tiled=True)
    moments = jnp.sum(moments.reshape(2, 2, 2, 2, 2, 4, TILE).sum(0).sum(0).sum(0).sum(0), axis=0)
    moments = lax.all_to_all(jnp.broadcast_to(moments[None], (N_REGION, 4, TILE)), "region", 0, 0, tiled=True)
    diffused, residual = pl.pallas_call(
        finish_kernel, out_shape=(shape(Q, ROWS), shape(Q, ROWS)), in_specs=[VMEM] * 5, out_specs=(VMEM, VMEM),
        compiler_params=PARAMS, name="finish",
    )(moments, v0, v1, v2, v3)
    return (diffused, residual)


def solution(mesh):
    in_specs = (
        P("row", None),
        P(("region", "row"), None),
        P(),
        P("region", "row"),
        P(("region", "row"), None, None),
        P(("region", "row")),
        P(("region", "row")),
    )
    out_specs = (P(None, ("region", "row")), P(None, ("region", "row")))
    return jax.shard_map(local, mesh=mesh, in_specs=in_specs, out_specs=out_specs, check_vma=False)
```

```python
import jax
import jax.numpy as jnp
from jax import lax
from jax.experimental import pallas as pl
from jax.experimental.pallas import tpu as pltpu
from jax.sharding import PartitionSpec as P

Q = 64
D = 512
TILE = 128
HALF = 2
ROWS = TILE * HALF
N_ROW = 32
N_REGION = 16
QS = Q // N_ROW
HOPS = (0, 1, -1, 3, -3, 8, -8, 16)
N_X = 4
N_Y = 8
SHARED = (1, 3)
SLOTS = len(HOPS) + 2
HIGHEST = lax.Precision.HIGHEST
F32 = jnp.float32
TAU = 1.0 / 0.9


def ring(count, hop):
    return [(i, (i + hop) % count) for i in range(count)]


def pack_kernel(queries_hbm, perm_hbm, out_ref, queries_ref, perm_ref, sems):
    pairs = ((queries_hbm, queries_ref), (perm_hbm, perm_ref))
    copies = [pltpu.make_async_copy(src, dst, sems.at[n]) for n, (src, dst) in enumerate(pairs)]
    for copy in copies:
        copy.start()
    for copy in copies:
        copy.wait()
    perm = perm_ref[...].astype(F32)
    out_ref[:, :, :D] = jnp.broadcast_to(queries_ref[...][None], (N_ROW, QS, D))
    for h in range(HALF):
        out_ref[:, h:h + 1, D:] = jnp.broadcast_to(perm[:, h * TILE:(h + 1) * TILE][None], (N_ROW, 1, TILE))


def scores_kernel(dev_ref, row_in_ref, col_in_ref, packed_ref, desc_ref, cand_ref, out_ref, row_ref, col_ref):
    for t in range(row_ref.shape[0]):
        row_ref[t] = row_in_ref[t]
        col_ref[t] = col_in_ref[t]
    scores = lax.dot_general(
        packed_ref[:, :D], desc_ref[...], (((1,), (1,)), ((), ())),
        precision=HIGHEST, preferred_element_type=F32,
    ) * (1.0 / (D ** 0.5))
    stored = jnp.exp(scores)
    cand = cand_ref[...]
    for h in range(HALF):
        hit = jnp.where(cand == dev_ref[0] * HALF + h, 1.0, 0.0)
        member = jnp.max(hit, axis=1, keepdims=True) > 0.5
        kept = jnp.where(member, stored[:, h * TILE:(h + 1) * TILE], 0.0)
        for q in range(QS):
            out_ref[pl.ds(q * HALF + h, N_ROW, stride=QS * HALF), :] = kept[q * N_ROW:(q + 1) * N_ROW]


GROUPS = 2


def permute_kernel(table_ref, packed_ref, graph_ref):
    rows = N_ROW * HALF
    perm = packed_ref[:, D:].astype(jnp.int32)
    for first in range(0, rows, 8 * GROUPS):
        spans = [slice(first + 8 * g, first + 8 * g + 8) for g in range(GROUPS)]
        low = [perm[span] & (TILE - 1) for span in spans]
        high = [perm[span] >> 7 for span in spans]
        acc = [[jnp.zeros((8, TILE), F32) for _ in spans] for _ in range(QS)]
        for sender in range(N_ROW):
            for h in range(HALF):
                hits = [x == sender * HALF + h for x in high]
                for q in range(QS):
                    line = table_ref[(sender * QS + q) * HALF + h:(sender * QS + q) * HALF + h + 1, :]
                    line = jnp.broadcast_to(line, (8, TILE))
                    for g in range(GROUPS):
                        acc[q][g] = jnp.where(hits[g], jnp.take_along_axis(line, low[g], axis=1), acc[q][g])
        for q in range(QS):
            for g, span in enumerate(spans):
                graph_ref[q, span, :] = acc[q][g]


def payload_kernel(graph_ref, low_ref, high_ref, out_ref):
    width = SLOTS * QS * HALF
    for q in range(QS):
        for h in range(HALF):
            mine = graph_ref[q, pl.ds(h, N_ROW, stride=HALF), :]
            for k, hop in enumerate(HOPS):
                hop = hop % N_ROW
                rolled = mine if hop == 0 else jnp.concatenate([mine[hop:], mine[:hop]], axis=0)
                out_ref[pl.ds((k * QS + q) * HALF + h, N_ROW, stride=width), :] = rolled
            for n, ref in enumerate((low_ref, high_ref)):
                out_ref[pl.ds(((len(HOPS) + n) * QS + q) * HALF + h, N_ROW, stride=width), :] = ref[
                    q, pl.ds(h, N_ROW, stride=HALF), :]


def first_slot(col, place_ref):
    hop = ((col >> 1) - place_ref[0]) & (N_ROW - 1)
    slot = jnp.int32(0)
    for k, h in enumerate(HOPS):
        slot = jnp.where(hop == h % N_ROW, k, slot)
    slot = slot * HALF + (col & 1)
    return jnp.where(col >= N_ROW * HALF, col - N_ROW * HALF + len(HOPS) * HALF, slot)


def any_slot(col, place_ref):
    owner = col >> 1
    hop = owner - place_ref[0]
    slot = owner >> 3
    for k, h in enumerate(SHARED + tuple(-h for h in SHARED)):
        slot = jnp.where(((hop * place_ref[1]) & (N_ROW - 1)) == h % N_ROW, N_X + k, slot)
    slot = slot * HALF + (col & 1)
    return jnp.where(col >= N_ROW * HALF, col - N_ROW * HALF + (N_X + 2 * len(SHARED)) * HALF, slot)


def split(x):
    high = x.astype(jnp.bfloat16)
    return high, (x - high.astype(F32)).astype(jnp.bfloat16)


def product(slots_ref, slot, tiles_ref, t):
    high, low = split(slots_ref[slot])
    tile_high, tile_low = split(tiles_ref[t])
    contract = (((1,), (1,)), ((), ()))
    both = lax.dot_general(jnp.concatenate([high, low], axis=0), tile_high, contract, preferred_element_type=F32)
    return both[:Q] + both[Q:] + lax.dot_general(high, tile_low, contract, preferred_element_type=F32)


def spread(slots_ref, k, block):
    for h in range(HALF):
        slots_ref[k * HALF + h] = block[:, h * TILE:(h + 1) * TILE]


def store(acc_ref, out_ref, copies_ref=None):
    for h in range(HALF):
        cols = slice(h * TILE, (h + 1) * TILE)
        out_ref[:, cols] = acc_ref[h]
        if copies_ref is not None:
            for x in range(N_X):
                copies_ref[x, :, cols] = acc_ref[h]


def first_kernel(place_ref, row_ref, col_ref, near_ref, tiles_ref, out_ref, copies_ref, own_ref, slots_ref, acc_ref):
    width = SLOTS * QS * HALF
    for k in range(SLOTS):
        for h in range(HALF):
            for q in range(QS):
                slots_ref[k * HALF + h, q * N_ROW:(q + 1) * N_ROW, :] = near_ref[
                    pl.ds((k * QS + q) * HALF + h, N_ROW, stride=width), :]
    for h in range(HALF):
        own_ref[:, h * TILE:(h + 1) * TILE] = slots_ref[h]
    acc_ref[...] = jnp.zeros_like(acc_ref)
    for t in range(tiles_ref.shape[0]):
        acc_ref[row_ref[t]] += product(slots_ref, first_slot(col_ref[t], place_ref), tiles_ref, t)
    store(acc_ref, out_ref, copies_ref)


def pair_kernel(core_ref, own_ref, low_ref, high_ref, out_ref):
    out_ref[0] = own_ref[...]
    out_ref[1] = jnp.where(core_ref[0] == 0, high_ref[...], low_ref[...])


def swap_kernel(*refs):
    *got, out_ref = refs
    for k, ref in enumerate(got):
        out_ref[k] = ref[1]


N_BLOCKS = 7


def times_s(place_ref, row_ref, col_ref, blocks, tiles_ref, slots_ref, acc_ref):
    _, line_ref, a_ref, b_ref, swapped_ref, low_ref, high_ref = blocks
    blocks = [line_ref[x] for x in range(N_X)] + [
        a_ref[0], b_ref[0], swapped_ref[0], swapped_ref[1], low_ref[...], high_ref[...]]
    for k, block in enumerate(blocks):
        spread(slots_ref, k, block)
    acc_ref[...] = jnp.zeros_like(acc_ref)
    for t in range(tiles_ref.shape[0]):
        acc_ref[row_ref[t]] += product(slots_ref, any_slot(col_ref[t], place_ref), tiles_ref, t)


def next_kernel(place_ref, row_ref, col_ref, *refs):
    tiles_ref, out_ref, copies_ref, slots_ref, acc_ref = refs[N_BLOCKS:]
    times_s(place_ref, row_ref, col_ref, refs[:N_BLOCKS], tiles_ref, slots_ref, acc_ref)
    store(acc_ref, out_ref, copies_ref)


def last_kernel(place_ref, row_ref, col_ref, *refs):
    blocks = refs[:N_BLOCKS]
    v0_ref, v1_ref, tiles_ref, out_ref, moments_ref, slots_ref, acc_ref = refs[N_BLOCKS:]
    times_s(place_ref, row_ref, col_ref, blocks, tiles_ref, slots_ref, acc_ref)
    store(acc_ref, out_ref)
    vs = [v0_ref[...], v1_ref[...], blocks[0][...], out_ref[...]]
    lane = lax.broadcasted_iota(jnp.int32, (Q, TILE), 1)
    packed = [jnp.zeros((Q, TILE), F32), jnp.zeros((Q, TILE), F32)]
    for m in range(6):
        prod = vs[m // 2] * vs[(m + 1) // 2]
        total = jnp.sum(prod[:, :TILE] + prod[:, TILE:], axis=1, keepdims=True)
        packed[m % 2] = jnp.where(lane == m // 2, total, packed[m % 2])
    moments_ref[...] = jnp.concatenate(packed, axis=0).T[:4]


def finish_kernel(moments_ref, v0_ref, v1_ref, v2_ref, v3_ref, diffused_ref, residual_ref):
    parts = [moments_ref[r] for r in range(N_REGION)]
    while len(parts) > 1:
        parts = [a + b for a, b in zip(parts[::2], parts[1::2])]
    square = jnp.concatenate([parts[0], jnp.zeros((TILE - 4, TILE), F32)], axis=0).T
    m = [square[(k % 2) * Q:(k % 2 + 1) * Q, k // 2:k // 2 + 1] for k in range(6)]
    g = [None] + [x / m[0] for x in m[1:]]
    d11 = g[2] - g[1] * g[1]
    d12 = g[3] - g[1] * g[2]
    d22 = g[4] - g[2] * g[2]
    f1 = g[4] - g[1] * g[3]
    f2 = g[5] - g[2] * g[3]
    ratio = d12 / d11
    c2 = -(f2 - ratio * f1) / (d22 - ratio * d12)
    c1 = -(f1 + d12 * c2) / d11
    c0 = -(g[3] + g[1] * c1 + g[2] * c2)
    e1 = TAU + c2
    e0 = e1 * TAU + c1
    scale = 1.0 / (e0 * TAU + c0)
    v0, v1, v2 = v0_ref[...], v1_ref[...], v2_ref[...]
    diffused_ref[...] = (TAU * scale) * (v2 + e1 * v1 + e0 * v0)
    residual_ref[...] = scale * (v3_ref[...] + c2 * v2 + c1 * v1 + c0 * v0)


SMEM = pl.BlockSpec(memory_space=pltpu.SMEM)
VMEM = pl.BlockSpec(memory_space=pltpu.VMEM)
HBM = pl.BlockSpec(memory_space=pltpu.MemorySpace.HBM)
PARAMS = pltpu.CompilerParams(vmem_limit_bytes=32 * 1024 * 1024)


def shape(*dims):
    return jax.ShapeDtypeStruct(dims, F32)


def local(queries, descriptors, candidates, cluster_perm, tile_vals, tile_row, tile_col):
    row_index = lax.axis_index("row").astype(jnp.int32)
    region = lax.axis_index("region").astype(jnp.int32)
    core = region & 1
    device = (region * N_ROW + row_index)[None]
    place = jnp.stack([row_index, 1 - 2 * core])

    packed = pl.pallas_call(
        pack_kernel, out_shape=shape(N_ROW, QS, D + TILE), in_specs=[HBM] * 2, out_specs=VMEM,
        scratch_shapes=[pltpu.VMEM(queries.shape, F32), pltpu.VMEM(cluster_perm.shape, jnp.int32),
                        pltpu.SemaphoreType.DMA((2,))],
        compiler_params=pltpu.CompilerParams(vmem_limit_bytes=64 * 1024 * 1024), name="pack",
    )(queries, cluster_perm)
    packed = lax.all_to_all(packed, "row", 0, 0, tiled=True).reshape(Q, D + TILE)
    index = jax.ShapeDtypeStruct(tile_row.shape, jnp.int32)
    by_query, tile_row, tile_col = pl.pallas_call(
        scores_kernel, out_shape=(shape(N_ROW * QS * HALF, TILE), index, index),
        in_specs=[SMEM] * 3 + [VMEM] * 3, out_specs=(VMEM, SMEM, SMEM), compiler_params=PARAMS, name="scores",
    )(device, tile_row, tile_col, packed, descriptors, candidates)
    table = lax.all_to_all(by_query.reshape(N_ROW, QS * HALF, TILE), "row", 0, 0, tiled=True)
    graph = pl.pallas_call(
        permute_kernel, out_shape=shape(QS, N_ROW * HALF, TILE), in_specs=[VMEM, VMEM], out_specs=VMEM,
        compiler_params=PARAMS, name="permute",
    )(table.reshape(N_ROW * QS * HALF, TILE), packed)

    def region_pair(v):
        return (lax.ppermute(v, "region", ring(N_REGION, 1)), lax.ppermute(v, "region", ring(N_REGION, -1)))

    def exchange(v, copies):
        low, high = region_pair(v)
        line = lax.all_to_all(
            copies, "row", 0, 0, tiled=True,
            axis_index_groups=[[x * N_Y + y for x in range(N_X)] for y in range(N_Y)])
        both = pl.pallas_call(
            pair_kernel, out_shape=shape(2, Q, ROWS), in_specs=[SMEM] + [VMEM] * 3, out_specs=VMEM,
            compiler_params=PARAMS, name="pair",
        )(core[None], v, low, high)
        got = []
        for hop in SHARED:
            pairs = [(r * N_ROW + i, r * N_ROW + (i - (hop if r % 2 == 0 else -hop)) % N_ROW)
                     for r in range(N_REGION) for i in range(N_ROW)]
            got.append(lax.ppermute(both, ("region", "row"), pairs))
        *got, line = lax.optimization_barrier((*got, line))
        swapped = pl.pallas_call(
            swap_kernel, out_shape=shape(len(got), Q, ROWS), in_specs=[VMEM] * len(got), out_specs=VMEM,
            compiler_params=PARAMS, name="swap",
        )(*got)
        swapped = lax.ppermute(swapped, "region", [(r, r ^ 1) for r in range(N_REGION)])
        return [v, line] + got + [swapped, low, high]

    slots = pltpu.VMEM((SLOTS * HALF, Q, TILE), F32)
    acc = pltpu.VMEM((HALF, Q, TILE), F32)
    width = SLOTS * QS * HALF
    near = pl.pallas_call(
        payload_kernel, out_shape=shape(N_ROW * width, TILE), in_specs=[VMEM] * 3, out_specs=VMEM,
        compiler_params=PARAMS, name="payload",
    )(graph, *region_pair(graph))
    near = lax.all_to_all(near.reshape(N_ROW, width, TILE), "row", 0, 0, tiled=True)
    with_copies = (shape(Q, ROWS), shape(N_X, Q, ROWS))
    v1, copies, v0 = pl.pallas_call(
        first_kernel, out_shape=with_copies + (shape(Q, ROWS),), in_specs=[SMEM] * 3 + [VMEM] * 2,
        out_specs=(VMEM, VMEM, VMEM), scratch_shapes=[slots, acc], compiler_params=PARAMS, name="first",
    )(place, tile_row, tile_col, near.reshape(N_ROW * width, TILE), tile_vals)
    v2, copies = pl.pallas_call(
        next_kernel, out_shape=with_copies, in_specs=[SMEM] * 3 + [VMEM] * (N_BLOCKS + 1), out_specs=(VMEM, VMEM),
        scratch_shapes=[slots, acc], compiler_params=PARAMS, name="second",
    )(place, tile_row, tile_col, *exchange(v1, copies), tile_vals)
    v3, moments = pl.pallas_call(
        last_kernel, out_shape=(shape(Q, ROWS), shape(4, TILE)),
        in_specs=[SMEM] * 3 + [VMEM] * (N_BLOCKS + 3), out_specs=(VMEM, VMEM),
        scratch_shapes=[slots, acc], compiler_params=PARAMS, name="third",
    )(place, tile_row, tile_col, *exchange(v2, copies), v0, v1, tile_vals)

    moments = lax.all_to_all(jnp.broadcast_to(moments[None], (N_ROW, 4, TILE)), "row", 0, 0, tiled=True)
    moments = jnp.sum(moments.reshape(2, 2, 2, 2, 2, 4, TILE).sum(0).sum(0).sum(0).sum(0), axis=0)
    moments = lax.all_to_all(jnp.broadcast_to(moments[None], (N_REGION, 4, TILE)), "region", 0, 0, tiled=True)
    diffused, residual = pl.pallas_call(
        finish_kernel, out_shape=(shape(Q, ROWS), shape(Q, ROWS)), in_specs=[VMEM] * 5, out_specs=(VMEM, VMEM),
        compiler_params=PARAMS, name="finish",
    )(moments, v0, v1, v2, v3)
    return (diffused, residual)


def solution(mesh):
    in_specs = (
        P("row", None),
        P(("region", "row"), None),
        P(),
        P("region", "row"),
        P(("region", "row"), None, None),
        P(("region", "row")),
        P(("region", "row")),
    )
    out_specs = (P(None, ("region", "row")), P(None, ("region", "row")))
    return jax.shard_map(local, mesh=mesh, in_specs=in_specs, out_specs=out_specs, check_vma=False)
```

```python
import jax
import jax.numpy as jnp
from jax import lax
from jax.experimental import pallas as pl
from jax.experimental.pallas import tpu as pltpu
from jax.sharding import PartitionSpec as P

Q = 64
D = 512
TILE = 128
HALF = 2
ROWS = TILE * HALF
N_ROW = 32
N_REGION = 16
QS = Q // N_ROW
HOPS = (0, 1, -1, 3, -3, 8, -8, 16)
N_X = 4
N_Y = 8
SHARED = (1, 3)
SLOTS = len(HOPS) + 2
HIGHEST = lax.Precision.HIGHEST
F32 = jnp.float32
TAU = 1.0 / 0.9


def ring(count, hop):
    return [(i, (i + hop) % count) for i in range(count)]


def pack_kernel(queries_hbm, perm_hbm, row_hbm, col_hbm, out_ref, row_ref, col_ref, queries_ref, perm_ref, sems):
    pairs = ((queries_hbm, queries_ref), (perm_hbm, perm_ref), (row_hbm, row_ref), (col_hbm, col_ref))
    copies = [pltpu.make_async_copy(src, dst, sems.at[n]) for n, (src, dst) in enumerate(pairs)]
    for copy in copies:
        copy.start()
    for copy in copies:
        copy.wait()
    perm = perm_ref[...].astype(F32)
    out_ref[:, :, :D] = jnp.broadcast_to(queries_ref[...][None], (N_ROW, QS, D))
    for h in range(HALF):
        out_ref[:, h:h + 1, D:] = jnp.broadcast_to(perm[:, h * TILE:(h + 1) * TILE][None], (N_ROW, 1, TILE))


def scores_kernel(dev_ref, packed_ref, desc_ref, cand_ref, out_ref):
    scores = lax.dot_general(
        packed_ref[:, :D], desc_ref[...], (((1,), (1,)), ((), ())),
        precision=HIGHEST, preferred_element_type=F32,
    ) * (1.0 / (D ** 0.5))
    stored = jnp.exp(scores)
    cand = cand_ref[...]
    for h in range(HALF):
        hit = jnp.where(cand == dev_ref[0] * HALF + h, 1.0, 0.0)
        member = jnp.max(hit, axis=1, keepdims=True) > 0.5
        kept = jnp.where(member, stored[:, h * TILE:(h + 1) * TILE], 0.0)
        for q in range(QS):
            out_ref[pl.ds(q * HALF + h, N_ROW, stride=QS * HALF), :] = kept[q * N_ROW:(q + 1) * N_ROW]


GROUPS = 2


def permute_kernel(table_ref, packed_ref, out_ref, graph_ref):
    rows = N_ROW * HALF
    perm = packed_ref[:, D:].astype(jnp.int32)
    for first in range(0, rows, 8 * GROUPS):
        spans = [slice(first + 8 * g, first + 8 * g + 8) for g in range(GROUPS)]
        low = [perm[span] & (TILE - 1) for span in spans]
        high = [perm[span] >> 7 for span in spans]
        acc = [[jnp.zeros((8, TILE), F32) for _ in spans] for _ in range(QS)]
        for sender in range(N_ROW):
            for h in range(HALF):
                hits = [x == sender * HALF + h for x in high]
                for q in range(QS):
                    line = table_ref[(sender * QS + q) * HALF + h:(sender * QS + q) * HALF + h + 1, :]
                    line = jnp.broadcast_to(line, (8, TILE))
                    for g in range(GROUPS):
                        acc[q][g] = jnp.where(hits[g], jnp.take_along_axis(line, low[g], axis=1), acc[q][g])
        for q in range(QS):
            for g, span in enumerate(spans):
                graph_ref[q, span, :] = acc[q][g]
    width = len(HOPS) * QS * HALF
    for q in range(QS):
        for h in range(HALF):
            mine = graph_ref[q, pl.ds(h, N_ROW, stride=HALF), :]
            for k, hop in enumerate(HOPS):
                hop = hop % N_ROW
                rolled = mine if hop == 0 else jnp.concatenate([mine[hop:], mine[:hop]], axis=0)
                out_ref[pl.ds((k * QS + q) * HALF + h, N_ROW, stride=width), :] = rolled


def near_slot(col, place_ref):
    hop = ((col >> 1) - place_ref[0]) & (N_ROW - 1)
    slot = jnp.int32(0)
    for k, h in enumerate(HOPS):
        slot = jnp.where(hop == h % N_ROW, k, slot)
    return slot * HALF + (col & 1)


def any_slot(col, place_ref):
    owner = col >> 1
    hop = owner - place_ref[0]
    slot = owner >> 3
    for k, h in enumerate(SHARED + tuple(-h for h in SHARED)):
        slot = jnp.where(((hop * place_ref[1]) & (N_ROW - 1)) == h % N_ROW, N_X + k, slot)
    slot = slot * HALF + (col & 1)
    return jnp.where(col >= N_ROW * HALF, col - N_ROW * HALF + (N_X + 2 * len(SHARED)) * HALF, slot)


def split(x):
    high = x.astype(jnp.bfloat16)
    return high, (x - high.astype(F32)).astype(jnp.bfloat16)


def product(slots_ref, slot, tiles_ref, t):
    high, low = split(slots_ref[slot])
    tile_high, tile_low = split(tiles_ref[t])
    contract = (((1,), (1,)), ((), ()))
    both = lax.dot_general(jnp.concatenate([high, low], axis=0), tile_high, contract, preferred_element_type=F32)
    return both[:Q] + both[Q:] + lax.dot_general(high, tile_low, contract, preferred_element_type=F32)


def spread(slots_ref, k, block):
    for h in range(HALF):
        slots_ref[k * HALF + h] = block[:, h * TILE:(h + 1) * TILE]


def store(acc_ref, out_ref, copies_ref=None):
    for h in range(HALF):
        cols = slice(h * TILE, (h + 1) * TILE)
        out_ref[:, cols] = acc_ref[h]
        if copies_ref is not None:
            for x in range(N_X):
                copies_ref[x, :, cols] = acc_ref[h]


def inner_kernel(place_ref, row_ref, col_ref, near_ref, tiles_ref, out_ref, slots_ref):
    width = len(HOPS) * QS * HALF
    for k in range(len(HOPS)):
        for h in range(HALF):
            for q in range(QS):
                slots_ref[k * HALF + h, q * N_ROW:(q + 1) * N_ROW, :] = near_ref[
                    pl.ds((k * QS + q) * HALF + h, N_ROW, stride=width), :]
    out_ref[...] = jnp.zeros_like(out_ref)
    for t in range(tiles_ref.shape[0]):
        inside = col_ref[t] < N_ROW * HALF
        slot = jnp.where(inside, near_slot(col_ref[t], place_ref), 0)
        out_ref[row_ref[t]] += jnp.where(inside, product(slots_ref, slot, tiles_ref, t), 0.0)


def outer_kernel(row_ref, col_ref, inner_ref, low_ref, high_ref, tiles_ref, out_ref, copies_ref, slots_ref, acc_ref):
    spread(slots_ref, 0, low_ref[...])
    spread(slots_ref, 1, high_ref[...])
    acc_ref[...] = inner_ref[...]
    for t in range(tiles_ref.shape[0]):
        @pl.when(col_ref[t] >= N_ROW * HALF)
        def _():
            acc_ref[row_ref[t]] += product(slots_ref, col_ref[t] - N_ROW * HALF, tiles_ref, t)
    store(acc_ref, out_ref, copies_ref)


def pair_kernel(core_ref, own_ref, low_ref, high_ref, out_ref):
    out_ref[0] = own_ref[...]
    out_ref[1] = jnp.where(core_ref[0] == 0, high_ref[...], low_ref[...])


def swap_kernel(*refs):
    *got, out_ref = refs
    for k, ref in enumerate(got):
        out_ref[k] = ref[1]


N_BLOCKS = 7


def times_s(place_ref, row_ref, col_ref, blocks, tiles_ref, slots_ref, acc_ref):
    _, line_ref, a_ref, b_ref, swapped_ref, low_ref, high_ref = blocks
    blocks = [line_ref[x] for x in range(N_X)] + [
        a_ref[0], b_ref[0], swapped_ref[0], swapped_ref[1], low_ref[...], high_ref[...]]
    for k, block in enumerate(blocks):
        spread(slots_ref, k, block)
    acc_ref[...] = jnp.zeros_like(acc_ref)
    for t in range(tiles_ref.shape[0]):
        acc_ref[row_ref[t]] += product(slots_ref, any_slot(col_ref[t], place_ref), tiles_ref, t)


def next_kernel(place_ref, row_ref, col_ref, *refs):
    tiles_ref, out_ref, copies_ref, slots_ref, acc_ref = refs[N_BLOCKS:]
    times_s(place_ref, row_ref, col_ref, refs[:N_BLOCKS], tiles_ref, slots_ref, acc_ref)
    store(acc_ref, out_ref, copies_ref)


def side(col, place_ref):
    hop = (col >> 1) - place_ref[0]
    kind = jnp.int32(0)
    for sign, value in ((1, 1), (-1, 2)):
        for h in SHARED:
            kind = jnp.where((hop & (N_ROW - 1)) == sign * h % N_ROW, value, kind)
    return jnp.where(col >= N_ROW * HALF, 0, kind)


def half_kernel(place_ref, row_ref, col_ref, v2_ref, line_ref, a_ref, b_ref, low_ref, high_ref, v0_ref, v1_ref, tiles_ref,
                part_ref, moments_ref, slots_ref, acc_ref):
    blocks = [line_ref[x] for x in range(N_X)] + [a_ref[...], b_ref[...], None, None, low_ref[...], high_ref[...]]
    for k, block in enumerate(blocks):
        if block is not None:
            spread(slots_ref, k, block)
    acc_ref[...] = jnp.zeros_like(acc_ref)
    for t in range(tiles_ref.shape[0]):
        kind = side(col_ref[t], place_ref)
        slot = jnp.where(kind == 2, 0, any_slot(col_ref[t], place_ref))
        acc_ref[kind * HALF + row_ref[t]] += product(slots_ref, slot, tiles_ref, t)
    doubled = []
    for h in range(HALF):
        part_ref[h] = acc_ref[h] + acc_ref[HALF + h]
        doubled.append(acc_ref[h] + 2.0 * acc_ref[HALF + h])
    vs = [v0_ref[...], v1_ref[...], v2_ref[...], jnp.concatenate(doubled, axis=1)]
    lane = lax.broadcasted_iota(jnp.int32, (Q, TILE), 1)
    packed = [jnp.zeros((Q, TILE), F32), jnp.zeros((Q, TILE), F32)]
    for m in range(6):
        prod = vs[m // 2] * vs[(m + 1) // 2]
        total = jnp.sum(prod[:, :TILE] + prod[:, TILE:], axis=1, keepdims=True)
        packed[m % 2] = jnp.where(lane == m // 2, total, packed[m % 2])
    moments_ref[...] = jnp.concatenate(packed, axis=0).T[:4]


def rest_kernel(place_ref, row_ref, col_ref, part_ref, a_ref, b_ref, tiles_ref, out_ref, slots_ref, acc_ref):
    spread(slots_ref, 0, a_ref[...])
    spread(slots_ref, 1, b_ref[...])
    acc_ref[...] = part_ref[...]
    for t in range(tiles_ref.shape[0]):
        @pl.when(side(col_ref[t], place_ref) == 2)
        def _():
            slot = any_slot(col_ref[t], place_ref) - (N_X + len(SHARED)) * HALF
            acc_ref[row_ref[t]] += product(slots_ref, slot, tiles_ref, t)
    store(acc_ref, out_ref)


def finish_kernel(moments_ref, v0_ref, v1_ref, v2_ref, v3_ref, diffused_ref, residual_ref):
    parts = [moments_ref[r] for r in range(N_REGION)]
    while len(parts) > 1:
        parts = [a + b for a, b in zip(parts[::2], parts[1::2])]
    square = jnp.concatenate([parts[0], jnp.zeros((TILE - 4, TILE), F32)], axis=0).T
    m = [square[(k % 2) * Q:(k % 2 + 1) * Q, k // 2:k // 2 + 1] for k in range(6)]
    g = [None] + [x / m[0] for x in m[1:]]
    d11 = g[2] - g[1] * g[1]
    d12 = g[3] - g[1] * g[2]
    d22 = g[4] - g[2] * g[2]
    f1 = g[4] - g[1] * g[3]
    f2 = g[5] - g[2] * g[3]
    ratio = d12 / d11
    c2 = -(f2 - ratio * f1) / (d22 - ratio * d12)
    c1 = -(f1 + d12 * c2) / d11
    c0 = -(g[3] + g[1] * c1 + g[2] * c2)
    e1 = TAU + c2
    e0 = e1 * TAU + c1
    scale = 1.0 / (e0 * TAU + c0)
    v0, v1, v2 = v0_ref[...], v1_ref[...], v2_ref[...]
    diffused_ref[...] = (TAU * scale) * (v2 + e1 * v1 + e0 * v0)
    residual_ref[...] = scale * (v3_ref[...] + c2 * v2 + c1 * v1 + c0 * v0)


SMEM = pl.BlockSpec(memory_space=pltpu.SMEM)
VMEM = pl.BlockSpec(memory_space=pltpu.VMEM)
HBM = pl.BlockSpec(memory_space=pltpu.MemorySpace.HBM)
PARAMS = pltpu.CompilerParams(vmem_limit_bytes=32 * 1024 * 1024)


def shape(*dims):
    return jax.ShapeDtypeStruct(dims, F32)


def local(queries, descriptors, candidates, cluster_perm, tile_vals, tile_row, tile_col):
    row_index = lax.axis_index("row").astype(jnp.int32)
    region = lax.axis_index("region").astype(jnp.int32)
    core = region & 1
    device = (region * N_ROW + row_index)[None]
    place = jnp.stack([row_index, 1 - 2 * core])
    upward = jnp.stack([row_index, jnp.int32(1)])

    index = jax.ShapeDtypeStruct(tile_row.shape, jnp.int32)
    packed, tile_row, tile_col = pl.pallas_call(
        pack_kernel, out_shape=(shape(N_ROW, QS, D + TILE), index, index), in_specs=[HBM] * 4, out_specs=(VMEM, SMEM, SMEM),
        scratch_shapes=[pltpu.VMEM(queries.shape, F32), pltpu.VMEM(cluster_perm.shape, jnp.int32),
                        pltpu.SemaphoreType.DMA((4,))],
        compiler_params=pltpu.CompilerParams(vmem_limit_bytes=64 * 1024 * 1024), name="pack",
    )(queries, cluster_perm, tile_row, tile_col)
    packed = lax.all_to_all(packed, "row", 0, 0, tiled=True).reshape(Q, D + TILE)
    by_query = pl.pallas_call(
        scores_kernel, out_shape=shape(N_ROW * QS * HALF, TILE), in_specs=[SMEM, VMEM, VMEM, VMEM], out_specs=VMEM,
        compiler_params=PARAMS, name="scores",
    )(device, packed, descriptors, candidates)
    table = lax.all_to_all(by_query.reshape(N_ROW, QS * HALF, TILE), "row", 0, 0, tiled=True)
    width = len(HOPS) * QS * HALF
    near = pl.pallas_call(
        permute_kernel, out_shape=shape(N_ROW * width, TILE), in_specs=[VMEM, VMEM], out_specs=VMEM,
        scratch_shapes=[pltpu.VMEM((QS, N_ROW * HALF, TILE), F32)],
        compiler_params=PARAMS, name="permute",
    )(table.reshape(N_ROW * QS * HALF, TILE), packed)
    near = lax.all_to_all(near.reshape(N_ROW, width, TILE), "row", 0, 0, tiled=True)
    v0 = near[:, :QS * HALF].reshape(N_ROW, QS, HALF, TILE).transpose(1, 0, 2, 3).reshape(Q, ROWS)

    def region_pair(v):
        return (lax.ppermute(v, "region", ring(N_REGION, 1)), lax.ppermute(v, "region", ring(N_REGION, -1)))

    def x_line(copies):
        return lax.all_to_all(
            copies, "row", 0, 0, tiled=True,
            axis_index_groups=[[x * N_Y + y for x in range(N_X)] for y in range(N_Y)])

    def exchange(v, copies):
        low, high = region_pair(v)
        line = x_line(copies)
        both = pl.pallas_call(
            pair_kernel, out_shape=shape(2, Q, ROWS), in_specs=[SMEM] + [VMEM] * 3, out_specs=VMEM,
            compiler_params=PARAMS, name="pair",
        )(core[None], v, low, high)
        got = []
        for hop in SHARED:
            pairs = [(r * N_ROW + i, r * N_ROW + (i - (hop if r % 2 == 0 else -hop)) % N_ROW)
                     for r in range(N_REGION) for i in range(N_ROW)]
            got.append(lax.ppermute(both, ("region", "row"), pairs))
        *got, line = lax.optimization_barrier((*got, line))
        swapped = pl.pallas_call(
            swap_kernel, out_shape=shape(len(got), Q, ROWS), in_specs=[VMEM] * len(got), out_specs=VMEM,
            compiler_params=PARAMS, name="swap",
        )(*got)
        swapped = lax.ppermute(swapped, "region", [(r, r ^ 1) for r in range(N_REGION)])
        return [v, line] + got + [swapped, low, high]

    slots = pltpu.VMEM((SLOTS * HALF, Q, TILE), F32)
    acc = pltpu.VMEM((HALF, Q, TILE), F32)
    low, high = region_pair(v0)
    inner = pl.pallas_call(
        inner_kernel, out_shape=shape(HALF, Q, TILE), in_specs=[SMEM] * 3 + [VMEM] * 2, out_specs=VMEM,
        scratch_shapes=[pltpu.VMEM((len(HOPS) * HALF, Q, TILE), F32)],
        cost_estimate=pl.CostEstimate(flops=2 * 12 * Q * TILE * TILE, bytes_accessed=2000000, transcendentals=0),
        compiler_params=PARAMS, name="first_inner",
    )(place, tile_row, tile_col, near.reshape(N_ROW * width, TILE), tile_vals)
    with_copies = (shape(Q, ROWS), shape(N_X, Q, ROWS))
    v1, copies = pl.pallas_call(
        outer_kernel, out_shape=with_copies, in_specs=[SMEM] * 2 + [VMEM] * 4, out_specs=(VMEM, VMEM),
        scratch_shapes=[pltpu.VMEM((2 * HALF, Q, TILE), F32), acc], compiler_params=PARAMS, name="first_outer",
    )(tile_row, tile_col, inner, low, high, tile_vals)
    v2, copies = pl.pallas_call(
        next_kernel, out_shape=with_copies, in_specs=[SMEM] * 3 + [VMEM] * (N_BLOCKS + 1), out_specs=(VMEM, VMEM),
        scratch_shapes=[slots, acc], compiler_params=PARAMS, name="second",
    )(place, tile_row, tile_col, *exchange(v1, copies), tile_vals)
    ahead = [lax.ppermute(v2, "row", ring(N_ROW, -hop)) for hop in SHARED]
    part, moments = pl.pallas_call(
        half_kernel, out_shape=(shape(HALF, Q, TILE), shape(4, TILE)), in_specs=[SMEM] * 3 + [VMEM] * 9,
        out_specs=(VMEM, VMEM), scratch_shapes=[slots, pltpu.VMEM((3 * HALF, Q, TILE), F32)],
        compiler_params=PARAMS, name="half",
    )(upward, tile_row, tile_col, v2, x_line(copies), *ahead, *region_pair(v2), v0, v1, tile_vals)
    later, moments = lax.optimization_barrier((v2, moments))
    behind = [lax.ppermute(later, "row", ring(N_ROW, hop)) for hop in SHARED]
    v3 = pl.pallas_call(
        rest_kernel, out_shape=shape(Q, ROWS), in_specs=[SMEM] * 3 + [VMEM] * 4, out_specs=VMEM,
        scratch_shapes=[pltpu.VMEM((2 * HALF, Q, TILE), F32), acc],
        cost_estimate=pl.CostEstimate(flops=2 * 12 * Q * TILE * TILE, bytes_accessed=2000000, transcendentals=0),
        compiler_params=PARAMS, name="rest",
    )(upward, tile_row, tile_col, part, *behind, tile_vals)

    moments = lax.all_to_all(jnp.broadcast_to(moments[None], (N_ROW, 4, TILE)), "row", 0, 0, tiled=True)
    moments = jnp.sum(moments.reshape(2, 2, 2, 2, 2, 4, TILE).sum(0).sum(0).sum(0).sum(0), axis=0)
    moments = lax.all_to_all(jnp.broadcast_to(moments[None], (N_REGION, 4, TILE)), "region", 0, 0, tiled=True)
    diffused, residual = pl.pallas_call(
        finish_kernel, out_shape=(shape(Q, ROWS), shape(Q, ROWS)), in_specs=[VMEM] * 5, out_specs=(VMEM, VMEM),
        compiler_params=PARAMS, name="finish",
    )(moments, v0, v1, v2, v3)
    return (diffused, residual)


def solution(mesh):
    in_specs = (
        P("row", None),
        P(("region", "row"), None),
        P(),
        P("region", "row"),
        P(("region", "row"), None, None),
        P(("region", "row")),
        P(("region", "row")),
    )
    out_specs = (P(None, ("region", "row")), P(None, ("region", "row")))
    return jax.shard_map(local, mesh=mesh, in_specs=in_specs, out_specs=out_specs, check_vma=False)
```

```python
import jax
import jax.numpy as jnp
from jax import lax
from jax.experimental import pallas as pl
from jax.experimental.pallas import tpu as pltpu
from jax.sharding import PartitionSpec as P

Q = 64
D = 512
TILE = 128
HALF = 2
ROWS = TILE * HALF
N_ROW = 32
N_REGION = 16
QS = Q // N_ROW
HOPS = (0, 1, -1, 3, -3, 8, -8, 16)
N_X = 4
N_Y = 8
SHARED = (1, 3)
SLOTS = len(HOPS) + 2
HIGHEST = lax.Precision.HIGHEST
F32 = jnp.float32
TAU = 1.0 / 0.9


def ring(count, hop):
    return [(i, (i + hop) % count) for i in range(count)]


def pack_kernel(queries_hbm, perm_hbm, row_hbm, col_hbm, out_ref, row_ref, col_ref, queries_ref, perm_ref, sems):
    pairs = ((queries_hbm, queries_ref), (perm_hbm, perm_ref), (row_hbm, row_ref), (col_hbm, col_ref))
    copies = [pltpu.make_async_copy(src, dst, sems.at[n]) for n, (src, dst) in enumerate(pairs)]
    for copy in copies:
        copy.start()
    for copy in copies:
        copy.wait()
    perm = perm_ref[...].astype(F32)
    out_ref[:, :, :D] = jnp.broadcast_to(queries_ref[...][None], (N_ROW, QS, D))
    for h in range(HALF):
        out_ref[:, h:h + 1, D:] = jnp.broadcast_to(perm[:, h * TILE:(h + 1) * TILE][None], (N_ROW, 1, TILE))


def scores_kernel(dev_ref, packed_ref, desc_ref, cand_ref, out_ref):
    scores = lax.dot_general(
        packed_ref[:, :D], desc_ref[...], (((1,), (1,)), ((), ())),
        precision=HIGHEST, preferred_element_type=F32,
    ) * (1.0 / (D ** 0.5))
    stored = jnp.exp(scores)
    cand = cand_ref[...]
    for h in range(HALF):
        hit = jnp.where(cand == dev_ref[0] * HALF + h, 1.0, 0.0)
        member = jnp.max(hit, axis=1, keepdims=True) > 0.5
        kept = jnp.where(member, stored[:, h * TILE:(h + 1) * TILE], 0.0)
        for q in range(QS):
            out_ref[pl.ds(q * HALF + h, N_ROW, stride=QS * HALF), :] = kept[q * N_ROW:(q + 1) * N_ROW]


GROUPS = 2


def permute_kernel(table_ref, packed_ref, out_ref, graph_ref):
    rows = N_ROW * HALF
    perm = packed_ref[:, D:].astype(jnp.int32)
    for first in range(0, rows, 8 * GROUPS):
        spans = [slice(first + 8 * g, first + 8 * g + 8) for g in range(GROUPS)]
        low = [perm[span] & (TILE - 1) for span in spans]
        high = [perm[span] >> 7 for span in spans]
        acc = [[jnp.zeros((8, TILE), F32) for _ in spans] for _ in range(QS)]
        for sender in range(N_ROW):
            for h in range(HALF):
                hits = [x == sender * HALF + h for x in high]
                for q in range(QS):
                    line = table_ref[(sender * QS + q) * HALF + h:(sender * QS + q) * HALF + h + 1, :]
                    line = jnp.broadcast_to(line, (8, TILE))
                    for g in range(GROUPS):
                        acc[q][g] = jnp.where(hits[g], jnp.take_along_axis(line, low[g], axis=1), acc[q][g])
        for q in range(QS):
            for g, span in enumerate(spans):
                graph_ref[q, span, :] = acc[q][g]
    width = len(HOPS) * QS * HALF
    for q in range(QS):
        for h in range(HALF):
            mine = graph_ref[q, pl.ds(h, N_ROW, stride=HALF), :]
            for k, hop in enumerate(HOPS):
                hop = hop % N_ROW
                rolled = mine if hop == 0 else jnp.concatenate([mine[hop:], mine[:hop]], axis=0)
                out_ref[pl.ds((k * QS + q) * HALF + h, N_ROW, stride=width), :] = rolled


def near_slot(col, place_ref):
    hop = ((col >> 1) - place_ref[0]) & (N_ROW - 1)
    slot = jnp.int32(0)
    for k, h in enumerate(HOPS):
        slot = jnp.where(hop == h % N_ROW, k, slot)
    return slot * HALF + (col & 1)


def any_slot(col, place_ref):
    owner = col >> 1
    hop = owner - place_ref[0]
    slot = owner >> 3
    for k, h in enumerate(SHARED + tuple(-h for h in SHARED)):
        slot = jnp.where(((hop * place_ref[1]) & (N_ROW - 1)) == h % N_ROW, N_X + k, slot)
    slot = slot * HALF + (col & 1)
    return jnp.where(col >= N_ROW * HALF, col - N_ROW * HALF + (N_X + 2 * len(SHARED)) * HALF, slot)


def split(x):
    high = x.astype(jnp.bfloat16)
    return high, (x - high.astype(F32)).astype(jnp.bfloat16)


def product(slots_ref, slot, tiles_ref, t):
    high, low = split(slots_ref[slot])
    tile_high, tile_low = split(tiles_ref[t])
    contract = (((1,), (1,)), ((), ()))
    both = lax.dot_general(jnp.concatenate([high, low], axis=0), tile_high, contract, preferred_element_type=F32)
    return both[:Q] + both[Q:] + lax.dot_general(high, tile_low, contract, preferred_element_type=F32)


def spread(slots_ref, k, block):
    for h in range(HALF):
        slots_ref[k * HALF + h] = block[:, h * TILE:(h + 1) * TILE]


def store(acc_ref, out_ref, copies_ref=None):
    for h in range(HALF):
        cols = slice(h * TILE, (h + 1) * TILE)
        out_ref[:, cols] = acc_ref[h]
        if copies_ref is not None:
            for x in range(N_X):
                copies_ref[x, :, cols] = acc_ref[h]


def inner_kernel(place_ref, row_ref, col_ref, near_ref, tiles_ref, out_ref, slots_ref):
    width = len(HOPS) * QS * HALF
    for k in range(len(HOPS)):
        for h in range(HALF):
            for q in range(QS):
                slots_ref[k * HALF + h, q * N_ROW:(q + 1) * N_ROW, :] = near_ref[
                    pl.ds((k * QS + q) * HALF + h, N_ROW, stride=width), :]
    out_ref[...] = jnp.zeros_like(out_ref)
    for t in range(tiles_ref.shape[0]):
        inside = col_ref[t] < N_ROW * HALF
        slot = jnp.where(inside, near_slot(col_ref[t], place_ref), 0)
        out_ref[row_ref[t]] += jnp.where(inside, product(slots_ref, slot, tiles_ref, t), 0.0)


def outer_kernel(row_ref, col_ref, inner_ref, low_ref, high_ref, tiles_ref, out_ref, copies_ref, slots_ref, acc_ref):
    spread(slots_ref, 0, low_ref[...])
    spread(slots_ref, 1, high_ref[...])
    acc_ref[...] = inner_ref[...]
    for t in range(tiles_ref.shape[0]):
        @pl.when(col_ref[t] >= N_ROW * HALF)
        def _():
            acc_ref[row_ref[t]] += product(slots_ref, col_ref[t] - N_ROW * HALF, tiles_ref, t)
    store(acc_ref, out_ref, copies_ref)


def pair_kernel(core_ref, own_ref, low_ref, high_ref, out_ref):
    out_ref[0] = own_ref[...]
    out_ref[1] = jnp.where(core_ref[0] == 0, high_ref[...], low_ref[...])


def swap_kernel(*refs):
    *got, out_ref = refs
    for k, ref in enumerate(got):
        out_ref[k] = ref[1]


N_BLOCKS = 7


def times_s(place_ref, row_ref, col_ref, blocks, tiles_ref, slots_ref, acc_ref):
    _, line_ref, a_ref, b_ref, swapped_ref, low_ref, high_ref = blocks
    blocks = [line_ref[x] for x in range(N_X)] + [
        a_ref[0], b_ref[0], swapped_ref[0], swapped_ref[1], low_ref[...], high_ref[...]]
    for k, block in enumerate(blocks):
        spread(slots_ref, k, block)
    acc_ref[...] = jnp.zeros_like(acc_ref)
    for t in range(tiles_ref.shape[0]):
        acc_ref[row_ref[t]] += product(slots_ref, any_slot(col_ref[t], place_ref), tiles_ref, t)


def next_kernel(place_ref, row_ref, col_ref, *refs):
    tiles_ref, out_ref, copies_ref, slots_ref, acc_ref = refs[N_BLOCKS:]
    times_s(place_ref, row_ref, col_ref, refs[:N_BLOCKS], tiles_ref, slots_ref, acc_ref)
    store(acc_ref, out_ref, copies_ref)


def side(col, place_ref):
    hop = (col >> 1) - place_ref[0]
    kind = jnp.int32(0)
    for sign, value in ((1, 1), (-1, 2)):
        for h in SHARED:
            kind = jnp.where((hop & (N_ROW - 1)) == sign * h % N_ROW, value, kind)
    return jnp.where(col >= N_ROW * HALF, 0, kind)


def half_kernel(place_ref, row_ref, col_ref, v2_ref, line_ref, low_ref, high_ref, a_ref, b_ref, v0_ref, v1_ref, tiles_ref,
                part_ref, moments_ref, slots_ref, acc_ref):
    blocks = [line_ref[x] for x in range(N_X)] + [a_ref[...], b_ref[...], None, None, low_ref[...], high_ref[...]]
    for k, block in enumerate(blocks):
        if block is not None:
            spread(slots_ref, k, block)
    acc_ref[...] = jnp.zeros_like(acc_ref)
    for t in range(tiles_ref.shape[0]):
        kind = side(col_ref[t], place_ref)
        slot = jnp.where(kind == 2, 0, any_slot(col_ref[t], place_ref))
        acc_ref[kind * HALF + row_ref[t]] += product(slots_ref, slot, tiles_ref, t)
    doubled = []
    for h in range(HALF):
        part_ref[h] = acc_ref[h] + acc_ref[HALF + h]
        doubled.append(acc_ref[h] + 2.0 * acc_ref[HALF + h])
    vs = [v0_ref[...], v1_ref[...], v2_ref[...], jnp.concatenate(doubled, axis=1)]
    lane = lax.broadcasted_iota(jnp.int32, (Q, TILE), 1)
    packed = [jnp.zeros((Q, TILE), F32), jnp.zeros((Q, TILE), F32)]
    for m in range(6):
        prod = vs[m // 2] * vs[(m + 1) // 2]
        total = jnp.sum(prod[:, :TILE] + prod[:, TILE:], axis=1, keepdims=True)
        packed[m % 2] = jnp.where(lane == m // 2, total, packed[m % 2])
    moments_ref[...] = jnp.concatenate(packed, axis=0).T[:4]


def rest_kernel(place_ref, row_ref, col_ref, part_ref, a_ref, b_ref, tiles_ref, out_ref, slots_ref, acc_ref):
    spread(slots_ref, 0, a_ref[...])
    spread(slots_ref, 1, b_ref[...])
    acc_ref[...] = part_ref[...]
    for t in range(tiles_ref.shape[0]):
        @pl.when(side(col_ref[t], place_ref) == 2)
        def _():
            slot = any_slot(col_ref[t], place_ref) - (N_X + len(SHARED)) * HALF
            acc_ref[row_ref[t]] += product(slots_ref, slot, tiles_ref, t)
    store(acc_ref, out_ref)


def finish_kernel(moments_ref, v0_ref, v1_ref, v2_ref, v3_ref, diffused_ref, residual_ref):
    parts = [moments_ref[r] for r in range(N_REGION)]
    while len(parts) > 1:
        parts = [a + b for a, b in zip(parts[::2], parts[1::2])]
    square = jnp.concatenate([parts[0], jnp.zeros((TILE - 4, TILE), F32)], axis=0).T
    m = [square[(k % 2) * Q:(k % 2 + 1) * Q, k // 2:k // 2 + 1] for k in range(6)]
    g = [None] + [x / m[0] for x in m[1:]]
    d11 = g[2] - g[1] * g[1]
    d12 = g[3] - g[1] * g[2]
    d22 = g[4] - g[2] * g[2]
    f1 = g[4] - g[1] * g[3]
    f2 = g[5] - g[2] * g[3]
    ratio = d12 / d11
    c2 = -(f2 - ratio * f1) / (d22 - ratio * d12)
    c1 = -(f1 + d12 * c2) / d11
    c0 = -(g[3] + g[1] * c1 + g[2] * c2)
    e1 = TAU + c2
    e0 = e1 * TAU + c1
    scale = 1.0 / (e0 * TAU + c0)
    v0, v1, v2 = v0_ref[...], v1_ref[...], v2_ref[...]
    diffused_ref[...] = (TAU * scale) * (v2 + e1 * v1 + e0 * v0)
    residual_ref[...] = scale * (v3_ref[...] + c2 * v2 + c1 * v1 + c0 * v0)


SMEM = pl.BlockSpec(memory_space=pltpu.SMEM)
VMEM = pl.BlockSpec(memory_space=pltpu.VMEM)
HBM = pl.BlockSpec(memory_space=pltpu.MemorySpace.HBM)
PARAMS = pltpu.CompilerParams(vmem_limit_bytes=32 * 1024 * 1024)


def shape(*dims):
    return jax.ShapeDtypeStruct(dims, F32)


def local(queries, descriptors, candidates, cluster_perm, tile_vals, tile_row, tile_col):
    row_index = lax.axis_index("row").astype(jnp.int32)
    region = lax.axis_index("region").astype(jnp.int32)
    core = region & 1
    device = (region * N_ROW + row_index)[None]
    place = jnp.stack([row_index, 1 - 2 * core])
    upward = jnp.stack([row_index, jnp.int32(1)])

    index = jax.ShapeDtypeStruct(tile_row.shape, jnp.int32)
    packed, tile_row, tile_col = pl.pallas_call(
        pack_kernel, out_shape=(shape(N_ROW, QS, D + TILE), index, index), in_specs=[HBM] * 4, out_specs=(VMEM, SMEM, SMEM),
        scratch_shapes=[pltpu.VMEM(queries.shape, F32), pltpu.VMEM(cluster_perm.shape, jnp.int32),
                        pltpu.SemaphoreType.DMA((4,))],
        compiler_params=pltpu.CompilerParams(vmem_limit_bytes=64 * 1024 * 1024), name="pack",
    )(queries, cluster_perm, tile_row, tile_col)
    packed = lax.all_to_all(packed, "row", 0, 0, tiled=True).reshape(Q, D + TILE)
    by_query = pl.pallas_call(
        scores_kernel, out_shape=shape(N_ROW * QS * HALF, TILE), in_specs=[SMEM, VMEM, VMEM, VMEM], out_specs=VMEM,
        compiler_params=PARAMS, name="scores",
    )(device, packed, descriptors, candidates)
    table = lax.all_to_all(by_query.reshape(N_ROW, QS * HALF, TILE), "row", 0, 0, tiled=True)
    width = len(HOPS) * QS * HALF
    near = pl.pallas_call(
        permute_kernel, out_shape=shape(N_ROW * width, TILE), in_specs=[VMEM, VMEM], out_specs=VMEM,
        scratch_shapes=[pltpu.VMEM((QS, N_ROW * HALF, TILE), F32)],
        compiler_params=PARAMS, name="permute",
    )(table.reshape(N_ROW * QS * HALF, TILE), packed)
    near = lax.all_to_all(near.reshape(N_ROW, width, TILE), "row", 0, 0, tiled=True)
    v0 = near[:, :QS * HALF].reshape(N_ROW, QS, HALF, TILE).transpose(1, 0, 2, 3).reshape(Q, ROWS)

    def region_pair(v):
        return (lax.ppermute(v, "region", ring(N_REGION, 1)), lax.ppermute(v, "region", ring(N_REGION, -1)))

    def x_line(copies):
        return lax.all_to_all(
            copies, "row", 0, 0, tiled=True,
            axis_index_groups=[[x * N_Y + y for x in range(N_X)] for y in range(N_Y)])

    def exchange(v, copies):
        low, high = region_pair(v)
        line = x_line(copies)
        both = pl.pallas_call(
            pair_kernel, out_shape=shape(2, Q, ROWS), in_specs=[SMEM] + [VMEM] * 3, out_specs=VMEM,
            compiler_params=PARAMS, name="pair",
        )(core[None], v, low, high)
        got = []
        for hop in SHARED:
            pairs = [(r * N_ROW + i, r * N_ROW + (i - (hop if r % 2 == 0 else -hop)) % N_ROW)
                     for r in range(N_REGION) for i in range(N_ROW)]
            got.append(lax.ppermute(both, ("region", "row"), pairs))
        *got, line = lax.optimization_barrier((*got, line))
        swapped = pl.pallas_call(
            swap_kernel, out_shape=shape(len(got), Q, ROWS), in_specs=[VMEM] * len(got), out_specs=VMEM,
            compiler_params=PARAMS, name="swap",
        )(*got)
        swapped = lax.ppermute(swapped, "region", [(r, r ^ 1) for r in range(N_REGION)])
        return [v, line] + got + [swapped, low, high]

    slots = pltpu.VMEM((SLOTS * HALF, Q, TILE), F32)
    acc = pltpu.VMEM((HALF, Q, TILE), F32)
    low, high = region_pair(v0)
    inner = pl.pallas_call(
        inner_kernel, out_shape=shape(HALF, Q, TILE), in_specs=[SMEM] * 3 + [VMEM] * 2, out_specs=VMEM,
        scratch_shapes=[pltpu.VMEM((len(HOPS) * HALF, Q, TILE), F32)],
        cost_estimate=pl.CostEstimate(flops=2 * 12 * Q * TILE * TILE, bytes_accessed=2000000, transcendentals=0),
        compiler_params=PARAMS, name="first_inner",
    )(place, tile_row, tile_col, near.reshape(N_ROW * width, TILE), tile_vals)
    with_copies = (shape(Q, ROWS), shape(N_X, Q, ROWS))
    v1, copies = pl.pallas_call(
        outer_kernel, out_shape=with_copies, in_specs=[SMEM] * 2 + [VMEM] * 4, out_specs=(VMEM, VMEM),
        scratch_shapes=[pltpu.VMEM((2 * HALF, Q, TILE), F32), acc], compiler_params=PARAMS, name="first_outer",
    )(tile_row, tile_col, inner, low, high, tile_vals)
    v2, copies = pl.pallas_call(
        next_kernel, out_shape=with_copies, in_specs=[SMEM] * 3 + [VMEM] * (N_BLOCKS + 1), out_specs=(VMEM, VMEM),
        scratch_shapes=[slots, acc], compiler_params=PARAMS, name="second",
    )(place, tile_row, tile_col, *exchange(v1, copies), tile_vals)
    low, high = region_pair(v2)
    ahead = [lax.ppermute(v2, "row", ring(N_ROW, -hop)) for hop in SHARED]
    part, moments = pl.pallas_call(
        half_kernel, out_shape=(shape(HALF, Q, TILE), shape(4, TILE)), in_specs=[SMEM] * 3 + [VMEM] * 9,
        out_specs=(VMEM, VMEM), scratch_shapes=[slots, pltpu.VMEM((3 * HALF, Q, TILE), F32)],
        compiler_params=PARAMS, name="half",
    )(upward, tile_row, tile_col, v2, x_line(copies), low, high, *ahead, v0, v1, tile_vals)
    v2_now, moments = lax.optimization_barrier((v2, moments))
    behind = [lax.ppermute(v2_now, "row", ring(N_ROW, hop)) for hop in SHARED]
    moments = lax.all_to_all(jnp.broadcast_to(moments[None], (N_ROW, 4, TILE)), "row", 0, 0, tiled=True)
    moments = jnp.sum(moments.reshape(2, 2, 2, 2, 2, 4, TILE).sum(0).sum(0).sum(0).sum(0), axis=0)
    v3 = pl.pallas_call(
        rest_kernel, out_shape=shape(Q, ROWS), in_specs=[SMEM] * 3 + [VMEM] * 4, out_specs=VMEM,
        scratch_shapes=[pltpu.VMEM((2 * HALF, Q, TILE), F32), acc],
        cost_estimate=pl.CostEstimate(flops=2 * 12 * Q * TILE * TILE, bytes_accessed=2000000, transcendentals=0),
        compiler_params=PARAMS, name="rest",
    )(upward, tile_row, tile_col, part, *behind, tile_vals)
    moments = lax.all_to_all(jnp.broadcast_to(moments[None], (N_REGION, 4, TILE)), "region", 0, 0, tiled=True)
    diffused, residual = pl.pallas_call(
        finish_kernel, out_shape=(shape(Q, ROWS), shape(Q, ROWS)), in_specs=[VMEM] * 5, out_specs=(VMEM, VMEM),
        compiler_params=PARAMS, name="finish",
    )(moments, v0, v1, v2, v3)
    return (diffused, residual)


def solution(mesh):
    in_specs = (
        P("row", None),
        P(("region", "row"), None),
        P(),
        P("region", "row"),
        P(("region", "row"), None, None),
        P(("region", "row")),
        P(("region", "row")),
    )
    out_specs = (P(None, ("region", "row")), P(None, ("region", "row")))
    return jax.shard_map(local, mesh=mesh, in_specs=in_specs, out_specs=out_specs, check_vma=False)
```

```python
import jax
import jax.numpy as jnp
from jax import lax
from jax.experimental import pallas as pl
from jax.experimental.pallas import tpu as pltpu
from jax.sharding import PartitionSpec as P

Q = 64
D = 512
TILE = 128
HALF = 2
ROWS = TILE * HALF
N_ROW = 32
N_REGION = 16
QS = Q // N_ROW
HOPS = (0, 1, -1, 3, -3, 8, -8, 16)
N_X = 4
N_Y = 8
SHARED = (1, 3)
SLOTS = len(HOPS) + 2
HIGHEST = lax.Precision.HIGHEST
F32 = jnp.float32
TAU = 1.0 / 0.9


def ring(count, hop):
    return [(i, (i + hop) % count) for i in range(count)]


def pack_kernel(queries_hbm, perm_hbm, row_hbm, col_hbm, out_ref, row_ref, col_ref, queries_ref, perm_ref, sems):
    pairs = ((queries_hbm, queries_ref), (perm_hbm, perm_ref), (row_hbm, row_ref), (col_hbm, col_ref))
    copies = [pltpu.make_async_copy(src, dst, sems.at[n]) for n, (src, dst) in enumerate(pairs)]
    for copy in copies:
        copy.start()
    for copy in copies:
        copy.wait()
    perm = perm_ref[...].astype(F32)
    out_ref[:, :, :D] = jnp.broadcast_to(queries_ref[...][None], (N_ROW, QS, D))
    for h in range(HALF):
        out_ref[:, h:h + 1, D:] = jnp.broadcast_to(perm[:, h * TILE:(h + 1) * TILE][None], (N_ROW, 1, TILE))


def scores_kernel(dev_ref, packed_ref, desc_ref, cand_ref, out_ref):
    scores = lax.dot_general(
        packed_ref[:, :D], desc_ref[...], (((1,), (1,)), ((), ())),
        precision=HIGHEST, preferred_element_type=F32,
    ) * (1.0 / (D ** 0.5))
    stored = jnp.exp(scores)
    cand = cand_ref[...]
    for h in range(HALF):
        hit = jnp.where(cand == dev_ref[0] * HALF + h, 1.0, 0.0)
        member = jnp.max(hit, axis=1, keepdims=True) > 0.5
        kept = jnp.where(member, stored[:, h * TILE:(h + 1) * TILE], 0.0)
        for q in range(QS):
            out_ref[pl.ds(q * HALF + h, N_ROW, stride=QS * HALF), :] = kept[q * N_ROW:(q + 1) * N_ROW]


GROUPS = 2


def permute_kernel(table_ref, packed_ref, out_ref, graph_ref):
    rows = N_ROW * HALF
    perm = packed_ref[:, D:].astype(jnp.int32)
    for first in range(0, rows, 8 * GROUPS):
        spans = [slice(first + 8 * g, first + 8 * g + 8) for g in range(GROUPS)]
        low = [perm[span] & (TILE - 1) for span in spans]
        high = [perm[span] >> 7 for span in spans]
        acc = [[jnp.zeros((8, TILE), F32) for _ in spans] for _ in range(QS)]
        for sender in range(N_ROW):
            for h in range(HALF):
                hits = [x == sender * HALF + h for x in high]
                for q in range(QS):
                    line = table_ref[(sender * QS + q) * HALF + h:(sender * QS + q) * HALF + h + 1, :]
                    line = jnp.broadcast_to(line, (8, TILE))
                    for g in range(GROUPS):
                        acc[q][g] = jnp.where(hits[g], jnp.take_along_axis(line, low[g], axis=1), acc[q][g])
        for q in range(QS):
            for g, span in enumerate(spans):
                graph_ref[q, span, :] = acc[q][g]
    width = len(HOPS) * QS * HALF
    for q in range(QS):
        for h in range(HALF):
            mine = graph_ref[q, pl.ds(h, N_ROW, stride=HALF), :]
            for k, hop in enumerate(HOPS):
                hop = hop % N_ROW
                rolled = mine if hop == 0 else jnp.concatenate([mine[hop:], mine[:hop]], axis=0)
                out_ref[pl.ds((k * QS + q) * HALF + h, N_ROW, stride=width), :] = rolled


def near_slot(col, place_ref):
    hop = ((col >> 1) - place_ref[0]) & (N_ROW - 1)
    slot = jnp.int32(0)
    for k, h in enumerate(HOPS):
        slot = jnp.where(hop == h % N_ROW, k, slot)
    return slot * HALF + (col & 1)


def any_slot(col, place_ref):
    owner = col >> 1
    hop = owner - place_ref[0]
    slot = owner >> 3
    for k, h in enumerate(SHARED + tuple(-h for h in SHARED)):
        slot = jnp.where(((hop * place_ref[1]) & (N_ROW - 1)) == h % N_ROW, N_X + k, slot)
    slot = slot * HALF + (col & 1)
    return jnp.where(col >= N_ROW * HALF, col - N_ROW * HALF + (N_X + 2 * len(SHARED)) * HALF, slot)


def split(x):
    high = x.astype(jnp.bfloat16)
    return high, (x - high.astype(F32)).astype(jnp.bfloat16)


def product(slots_ref, slot, tiles_ref, t):
    high, low = split(slots_ref[slot])
    tile_high, tile_low = split(tiles_ref[t])
    contract = (((1,), (1,)), ((), ()))
    both = lax.dot_general(jnp.concatenate([high, low], axis=0), tile_high, contract, preferred_element_type=F32)
    return both[:Q] + both[Q:] + lax.dot_general(high, tile_low, contract, preferred_element_type=F32)


def spread(slots_ref, k, block):
    for h in range(HALF):
        slots_ref[k * HALF + h] = block[:, h * TILE:(h + 1) * TILE]


def store(acc_ref, out_ref, copies_ref=None):
    for h in range(HALF):
        cols = slice(h * TILE, (h + 1) * TILE)
        out_ref[:, cols] = acc_ref[h]
        if copies_ref is not None:
            for x in range(N_X):
                copies_ref[x, :, cols] = acc_ref[h]


def inner_kernel(place_ref, row_ref, col_ref, near_ref, tiles_ref, out_ref, slots_ref):
    width = len(HOPS) * QS * HALF
    for k in range(len(HOPS)):
        for h in range(HALF):
            for q in range(QS):
                slots_ref[k * HALF + h, q * N_ROW:(q + 1) * N_ROW, :] = near_ref[
                    pl.ds((k * QS + q) * HALF + h, N_ROW, stride=width), :]
    out_ref[...] = jnp.zeros_like(out_ref)
    for t in range(tiles_ref.shape[0]):
        inside = col_ref[t] < N_ROW * HALF
        slot = jnp.where(inside, near_slot(col_ref[t], place_ref), 0)
        out_ref[row_ref[t]] += jnp.where(inside, product(slots_ref, slot, tiles_ref, t), 0.0)


def outer_kernel(row_ref, col_ref, inner_ref, low_ref, high_ref, tiles_ref, out_ref, copies_ref, slots_ref, acc_ref):
    spread(slots_ref, 0, low_ref[...])
    spread(slots_ref, 1, high_ref[...])
    acc_ref[...] = inner_ref[...]
    for t in range(tiles_ref.shape[0]):
        @pl.when(col_ref[t] >= N_ROW * HALF)
        def _():
            acc_ref[row_ref[t]] += product(slots_ref, col_ref[t] - N_ROW * HALF, tiles_ref, t)
    store(acc_ref, out_ref, copies_ref)


def pair_kernel(core_ref, own_ref, low_ref, high_ref, out_ref):
    out_ref[0] = own_ref[...]
    out_ref[1] = jnp.where(core_ref[0] == 0, high_ref[...], low_ref[...])


def swap_kernel(*refs):
    *got, out_ref = refs
    for k, ref in enumerate(got):
        out_ref[k] = ref[1]


N_BLOCKS = 7


def times_s(place_ref, row_ref, col_ref, blocks, tiles_ref, slots_ref, acc_ref):
    _, line_ref, a_ref, b_ref, swapped_ref, low_ref, high_ref = blocks
    blocks = [line_ref[x] for x in range(N_X)] + [
        a_ref[0], b_ref[0], swapped_ref[0], swapped_ref[1], low_ref[...], high_ref[...]]
    for k, block in enumerate(blocks):
        spread(slots_ref, k, block)
    acc_ref[...] = jnp.zeros_like(acc_ref)
    for t in range(tiles_ref.shape[0]):
        acc_ref[row_ref[t]] += product(slots_ref, any_slot(col_ref[t], place_ref), tiles_ref, t)


def next_kernel(place_ref, row_ref, col_ref, *refs):
    tiles_ref, out_ref, copies_ref, slots_ref, acc_ref = refs[N_BLOCKS:]
    times_s(place_ref, row_ref, col_ref, refs[:N_BLOCKS], tiles_ref, slots_ref, acc_ref)
    store(acc_ref, out_ref, copies_ref)


def side(col, place_ref):
    hop = ((col >> 1) - place_ref[0]) * place_ref[1]
    kind = jnp.int32(0)
    for sign, value in ((1, 1), (-1, 2)):
        for h in SHARED:
            kind = jnp.where((hop & (N_ROW - 1)) == sign * h % N_ROW, value, kind)
    return jnp.where(col >= N_ROW * HALF, 0, kind)


def half_kernel(place_ref, row_ref, col_ref, v2_ref, line_ref, low_ref, high_ref, a_ref, b_ref, v0_ref, v1_ref, tiles_ref,
                part_ref, moments_ref, slots_ref, acc_ref):
    blocks = [line_ref[x] for x in range(N_X)] + [a_ref[0], b_ref[0], None, None, low_ref[...], high_ref[...]]
    for k, block in enumerate(blocks):
        if block is not None:
            spread(slots_ref, k, block)
    acc_ref[...] = jnp.zeros_like(acc_ref)
    for t in range(tiles_ref.shape[0]):
        kind = side(col_ref[t], place_ref)
        slot = jnp.where(kind == 2, 0, any_slot(col_ref[t], place_ref))
        acc_ref[kind * HALF + row_ref[t]] += product(slots_ref, slot, tiles_ref, t)
    doubled = []
    for h in range(HALF):
        part_ref[h] = acc_ref[h] + acc_ref[HALF + h]
        doubled.append(acc_ref[h] + 2.0 * acc_ref[HALF + h])
    vs = [v0_ref[...], v1_ref[...], v2_ref[...], jnp.concatenate(doubled, axis=1)]
    lane = lax.broadcasted_iota(jnp.int32, (Q, TILE), 1)
    packed = [jnp.zeros((Q, TILE), F32), jnp.zeros((Q, TILE), F32)]
    for m in range(6):
        prod = vs[m // 2] * vs[(m + 1) // 2]
        total = jnp.sum(prod[:, :TILE] + prod[:, TILE:], axis=1, keepdims=True)
        packed[m % 2] = jnp.where(lane == m // 2, total, packed[m % 2])
    moments_ref[...] = jnp.concatenate(packed, axis=0).T[:4]


def rest_kernel(place_ref, row_ref, col_ref, part_ref, swapped_ref, tiles_ref, out_ref, slots_ref, acc_ref):
    for k in range(len(SHARED)):
        spread(slots_ref, k, swapped_ref[k])
    acc_ref[...] = part_ref[...]
    for t in range(tiles_ref.shape[0]):
        @pl.when(side(col_ref[t], place_ref) == 2)
        def _():
            slot = any_slot(col_ref[t], place_ref) - (N_X + len(SHARED)) * HALF
            acc_ref[row_ref[t]] += product(slots_ref, slot, tiles_ref, t)
    store(acc_ref, out_ref)


def finish_kernel(moments_ref, v0_ref, v1_ref, v2_ref, v3_ref, diffused_ref, residual_ref):
    parts = [moments_ref[r] for r in range(N_REGION)]
    while len(parts) > 1:
        parts = [a + b for a, b in zip(parts[::2], parts[1::2])]
    square = jnp.concatenate([parts[0], jnp.zeros((TILE - 4, TILE), F32)], axis=0).T
    m = [square[(k % 2) * Q:(k % 2 + 1) * Q, k // 2:k // 2 + 1] for k in range(6)]
    g = [None] + [x / m[0] for x in m[1:]]
    d11 = g[2] - g[1] * g[1]
    d12 = g[3] - g[1] * g[2]
    d22 = g[4] - g[2] * g[2]
    f1 = g[4] - g[1] * g[3]
    f2 = g[5] - g[2] * g[3]
    ratio = d12 / d11
    c2 = -(f2 - ratio * f1) / (d22 - ratio * d12)
    c1 = -(f1 + d12 * c2) / d11
    c0 = -(g[3] + g[1] * c1 + g[2] * c2)
    e1 = TAU + c2
    e0 = e1 * TAU + c1
    scale = 1.0 / (e0 * TAU + c0)
    v0, v1, v2 = v0_ref[...], v1_ref[...], v2_ref[...]
    diffused_ref[...] = (TAU * scale) * (v2 + e1 * v1 + e0 * v0)
    residual_ref[...] = scale * (v3_ref[...] + c2 * v2 + c1 * v1 + c0 * v0)


SMEM = pl.BlockSpec(memory_space=pltpu.SMEM)
VMEM = pl.BlockSpec(memory_space=pltpu.VMEM)
HBM = pl.BlockSpec(memory_space=pltpu.MemorySpace.HBM)
PARAMS = pltpu.CompilerParams(vmem_limit_bytes=32 * 1024 * 1024)


def shape(*dims):
    return jax.ShapeDtypeStruct(dims, F32)


def local(queries, descriptors, candidates, cluster_perm, tile_vals, tile_row, tile_col):
    row_index = lax.axis_index("row").astype(jnp.int32)
    region = lax.axis_index("region").astype(jnp.int32)
    core = region & 1
    device = (region * N_ROW + row_index)[None]
    place = jnp.stack([row_index, 1 - 2 * core])

    index = jax.ShapeDtypeStruct(tile_row.shape, jnp.int32)
    packed, tile_row, tile_col = pl.pallas_call(
        pack_kernel, out_shape=(shape(N_ROW, QS, D + TILE), index, index), in_specs=[HBM] * 4, out_specs=(VMEM, SMEM, SMEM),
        scratch_shapes=[pltpu.VMEM(queries.shape, F32), pltpu.VMEM(cluster_perm.shape, jnp.int32),
                        pltpu.SemaphoreType.DMA((4,))],
        compiler_params=pltpu.CompilerParams(vmem_limit_bytes=64 * 1024 * 1024), name="pack",
    )(queries, cluster_perm, tile_row, tile_col)
    packed = lax.all_to_all(packed, "row", 0, 0, tiled=True).reshape(Q, D + TILE)
    by_query = pl.pallas_call(
        scores_kernel, out_shape=shape(N_ROW * QS * HALF, TILE), in_specs=[SMEM, VMEM, VMEM, VMEM], out_specs=VMEM,
        compiler_params=PARAMS, name="scores",
    )(device, packed, descriptors, candidates)
    table = lax.all_to_all(by_query.reshape(N_ROW, QS * HALF, TILE), "row", 0, 0, tiled=True)
    width = len(HOPS) * QS * HALF
    near = pl.pallas_call(
        permute_kernel, out_shape=shape(N_ROW * width, TILE), in_specs=[VMEM, VMEM], out_specs=VMEM,
        scratch_shapes=[pltpu.VMEM((QS, N_ROW * HALF, TILE), F32)],
        compiler_params=PARAMS, name="permute",
    )(table.reshape(N_ROW * QS * HALF, TILE), packed)
    near = lax.all_to_all(near.reshape(N_ROW, width, TILE), "row", 0, 0, tiled=True)
    v0 = near[:, :QS * HALF].reshape(N_ROW, QS, HALF, TILE).transpose(1, 0, 2, 3).reshape(Q, ROWS)

    def region_pair(v):
        return (lax.ppermute(v, "region", ring(N_REGION, 1)), lax.ppermute(v, "region", ring(N_REGION, -1)))

    def x_line(copies):
        return lax.all_to_all(
            copies, "row", 0, 0, tiled=True,
            axis_index_groups=[[x * N_Y + y for x in range(N_X)] for y in range(N_Y)])

    def fetch(v, copies):
        low, high = region_pair(v)
        line = x_line(copies)
        both = pl.pallas_call(
            pair_kernel, out_shape=shape(2, Q, ROWS), in_specs=[SMEM] + [VMEM] * 3, out_specs=VMEM,
            compiler_params=PARAMS, name="pair",
        )(core[None], v, low, high)
        got = []
        for hop in SHARED:
            pairs = [(r * N_ROW + i, r * N_ROW + (i - (hop if r % 2 == 0 else -hop)) % N_ROW)
                     for r in range(N_REGION) for i in range(N_ROW)]
            got.append(lax.ppermute(both, ("region", "row"), pairs))
        *got, line = lax.optimization_barrier((*got, line))
        return line, low, high, got

    def swap(got):
        swapped = pl.pallas_call(
            swap_kernel, out_shape=shape(len(got), Q, ROWS), in_specs=[VMEM] * len(got), out_specs=VMEM,
            compiler_params=PARAMS, name="swap",
        )(*got)
        return lax.ppermute(swapped, "region", [(r, r ^ 1) for r in range(N_REGION)])

    slots = pltpu.VMEM((SLOTS * HALF, Q, TILE), F32)
    acc = pltpu.VMEM((HALF, Q, TILE), F32)
    low, high = region_pair(v0)
    inner = pl.pallas_call(
        inner_kernel, out_shape=shape(HALF, Q, TILE), in_specs=[SMEM] * 3 + [VMEM] * 2, out_specs=VMEM,
        scratch_shapes=[pltpu.VMEM((len(HOPS) * HALF, Q, TILE), F32)],
        cost_estimate=pl.CostEstimate(flops=2 * 12 * Q * TILE * TILE, bytes_accessed=2000000, transcendentals=0),
        compiler_params=PARAMS, name="first_inner",
    )(place, tile_row, tile_col, near.reshape(N_ROW * width, TILE), tile_vals)
    with_copies = (shape(Q, ROWS), shape(N_X, Q, ROWS))
    v1, copies = pl.pallas_call(
        outer_kernel, out_shape=with_copies, in_specs=[SMEM] * 2 + [VMEM] * 4, out_specs=(VMEM, VMEM),
        scratch_shapes=[pltpu.VMEM((2 * HALF, Q, TILE), F32), acc], compiler_params=PARAMS, name="first_outer",
    )(tile_row, tile_col, inner, low, high, tile_vals)
    line, low, high, got = fetch(v1, copies)
    v2, copies = pl.pallas_call(
        next_kernel, out_shape=with_copies, in_specs=[SMEM] * 3 + [VMEM] * (N_BLOCKS + 1), out_specs=(VMEM, VMEM),
        scratch_shapes=[slots, acc], compiler_params=PARAMS, name="second",
    )(place, tile_row, tile_col, v1, line, *got, swap(got), low, high, tile_vals)
    line, low, high, got = fetch(v2, copies)
    part, moments = pl.pallas_call(
        half_kernel, out_shape=(shape(HALF, Q, TILE), shape(4, TILE)), in_specs=[SMEM] * 3 + [VMEM] * 9,
        out_specs=(VMEM, VMEM), scratch_shapes=[slots, pltpu.VMEM((3 * HALF, Q, TILE), F32)],
        compiler_params=PARAMS, name="half",
    )(place, tile_row, tile_col, v2, line, low, high, *got, v0, v1, tile_vals)
    *got, moments = lax.optimization_barrier((*got, moments))
    moments = lax.all_to_all(jnp.broadcast_to(moments[None], (N_ROW, 4, TILE)), "row", 0, 0, tiled=True)
    moments = jnp.sum(moments.reshape(2, 2, 2, 2, 2, 4, TILE).sum(0).sum(0).sum(0).sum(0), axis=0)
    v3 = pl.pallas_call(
        rest_kernel, out_shape=shape(Q, ROWS), in_specs=[SMEM] * 3 + [VMEM] * 3, out_specs=VMEM,
        scratch_shapes=[pltpu.VMEM((2 * HALF, Q, TILE), F32), acc],
        cost_estimate=pl.CostEstimate(flops=2 * 12 * Q * TILE * TILE, bytes_accessed=2000000, transcendentals=0),
        compiler_params=PARAMS, name="rest",
    )(place, tile_row, tile_col, part, swap(got), tile_vals)
    moments = lax.all_to_all(jnp.broadcast_to(moments[None], (N_REGION, 4, TILE)), "region", 0, 0, tiled=True)
    diffused, residual = pl.pallas_call(
        finish_kernel, out_shape=(shape(Q, ROWS), shape(Q, ROWS)), in_specs=[VMEM] * 5, out_specs=(VMEM, VMEM),
        compiler_params=PARAMS, name="finish",
    )(moments, v0, v1, v2, v3)
    return (diffused, residual)


def solution(mesh):
    in_specs = (
        P("row", None),
        P(("region", "row"), None),
        P(),
        P("region", "row"),
        P(("region", "row"), None, None),
        P(("region", "row")),
        P(("region", "row")),
    )
    out_specs = (P(None, ("region", "row")), P(None, ("region", "row")))
    return jax.shard_map(local, mesh=mesh, in_specs=in_specs, out_specs=out_specs, check_vma=False)
```

```python
import jax
import jax.numpy as jnp
from jax import lax
from jax.experimental import pallas as pl
from jax.experimental.pallas import tpu as pltpu
from jax.sharding import PartitionSpec as P

Q = 64
D = 512
TILE = 128
HALF = 2
ROWS = TILE * HALF
N_ROW = 32
N_REGION = 16
QS = Q // N_ROW
HOPS = (0, 1, -1, 3, -3, 8, -8, 16)
N_X = 4
N_Y = 8
SHARED = (1, 3)
SLOTS = len(HOPS) + 2
HIGHEST = lax.Precision.HIGHEST
F32 = jnp.float32
TAU = 1.0 / 0.9


def ring(count, hop):
    return [(i, (i + hop) % count) for i in range(count)]


def pack_kernel(queries_hbm, perm_hbm, row_hbm, col_hbm, out_ref, row_ref, col_ref, queries_ref, perm_ref, sems):
    pairs = ((queries_hbm, queries_ref), (perm_hbm, perm_ref), (row_hbm, row_ref), (col_hbm, col_ref))
    copies = [pltpu.make_async_copy(src, dst, sems.at[n]) for n, (src, dst) in enumerate(pairs)]
    for copy in copies:
        copy.start()
    for copy in copies:
        copy.wait()
    perm = perm_ref[...].astype(F32)
    out_ref[:, :, :D] = jnp.broadcast_to(queries_ref[...][None], (N_ROW, QS, D))
    for h in range(HALF):
        out_ref[:, h:h + 1, D:] = jnp.broadcast_to(perm[:, h * TILE:(h + 1) * TILE][None], (N_ROW, 1, TILE))


def scores_kernel(dev_ref, packed_ref, desc_ref, cand_ref, out_ref):
    scores = lax.dot_general(
        packed_ref[:, :D], desc_ref[...], (((1,), (1,)), ((), ())),
        precision=HIGHEST, preferred_element_type=F32,
    ) * (1.0 / (D ** 0.5))
    stored = jnp.exp(scores)
    cand = cand_ref[...]
    for h in range(HALF):
        hit = jnp.where(cand == dev_ref[0] * HALF + h, 1.0, 0.0)
        member = jnp.max(hit, axis=1, keepdims=True) > 0.5
        kept = jnp.where(member, stored[:, h * TILE:(h + 1) * TILE], 0.0)
        for q in range(QS):
            out_ref[pl.ds(q * HALF + h, N_ROW, stride=QS * HALF), :] = kept[q * N_ROW:(q + 1) * N_ROW]


GROUPS = 2


def permute_kernel(table_ref, packed_ref, out_ref, graph_ref):
    rows = N_ROW * HALF
    perm = packed_ref[:, D:].astype(jnp.int32)
    for first in range(0, rows, 8 * GROUPS):
        spans = [slice(first + 8 * g, first + 8 * g + 8) for g in range(GROUPS)]
        low = [perm[span] & (TILE - 1) for span in spans]
        high = [perm[span] >> 7 for span in spans]
        acc = [[jnp.zeros((8, TILE), F32) for _ in spans] for _ in range(QS)]
        for sender in range(N_ROW):
            for h in range(HALF):
                hits = [x == sender * HALF + h for x in high]
                for q in range(QS):
                    line = table_ref[(sender * QS + q) * HALF + h:(sender * QS + q) * HALF + h + 1, :]
                    line = jnp.broadcast_to(line, (8, TILE))
                    for g in range(GROUPS):
                        acc[q][g] = jnp.where(hits[g], jnp.take_along_axis(line, low[g], axis=1), acc[q][g])
        for q in range(QS):
            for g, span in enumerate(spans):
                graph_ref[q, span, :] = acc[q][g]
    width = len(HOPS) * QS * HALF
    for q in range(QS):
        for h in range(HALF):
            mine = graph_ref[q, pl.ds(h, N_ROW, stride=HALF), :]
            for k, hop in enumerate(HOPS):
                hop = hop % N_ROW
                rolled = mine if hop == 0 else jnp.concatenate([mine[hop:], mine[:hop]], axis=0)
                out_ref[pl.ds((k * QS + q) * HALF + h, N_ROW, stride=width), :] = rolled


def place(dev_ref):
    return dev_ref[0] & (N_ROW - 1), 1 - 2 * ((dev_ref[0] >> 5) & 1)


def near_slot(col, here):
    hop = ((col >> 1) - here[0]) & (N_ROW - 1)
    slot = jnp.int32(0)
    for k, h in enumerate(HOPS):
        slot = jnp.where(hop == h % N_ROW, k, slot)
    return slot * HALF + (col & 1)


def any_slot(col, here):
    owner = col >> 1
    hop = owner - here[0]
    slot = owner >> 3
    for k, h in enumerate(SHARED + tuple(-h for h in SHARED)):
        slot = jnp.where(((hop * here[1]) & (N_ROW - 1)) == h % N_ROW, N_X + k, slot)
    slot = slot * HALF + (col & 1)
    return jnp.where(col >= N_ROW * HALF, col - N_ROW * HALF + (N_X + 2 * len(SHARED)) * HALF, slot)


def split(x):
    high = x.astype(jnp.bfloat16)
    return high, (x - high.astype(F32)).astype(jnp.bfloat16)


def product(slots_ref, slot, tiles_ref, t):
    high, low = split(slots_ref[slot])
    tile_high, tile_low = split(tiles_ref[t])
    contract = (((1,), (1,)), ((), ()))
    both = lax.dot_general(jnp.concatenate([high, low], axis=0), tile_high, contract, preferred_element_type=F32)
    return both[:Q] + both[Q:] + lax.dot_general(high, tile_low, contract, preferred_element_type=F32)


def spread(slots_ref, k, block):
    for h in range(HALF):
        slots_ref[k * HALF + h] = block[:, h * TILE:(h + 1) * TILE]


def store(acc_ref, out_ref, copies_ref=None):
    for h in range(HALF):
        cols = slice(h * TILE, (h + 1) * TILE)
        out_ref[:, cols] = acc_ref[h]
        if copies_ref is not None:
            for x in range(N_X):
                copies_ref[x, :, cols] = acc_ref[h]


def inner_kernel(dev_ref, row_ref, col_ref, near_ref, tiles_ref, out_ref, slots_ref):
    width = len(HOPS) * QS * HALF
    for k in range(len(HOPS)):
        for h in range(HALF):
            for q in range(QS):
                slots_ref[k * HALF + h, q * N_ROW:(q + 1) * N_ROW, :] = near_ref[
                    pl.ds((k * QS + q) * HALF + h, N_ROW, stride=width), :]
    out_ref[...] = jnp.zeros_like(out_ref)
    for t in range(tiles_ref.shape[0]):
        inside = col_ref[t] < N_ROW * HALF
        slot = jnp.where(inside, near_slot(col_ref[t], place(dev_ref)), 0)
        out_ref[row_ref[t]] += jnp.where(inside, product(slots_ref, slot, tiles_ref, t), 0.0)


def outer_kernel(row_ref, col_ref, inner_ref, low_ref, high_ref, tiles_ref, out_ref, copies_ref, slots_ref, acc_ref):
    spread(slots_ref, 0, low_ref[...])
    spread(slots_ref, 1, high_ref[...])
    acc_ref[...] = inner_ref[...]
    for t in range(tiles_ref.shape[0]):
        @pl.when(col_ref[t] >= N_ROW * HALF)
        def _():
            acc_ref[row_ref[t]] += product(slots_ref, col_ref[t] - N_ROW * HALF, tiles_ref, t)
    store(acc_ref, out_ref, copies_ref)


def pair_kernel(dev_ref, own_ref, low_ref, high_ref, out_ref):
    out_ref[0] = own_ref[...]
    out_ref[1] = jnp.where(place(dev_ref)[1] == 1, high_ref[...], low_ref[...])


def swap_kernel(*refs):
    *got, out_ref = refs
    for k, ref in enumerate(got):
        out_ref[k] = ref[1]


N_BLOCKS = 7


def times_s(dev_ref, row_ref, col_ref, blocks, tiles_ref, slots_ref, acc_ref):
    _, line_ref, a_ref, b_ref, swapped_ref, low_ref, high_ref = blocks
    blocks = [line_ref[x] for x in range(N_X)] + [
        a_ref[0], b_ref[0], swapped_ref[0], swapped_ref[1], low_ref[...], high_ref[...]]
    for k, block in enumerate(blocks):
        spread(slots_ref, k, block)
    acc_ref[...] = jnp.zeros_like(acc_ref)
    for t in range(tiles_ref.shape[0]):
        acc_ref[row_ref[t]] += product(slots_ref, any_slot(col_ref[t], place(dev_ref)), tiles_ref, t)


def next_kernel(dev_ref, row_ref, col_ref, *refs):
    tiles_ref, out_ref, copies_ref, slots_ref, acc_ref = refs[N_BLOCKS:]
    times_s(dev_ref, row_ref, col_ref, refs[:N_BLOCKS], tiles_ref, slots_ref, acc_ref)
    store(acc_ref, out_ref, copies_ref)


def side(col, here):
    hop = ((col >> 1) - here[0]) * here[1]
    kind = jnp.int32(0)
    for sign, value in ((1, 1), (-1, 2)):
        for h in SHARED:
            kind = jnp.where((hop & (N_ROW - 1)) == sign * h % N_ROW, value, kind)
    return jnp.where(col >= N_ROW * HALF, 0, kind)


def half_kernel(dev_ref, row_ref, col_ref, v2_ref, line_ref, low_ref, high_ref, a_ref, b_ref, v0_ref, v1_ref, tiles_ref,
                part_ref, moments_ref, slots_ref, acc_ref):
    blocks = [line_ref[x] for x in range(N_X)] + [a_ref[0], b_ref[0], None, None, low_ref[...], high_ref[...]]
    for k, block in enumerate(blocks):
        if block is not None:
            spread(slots_ref, k, block)
    acc_ref[...] = jnp.zeros_like(acc_ref)
    for t in range(tiles_ref.shape[0]):
        kind = side(col_ref[t], place(dev_ref))
        slot = jnp.where(kind == 2, 0, any_slot(col_ref[t], place(dev_ref)))
        acc_ref[kind * HALF + row_ref[t]] += product(slots_ref, slot, tiles_ref, t)
    doubled = []
    for h in range(HALF):
        part_ref[h] = acc_ref[h] + acc_ref[HALF + h]
        doubled.append(acc_ref[h] + 2.0 * acc_ref[HALF + h])
    vs = [v0_ref[...], v1_ref[...], v2_ref[...], jnp.concatenate(doubled, axis=1)]
    lane = lax.broadcasted_iota(jnp.int32, (Q, TILE), 1)
    packed = [jnp.zeros((Q, TILE), F32), jnp.zeros((Q, TILE), F32)]
    for m in range(6):
        prod = vs[m // 2] * vs[(m + 1) // 2]
        total = jnp.sum(prod[:, :TILE] + prod[:, TILE:], axis=1, keepdims=True)
        packed[m % 2] = jnp.where(lane == m // 2, total, packed[m % 2])
    moments_ref[...] = jnp.concatenate(packed, axis=0).T[:4]


def rest_kernel(dev_ref, row_ref, col_ref, part_ref, swapped_ref, tiles_ref, out_ref, slots_ref, acc_ref):
    for k in range(len(SHARED)):
        spread(slots_ref, k, swapped_ref[k])
    acc_ref[...] = part_ref[...]
    for t in range(tiles_ref.shape[0]):
        @pl.when(side(col_ref[t], place(dev_ref)) == 2)
        def _():
            slot = any_slot(col_ref[t], place(dev_ref)) - (N_X + len(SHARED)) * HALF
            acc_ref[row_ref[t]] += product(slots_ref, slot, tiles_ref, t)
    store(acc_ref, out_ref)


def finish_kernel(moments_ref, v0_ref, v1_ref, v2_ref, v3_ref, diffused_ref, residual_ref):
    parts = [moments_ref[r] for r in range(N_REGION)]
    while len(parts) > 1:
        parts = [a + b for a, b in zip(parts[::2], parts[1::2])]
    square = jnp.concatenate([parts[0], jnp.zeros((TILE - 4, TILE), F32)], axis=0).T
    m = [square[(k % 2) * Q:(k % 2 + 1) * Q, k // 2:k // 2 + 1] for k in range(6)]
    g = [None] + [x / m[0] for x in m[1:]]
    d11 = g[2] - g[1] * g[1]
    d12 = g[3] - g[1] * g[2]
    d22 = g[4] - g[2] * g[2]
    f1 = g[4] - g[1] * g[3]
    f2 = g[5] - g[2] * g[3]
    ratio = d12 / d11
    c2 = -(f2 - ratio * f1) / (d22 - ratio * d12)
    c1 = -(f1 + d12 * c2) / d11
    c0 = -(g[3] + g[1] * c1 + g[2] * c2)
    e1 = TAU + c2
    e0 = e1 * TAU + c1
    scale = 1.0 / (e0 * TAU + c0)
    v0, v1, v2 = v0_ref[...], v1_ref[...], v2_ref[...]
    diffused_ref[...] = (TAU * scale) * (v2 + e1 * v1 + e0 * v0)
    residual_ref[...] = scale * (v3_ref[...] + c2 * v2 + c1 * v1 + c0 * v0)


SMEM = pl.BlockSpec(memory_space=pltpu.SMEM)
VMEM = pl.BlockSpec(memory_space=pltpu.VMEM)
HBM = pl.BlockSpec(memory_space=pltpu.MemorySpace.HBM)
PARAMS = pltpu.CompilerParams(vmem_limit_bytes=32 * 1024 * 1024)


def shape(*dims):
    return jax.ShapeDtypeStruct(dims, F32)


def local(queries, descriptors, candidates, cluster_perm, tile_vals, tile_row, tile_col):
    row_index = lax.axis_index("row").astype(jnp.int32)
    region = lax.axis_index("region").astype(jnp.int32)
    device = (region * N_ROW + row_index)[None]

    index = jax.ShapeDtypeStruct(tile_row.shape, jnp.int32)
    packed, tile_row, tile_col = pl.pallas_call(
        pack_kernel, out_shape=(shape(N_ROW, QS, D + TILE), index, index), in_specs=[HBM] * 4, out_specs=(VMEM, SMEM, SMEM),
        scratch_shapes=[pltpu.VMEM(queries.shape, F32), pltpu.VMEM(cluster_perm.shape, jnp.int32),
                        pltpu.SemaphoreType.DMA((4,))],
        compiler_params=pltpu.CompilerParams(vmem_limit_bytes=64 * 1024 * 1024), name="pack",
    )(queries, cluster_perm, tile_row, tile_col)
    packed = lax.all_to_all(packed, "row", 0, 0, tiled=True).reshape(Q, D + TILE)
    by_query = pl.pallas_call(
        scores_kernel, out_shape=shape(N_ROW * QS * HALF, TILE), in_specs=[SMEM, VMEM, VMEM, VMEM], out_specs=VMEM,
        compiler_params=PARAMS, name="scores",
    )(device, packed, descriptors, candidates)
    table = lax.all_to_all(by_query.reshape(N_ROW, QS * HALF, TILE), "row", 0, 0, tiled=True)
    width = len(HOPS) * QS * HALF
    near = pl.pallas_call(
        permute_kernel, out_shape=shape(N_ROW * width, TILE), in_specs=[VMEM, VMEM], out_specs=VMEM,
        scratch_shapes=[pltpu.VMEM((QS, N_ROW * HALF, TILE), F32)],
        compiler_params=PARAMS, name="permute",
    )(table.reshape(N_ROW * QS * HALF, TILE), packed)
    near = lax.all_to_all(near.reshape(N_ROW, width, TILE), "row", 0, 0, tiled=True)
    v0 = near[:, :QS * HALF].reshape(N_ROW, QS, HALF, TILE).transpose(1, 0, 2, 3).reshape(Q, ROWS)

    def region_pair(v):
        return (lax.ppermute(v, "region", ring(N_REGION, 1)), lax.ppermute(v, "region", ring(N_REGION, -1)))

    def x_line(copies):
        return lax.all_to_all(
            copies, "row", 0, 0, tiled=True,
            axis_index_groups=[[x * N_Y + y for x in range(N_X)] for y in range(N_Y)])

    def fetch(v, copies):
        low, high = region_pair(v)
        line = x_line(copies)
        both = pl.pallas_call(
            pair_kernel, out_shape=shape(2, Q, ROWS), in_specs=[SMEM] + [VMEM] * 3, out_specs=VMEM,
            compiler_params=PARAMS, name="pair",
        )(device, v, low, high)
        got = []
        for hop in SHARED:
            pairs = [(r * N_ROW + i, r * N_ROW + (i - (hop if r % 2 == 0 else -hop)) % N_ROW)
                     for r in range(N_REGION) for i in range(N_ROW)]
            got.append(lax.ppermute(both, ("region", "row"), pairs))
        *got, line = lax.optimization_barrier((*got, line))
        return line, low, high, got

    def swap(got):
        swapped = pl.pallas_call(
            swap_kernel, out_shape=shape(len(got), Q, ROWS), in_specs=[VMEM] * len(got), out_specs=VMEM,
            compiler_params=PARAMS, name="swap",
        )(*got)
        return lax.ppermute(swapped, "region", [(r, r ^ 1) for r in range(N_REGION)])

    slots = pltpu.VMEM((SLOTS * HALF, Q, TILE), F32)
    acc = pltpu.VMEM((HALF, Q, TILE), F32)
    low, high = region_pair(v0)
    inner = pl.pallas_call(
        inner_kernel, out_shape=shape(HALF, Q, TILE), in_specs=[SMEM] * 3 + [VMEM] * 2, out_specs=VMEM,
        scratch_shapes=[pltpu.VMEM((len(HOPS) * HALF, Q, TILE), F32)],
        cost_estimate=pl.CostEstimate(flops=2 * 12 * Q * TILE * TILE, bytes_accessed=2000000, transcendentals=0),
        compiler_params=PARAMS, name="first_inner",
    )(device, tile_row, tile_col, near.reshape(N_ROW * width, TILE), tile_vals)
    with_copies = (shape(Q, ROWS), shape(N_X, Q, ROWS))
    v1, copies = pl.pallas_call(
        outer_kernel, out_shape=with_copies, in_specs=[SMEM] * 2 + [VMEM] * 4, out_specs=(VMEM, VMEM),
        scratch_shapes=[pltpu.VMEM((2 * HALF, Q, TILE), F32), acc], compiler_params=PARAMS, name="first_outer",
    )(tile_row, tile_col, inner, low, high, tile_vals)
    line, low, high, got = fetch(v1, copies)
    v2, copies = pl.pallas_call(
        next_kernel, out_shape=with_copies, in_specs=[SMEM] * 3 + [VMEM] * (N_BLOCKS + 1), out_specs=(VMEM, VMEM),
        scratch_shapes=[slots, acc], compiler_params=PARAMS, name="second",
    )(device, tile_row, tile_col, v1, line, *got, swap(got), low, high, tile_vals)
    line, low, high, got = fetch(v2, copies)
    part, moments = pl.pallas_call(
        half_kernel, out_shape=(shape(HALF, Q, TILE), shape(4, TILE)), in_specs=[SMEM] * 3 + [VMEM] * 9,
        out_specs=(VMEM, VMEM), scratch_shapes=[slots, pltpu.VMEM((3 * HALF, Q, TILE), F32)],
        compiler_params=PARAMS, name="half",
    )(device, tile_row, tile_col, v2, line, low, high, *got, v0, v1, tile_vals)
    *got, moments = lax.optimization_barrier((*got, moments))
    moments = lax.all_to_all(jnp.broadcast_to(moments[None], (N_ROW, 4, TILE)), "row", 0, 0, tiled=True)
    moments = jnp.sum(moments.reshape(2, 2, 2, 2, 2, 4, TILE).sum(0).sum(0).sum(0).sum(0), axis=0)
    v3 = pl.pallas_call(
        rest_kernel, out_shape=shape(Q, ROWS), in_specs=[SMEM] * 3 + [VMEM] * 3, out_specs=VMEM,
        scratch_shapes=[pltpu.VMEM((2 * HALF, Q, TILE), F32), acc],
        cost_estimate=pl.CostEstimate(flops=2 * 12 * Q * TILE * TILE, bytes_accessed=2000000, transcendentals=0),
        compiler_params=PARAMS, name="rest",
    )(device, tile_row, tile_col, part, swap(got), tile_vals)
    moments = lax.all_to_all(jnp.broadcast_to(moments[None], (N_REGION, 4, TILE)), "region", 0, 0, tiled=True)
    diffused, residual = pl.pallas_call(
        finish_kernel, out_shape=(shape(Q, ROWS), shape(Q, ROWS)), in_specs=[VMEM] * 5, out_specs=(VMEM, VMEM),
        compiler_params=PARAMS, name="finish",
    )(moments, v0, v1, v2, v3)
    return (diffused, residual)


def solution(mesh):
    in_specs = (
        P("row", None),
        P(("region", "row"), None),
        P(),
        P("region", "row"),
        P(("region", "row"), None, None),
        P(("region", "row")),
        P(("region", "row")),
    )
    out_specs = (P(None, ("region", "row")), P(None, ("region", "row")))
    return jax.shard_map(local, mesh=mesh, in_specs=in_specs, out_specs=out_specs, check_vma=False)
```

```python
import jax
import jax.numpy as jnp
from jax import lax
from jax.experimental import pallas as pl
from jax.experimental.pallas import tpu as pltpu
from jax.sharding import PartitionSpec as P

Q = 64
D = 512
TILE = 128
HALF = 2
ROWS = TILE * HALF
N_ROW = 32
N_REGION = 16
QS = Q // N_ROW
HOPS = (0, 1, -1, 3, -3, 8, -8, 16)
N_X = 4
N_Y = 8
SHARED = (1, 3)
SLOTS = len(HOPS) + 2
HIGHEST = lax.Precision.HIGHEST
F32 = jnp.float32
TAU = 1.0 / 0.9


def ring(count, hop):
    return [(i, (i + hop) % count) for i in range(count)]


def pack_kernel(queries_hbm, perm_hbm, row_hbm, col_hbm, out_ref, row_ref, col_ref, queries_ref, perm_ref, sems):
    pairs = ((queries_hbm, queries_ref), (perm_hbm, perm_ref), (row_hbm, row_ref), (col_hbm, col_ref))
    copies = [pltpu.make_async_copy(src, dst, sems.at[n]) for n, (src, dst) in enumerate(pairs)]
    for copy in copies:
        copy.start()
    for copy in copies:
        copy.wait()
    perm = perm_ref[...].astype(F32)
    out_ref[:, :, :D] = jnp.broadcast_to(queries_ref[...][None], (N_ROW, QS, D))
    for h in range(HALF):
        out_ref[:, h:h + 1, D:] = jnp.broadcast_to(perm[:, h * TILE:(h + 1) * TILE][None], (N_ROW, 1, TILE))


def scores_kernel(dev_ref, packed_ref, desc_ref, cand_ref, out_ref):
    scores = lax.dot_general(
        packed_ref[:, :D], desc_ref[...], (((1,), (1,)), ((), ())),
        precision=HIGHEST, preferred_element_type=F32,
    ) * (1.0 / (D ** 0.5))
    stored = jnp.exp(scores)
    cand = cand_ref[...]
    for h in range(HALF):
        hit = jnp.where(cand == dev_ref[0] * HALF + h, 1.0, 0.0)
        member = jnp.max(hit, axis=1, keepdims=True) > 0.5
        kept = jnp.where(member, stored[:, h * TILE:(h + 1) * TILE], 0.0)
        for q in range(QS):
            out_ref[pl.ds(q * HALF + h, N_ROW, stride=QS * HALF), :] = kept[q * N_ROW:(q + 1) * N_ROW]


GROUPS = 2


def permute_kernel(table_ref, packed_ref, out_ref, graph_ref):
    rows = N_ROW * HALF
    perm = packed_ref[:, D:].astype(jnp.int32)
    for first in range(0, rows, 8 * GROUPS):
        spans = [slice(first + 8 * g, first + 8 * g + 8) for g in range(GROUPS)]
        low = [perm[span] & (TILE - 1) for span in spans]
        high = [perm[span] >> 7 for span in spans]
        acc = [[jnp.zeros((8, TILE), F32) for _ in spans] for _ in range(QS)]
        for sender in range(N_ROW):
            for h in range(HALF):
                hits = [x == sender * HALF + h for x in high]
                for q in range(QS):
                    line = table_ref[(sender * QS + q) * HALF + h:(sender * QS + q) * HALF + h + 1, :]
                    line = jnp.broadcast_to(line, (8, TILE))
                    for g in range(GROUPS):
                        acc[q][g] = jnp.where(hits[g], jnp.take_along_axis(line, low[g], axis=1), acc[q][g])
        for q in range(QS):
            for g, span in enumerate(spans):
                graph_ref[q, span, :] = acc[q][g]
    width = len(HOPS) * QS * HALF
    for q in range(QS):
        for h in range(HALF):
            mine = graph_ref[q, pl.ds(h, N_ROW, stride=HALF), :]
            for k, hop in enumerate(HOPS):
                hop = hop % N_ROW
                rolled = mine if hop == 0 else jnp.concatenate([mine[hop:], mine[:hop]], axis=0)
                out_ref[pl.ds((k * QS + q) * HALF + h, N_ROW, stride=width), :] = rolled


def place(dev_ref):
    return dev_ref[0] & (N_ROW - 1), 1 - 2 * ((dev_ref[0] >> 5) & 1)


def near_slot(col, here):
    hop = ((col >> 1) - here[0]) & (N_ROW - 1)
    slot = jnp.int32(0)
    for k, h in enumerate(HOPS):
        slot = jnp.where(hop == h % N_ROW, k, slot)
    return slot * HALF + (col & 1)


def any_slot(col, here):
    owner = col >> 1
    hop = owner - here[0]
    slot = owner >> 3
    for k, h in enumerate(SHARED + tuple(-h for h in SHARED)):
        slot = jnp.where(((hop * here[1]) & (N_ROW - 1)) == h % N_ROW, N_X + k, slot)
    slot = slot * HALF + (col & 1)
    return jnp.where(col >= N_ROW * HALF, col - N_ROW * HALF + (N_X + 2 * len(SHARED)) * HALF, slot)


def split(x):
    high = x.astype(jnp.bfloat16)
    return high, (x - high.astype(F32)).astype(jnp.bfloat16)


def product(slots_ref, slot, tiles_ref, t):
    high, low = split(slots_ref[slot])
    tile_high, tile_low = split(tiles_ref[t])
    contract = (((1,), (1,)), ((), ()))
    both = lax.dot_general(jnp.concatenate([high, low], axis=0), tile_high, contract, preferred_element_type=F32)
    return both[:Q] + both[Q:] + lax.dot_general(high, tile_low, contract, preferred_element_type=F32)


def spread(slots_ref, k, block):
    for h in range(HALF):
        slots_ref[k * HALF + h] = block[:, h * TILE:(h + 1) * TILE]


def store(acc_ref, out_ref, copies_ref=None):
    for h in range(HALF):
        cols = slice(h * TILE, (h + 1) * TILE)
        out_ref[:, cols] = acc_ref[h]
        if copies_ref is not None:
            for x in range(N_X):
                copies_ref[x, :, cols] = acc_ref[h]


def inner_kernel(dev_ref, row_ref, col_ref, near_ref, tiles_ref, out_ref, slots_ref):
    width = len(HOPS) * QS * HALF
    for k in range(len(HOPS)):
        for h in range(HALF):
            for q in range(QS):
                slots_ref[k * HALF + h, q * N_ROW:(q + 1) * N_ROW, :] = near_ref[
                    pl.ds((k * QS + q) * HALF + h, N_ROW, stride=width), :]
    out_ref[...] = jnp.zeros_like(out_ref)
    for t in range(tiles_ref.shape[0]):
        inside = col_ref[t] < N_ROW * HALF
        slot = jnp.where(inside, near_slot(col_ref[t], place(dev_ref)), 0)
        out_ref[row_ref[t]] += jnp.where(inside, product(slots_ref, slot, tiles_ref, t), 0.0)


def outer_kernel(row_ref, col_ref, inner_ref, low_ref, high_ref, tiles_ref, out_ref, copies_ref, slots_ref, acc_ref):
    spread(slots_ref, 0, low_ref[...])
    spread(slots_ref, 1, high_ref[...])
    acc_ref[...] = inner_ref[...]
    for t in range(tiles_ref.shape[0]):
        @pl.when(col_ref[t] >= N_ROW * HALF)
        def _():
            acc_ref[row_ref[t]] += product(slots_ref, col_ref[t] - N_ROW * HALF, tiles_ref, t)
    store(acc_ref, out_ref, copies_ref)


def pair_kernel(dev_ref, own_ref, low_ref, high_ref, out_ref):
    out_ref[0] = own_ref[...]
    out_ref[1] = jnp.where(place(dev_ref)[1] == 1, high_ref[...], low_ref[...])


def swap_kernel(*refs):
    *got, out_ref = refs
    for k, ref in enumerate(got):
        out_ref[k] = ref[1]


N_BLOCKS = 7


def times_s(dev_ref, row_ref, col_ref, blocks, tiles_ref, slots_ref, acc_ref):
    _, line_ref, a_ref, b_ref, swapped_ref, low_ref, high_ref = blocks
    blocks = [line_ref[x] for x in range(N_X)] + [
        a_ref[0], b_ref[0], swapped_ref[0], swapped_ref[1], low_ref[...], high_ref[...]]
    for k, block in enumerate(blocks):
        spread(slots_ref, k, block)
    acc_ref[...] = jnp.zeros_like(acc_ref)
    for t in range(tiles_ref.shape[0]):
        acc_ref[row_ref[t]] += product(slots_ref, any_slot(col_ref[t], place(dev_ref)), tiles_ref, t)


def next_kernel(dev_ref, row_ref, col_ref, *refs):
    tiles_ref, out_ref, copies_ref, slots_ref, acc_ref = refs[N_BLOCKS:]
    times_s(dev_ref, row_ref, col_ref, refs[:N_BLOCKS], tiles_ref, slots_ref, acc_ref)
    store(acc_ref, out_ref, copies_ref)


def side(col, here):
    hop = ((col >> 1) - here[0]) * here[1]
    kind = jnp.int32(0)
    for sign, value in ((1, 1), (-1, 2)):
        for h in SHARED:
            kind = jnp.where((hop & (N_ROW - 1)) == sign * h % N_ROW, value, kind)
    return jnp.where(col >= N_ROW * HALF, 0, kind)


def half_kernel(dev_ref, row_ref, col_ref, v2_ref, line_ref, low_ref, high_ref, a_ref, b_ref, v0_ref, v1_ref, tiles_ref,
                part_ref, moments_ref, slots_ref, acc_ref):
    blocks = [line_ref[x] for x in range(N_X)] + [a_ref[...], b_ref[...], None, None, low_ref[...], high_ref[...]]
    for k, block in enumerate(blocks):
        if block is not None:
            spread(slots_ref, k, block)
    acc_ref[...] = jnp.zeros_like(acc_ref)
    for t in range(tiles_ref.shape[0]):
        kind = side(col_ref[t], (place(dev_ref)[0], 1))
        slot = jnp.where(kind == 2, 0, any_slot(col_ref[t], (place(dev_ref)[0], 1)))
        acc_ref[kind * HALF + row_ref[t]] += product(slots_ref, slot, tiles_ref, t)
    doubled = []
    for h in range(HALF):
        part_ref[h] = acc_ref[h] + acc_ref[HALF + h]
        doubled.append(acc_ref[h] + 2.0 * acc_ref[HALF + h])
    vs = [v0_ref[...], v1_ref[...], v2_ref[...], jnp.concatenate(doubled, axis=1)]
    lane = lax.broadcasted_iota(jnp.int32, (Q, TILE), 1)
    packed = [jnp.zeros((Q, TILE), F32), jnp.zeros((Q, TILE), F32)]
    for m in range(6):
        prod = vs[m // 2] * vs[(m + 1) // 2]
        total = jnp.sum(prod[:, :TILE] + prod[:, TILE:], axis=1, keepdims=True)
        packed[m % 2] = jnp.where(lane == m // 2, total, packed[m % 2])
    moments_ref[...] = jnp.concatenate(packed, axis=0).T[:4]


def rest_kernel(dev_ref, row_ref, col_ref, part_ref, a_ref, b_ref, tiles_ref, out_ref, slots_ref, acc_ref):
    spread(slots_ref, 0, a_ref[...])
    spread(slots_ref, 1, b_ref[...])
    acc_ref[...] = part_ref[...]
    for t in range(tiles_ref.shape[0]):
        @pl.when(side(col_ref[t], (place(dev_ref)[0], 1)) == 2)
        def _():
            slot = any_slot(col_ref[t], (place(dev_ref)[0], 1)) - (N_X + len(SHARED)) * HALF
            acc_ref[row_ref[t]] += product(slots_ref, slot, tiles_ref, t)
    store(acc_ref, out_ref)


def finish_kernel(moments_ref, v0_ref, v1_ref, v2_ref, v3_ref, diffused_ref, residual_ref):
    parts = [moments_ref[r] for r in range(N_REGION)]
    while len(parts) > 1:
        parts = [a + b for a, b in zip(parts[::2], parts[1::2])]
    square = jnp.concatenate([parts[0], jnp.zeros((TILE - 4, TILE), F32)], axis=0).T
    m = [square[(k % 2) * Q:(k % 2 + 1) * Q, k // 2:k // 2 + 1] for k in range(6)]
    g = [None] + [x / m[0] for x in m[1:]]
    d11 = g[2] - g[1] * g[1]
    d12 = g[3] - g[1] * g[2]
    d22 = g[4] - g[2] * g[2]
    f1 = g[4] - g[1] * g[3]
    f2 = g[5] - g[2] * g[3]
    ratio = d12 / d11
    c2 = -(f2 - ratio * f1) / (d22 - ratio * d12)
    c1 = -(f1 + d12 * c2) / d11
    c0 = -(g[3] + g[1] * c1 + g[2] * c2)
    e1 = TAU + c2
    e0 = e1 * TAU + c1
    scale = 1.0 / (e0 * TAU + c0)
    v0, v1, v2 = v0_ref[...], v1_ref[...], v2_ref[...]
    diffused_ref[...] = (TAU * scale) * (v2 + e1 * v1 + e0 * v0)
    residual_ref[...] = scale * (v3_ref[...] + c2 * v2 + c1 * v1 + c0 * v0)


SMEM = pl.BlockSpec(memory_space=pltpu.SMEM)
VMEM = pl.BlockSpec(memory_space=pltpu.VMEM)
HBM = pl.BlockSpec(memory_space=pltpu.MemorySpace.HBM)
PARAMS = pltpu.CompilerParams(vmem_limit_bytes=32 * 1024 * 1024)


def shape(*dims):
    return jax.ShapeDtypeStruct(dims, F32)


def local(queries, descriptors, candidates, cluster_perm, tile_vals, tile_row, tile_col):
    row_index = lax.axis_index("row").astype(jnp.int32)
    region = lax.axis_index("region").astype(jnp.int32)
    device = (region * N_ROW + row_index)[None]

    index = jax.ShapeDtypeStruct(tile_row.shape, jnp.int32)
    packed, tile_row, tile_col = pl.pallas_call(
        pack_kernel, out_shape=(shape(N_ROW, QS, D + TILE), index, index), in_specs=[HBM] * 4, out_specs=(VMEM, SMEM, SMEM),
        scratch_shapes=[pltpu.VMEM(queries.shape, F32), pltpu.VMEM(cluster_perm.shape, jnp.int32),
                        pltpu.SemaphoreType.DMA((4,))],
        compiler_params=pltpu.CompilerParams(vmem_limit_bytes=64 * 1024 * 1024), name="pack",
    )(queries, cluster_perm, tile_row, tile_col)
    packed = lax.all_to_all(packed, "row", 0, 0, tiled=True).reshape(Q, D + TILE)
    by_query = pl.pallas_call(
        scores_kernel, out_shape=shape(N_ROW * QS * HALF, TILE), in_specs=[SMEM, VMEM, VMEM, VMEM], out_specs=VMEM,
        compiler_params=PARAMS, name="scores",
    )(device, packed, descriptors, candidates)
    table = lax.all_to_all(by_query.reshape(N_ROW, QS * HALF, TILE), "row", 0, 0, tiled=True)
    width = len(HOPS) * QS * HALF
    near = pl.pallas_call(
        permute_kernel, out_shape=shape(N_ROW * width, TILE), in_specs=[VMEM, VMEM], out_specs=VMEM,
        scratch_shapes=[pltpu.VMEM((QS, N_ROW * HALF, TILE), F32)],
        compiler_params=PARAMS, name="permute",
    )(table.reshape(N_ROW * QS * HALF, TILE), packed)
    near = lax.all_to_all(near.reshape(N_ROW, width, TILE), "row", 0, 0, tiled=True)
    v0 = near[:, :QS * HALF].reshape(N_ROW, QS, HALF, TILE).transpose(1, 0, 2, 3).reshape(Q, ROWS)

    def region_pair(v):
        return (lax.ppermute(v, "region", ring(N_REGION, 1)), lax.ppermute(v, "region", ring(N_REGION, -1)))

    def x_line(copies):
        return lax.all_to_all(
            copies, "row", 0, 0, tiled=True,
            axis_index_groups=[[x * N_Y + y for x in range(N_X)] for y in range(N_Y)])

    def fetch(v, copies):
        low, high = region_pair(v)
        line = x_line(copies)
        both = pl.pallas_call(
            pair_kernel, out_shape=shape(2, Q, ROWS), in_specs=[SMEM] + [VMEM] * 3, out_specs=VMEM,
            compiler_params=PARAMS, name="pair",
        )(device, v, low, high)
        got = []
        for hop in SHARED:
            pairs = [(r * N_ROW + i, r * N_ROW + (i - (hop if r % 2 == 0 else -hop)) % N_ROW)
                     for r in range(N_REGION) for i in range(N_ROW)]
            got.append(lax.ppermute(both, ("region", "row"), pairs))
        *got, line = lax.optimization_barrier((*got, line))
        return line, low, high, got

    def swap(got):
        swapped = pl.pallas_call(
            swap_kernel, out_shape=shape(len(got), Q, ROWS), in_specs=[VMEM] * len(got), out_specs=VMEM,
            compiler_params=PARAMS, name="swap",
        )(*got)
        return lax.ppermute(swapped, "region", [(r, r ^ 1) for r in range(N_REGION)])

    slots = pltpu.VMEM((SLOTS * HALF, Q, TILE), F32)
    acc = pltpu.VMEM((HALF, Q, TILE), F32)
    low, high = region_pair(v0)
    inner = pl.pallas_call(
        inner_kernel, out_shape=shape(HALF, Q, TILE), in_specs=[SMEM] * 3 + [VMEM] * 2, out_specs=VMEM,
        scratch_shapes=[pltpu.VMEM((len(HOPS) * HALF, Q, TILE), F32)],
        cost_estimate=pl.CostEstimate(flops=2 * 12 * Q * TILE * TILE, bytes_accessed=2000000, transcendentals=0),
        compiler_params=PARAMS, name="first_inner",
    )(device, tile_row, tile_col, near.reshape(N_ROW * width, TILE), tile_vals)
    with_copies = (shape(Q, ROWS), shape(N_X, Q, ROWS))
    v1, copies = pl.pallas_call(
        outer_kernel, out_shape=with_copies, in_specs=[SMEM] * 2 + [VMEM] * 4, out_specs=(VMEM, VMEM),
        scratch_shapes=[pltpu.VMEM((2 * HALF, Q, TILE), F32), acc], compiler_params=PARAMS, name="first_outer",
    )(tile_row, tile_col, inner, low, high, tile_vals)
    line, low, high, got = fetch(v1, copies)
    v2, copies = pl.pallas_call(
        next_kernel, out_shape=with_copies, in_specs=[SMEM] * 3 + [VMEM] * (N_BLOCKS + 1), out_specs=(VMEM, VMEM),
        scratch_shapes=[slots, acc], compiler_params=PARAMS, name="second",
    )(device, tile_row, tile_col, v1, line, *got, swap(got), low, high, tile_vals)
    low, high = region_pair(v2)
    ahead = [lax.ppermute(v2, "row", ring(N_ROW, -hop)) for hop in SHARED]
    part, moments = pl.pallas_call(
        half_kernel, out_shape=(shape(HALF, Q, TILE), shape(4, TILE)), in_specs=[SMEM] * 3 + [VMEM] * 9,
        out_specs=(VMEM, VMEM), scratch_shapes=[slots, pltpu.VMEM((3 * HALF, Q, TILE), F32)],
        compiler_params=PARAMS, name="half",
    )(device, tile_row, tile_col, v2, x_line(copies), low, high, *ahead, v0, v1, tile_vals)
    later, moments = lax.optimization_barrier((v2, moments))
    behind = [lax.ppermute(later, "row", ring(N_ROW, hop)) for hop in SHARED]
    moments = lax.all_to_all(jnp.broadcast_to(moments[None], (N_ROW, 4, TILE)), "row", 0, 0, tiled=True)
    moments = jnp.sum(moments.reshape(2, 2, 2, 2, 2, 4, TILE).sum(0).sum(0).sum(0).sum(0), axis=0)
    v3 = pl.pallas_call(
        rest_kernel, out_shape=shape(Q, ROWS), in_specs=[SMEM] * 3 + [VMEM] * 4, out_specs=VMEM,
        scratch_shapes=[pltpu.VMEM((2 * HALF, Q, TILE), F32), acc],
        cost_estimate=pl.CostEstimate(flops=2 * 12 * Q * TILE * TILE, bytes_accessed=2000000, transcendentals=0),
        compiler_params=PARAMS, name="rest",
    )(device, tile_row, tile_col, part, *behind, tile_vals)
    moments = lax.all_to_all(jnp.broadcast_to(moments[None], (N_REGION, 4, TILE)), "region", 0, 0, tiled=True)
    diffused, residual = pl.pallas_call(
        finish_kernel, out_shape=(shape(Q, ROWS), shape(Q, ROWS)), in_specs=[VMEM] * 5, out_specs=(VMEM, VMEM),
        compiler_params=PARAMS, name="finish",
    )(moments, v0, v1, v2, v3)
    return (diffused, residual)


def solution(mesh):
    in_specs = (
        P("row", None),
        P(("region", "row"), None),
        P(),
        P("region", "row"),
        P(("region", "row"), None, None),
        P(("region", "row")),
        P(("region", "row")),
    )
    out_specs = (P(None, ("region", "row")), P(None, ("region", "row")))
    return jax.shard_map(local, mesh=mesh, in_specs=in_specs, out_specs=out_specs, check_vma=False)
```

```python
import jax
import jax.numpy as jnp
from jax import lax
from jax.experimental import pallas as pl
from jax.experimental.pallas import tpu as pltpu
from jax.sharding import PartitionSpec as P

Q = 64
D = 512
TILE = 128
HALF = 2
ROWS = TILE * HALF
N_ROW = 32
N_REGION = 16
QS = Q // N_ROW
HOPS = (0, 1, -1, 3, -3, 8, -8, 16)
N_X = 4
N_Y = 8
SHARED = (3, 1)
SLOTS = len(HOPS) + 2
HIGHEST = lax.Precision.HIGHEST
F32 = jnp.float32
TAU = 1.0 / 0.9


def ring(count, hop):
    return [(i, (i + hop) % count) for i in range(count)]


def pack_kernel(queries_hbm, perm_hbm, row_hbm, col_hbm, out_ref, row_ref, col_ref, queries_ref, perm_ref, sems):
    pairs = ((queries_hbm, queries_ref), (perm_hbm, perm_ref), (row_hbm, row_ref), (col_hbm, col_ref))
    copies = [pltpu.make_async_copy(src, dst, sems.at[n]) for n, (src, dst) in enumerate(pairs)]
    for copy in copies:
        copy.start()
    for copy in copies:
        copy.wait()
    perm = perm_ref[...].astype(F32)
    out_ref[:, :, :D] = jnp.broadcast_to(queries_ref[...][None], (N_ROW, QS, D))
    for h in range(HALF):
        out_ref[:, h:h + 1, D:] = jnp.broadcast_to(perm[:, h * TILE:(h + 1) * TILE][None], (N_ROW, 1, TILE))


def scores_kernel(dev_ref, packed_ref, desc_ref, cand_ref, out_ref):
    scores = lax.dot_general(
        packed_ref[:, :D], desc_ref[...], (((1,), (1,)), ((), ())),
        precision=HIGHEST, preferred_element_type=F32,
    ) * (1.0 / (D ** 0.5))
    stored = jnp.exp(scores)
    cand = cand_ref[...]
    for h in range(HALF):
        hit = jnp.where(cand == dev_ref[0] * HALF + h, 1.0, 0.0)
        member = jnp.max(hit, axis=1, keepdims=True) > 0.5
        kept = jnp.where(member, stored[:, h * TILE:(h + 1) * TILE], 0.0)
        for q in range(QS):
            out_ref[pl.ds(q * HALF + h, N_ROW, stride=QS * HALF), :] = kept[q * N_ROW:(q + 1) * N_ROW]


GROUPS = 2


def permute_kernel(table_ref, packed_ref, out_ref, graph_ref):
    rows = N_ROW * HALF
    perm = packed_ref[:, D:].astype(jnp.int32)
    for first in range(0, rows, 8 * GROUPS):
        spans = [slice(first + 8 * g, first + 8 * g + 8) for g in range(GROUPS)]
        low = [perm[span] & (TILE - 1) for span in spans]
        high = [perm[span] >> 7 for span in spans]
        acc = [[jnp.zeros((8, TILE), F32) for _ in spans] for _ in range(QS)]
        for sender in range(N_ROW):
            for h in range(HALF):
                hits = [x == sender * HALF + h for x in high]
                for q in range(QS):
                    line = table_ref[(sender * QS + q) * HALF + h:(sender * QS + q) * HALF + h + 1, :]
                    line = jnp.broadcast_to(line, (8, TILE))
                    for g in range(GROUPS):
                        acc[q][g] = jnp.where(hits[g], jnp.take_along_axis(line, low[g], axis=1), acc[q][g])
        for q in range(QS):
            for g, span in enumerate(spans):
                graph_ref[q, span, :] = acc[q][g]
    width = len(HOPS) * QS * HALF
    for q in range(QS):
        for h in range(HALF):
            mine = graph_ref[q, pl.ds(h, N_ROW, stride=HALF), :]
            for k, hop in enumerate(HOPS):
                hop = hop % N_ROW
                rolled = mine if hop == 0 else jnp.concatenate([mine[hop:], mine[:hop]], axis=0)
                out_ref[pl.ds((k * QS + q) * HALF + h, N_ROW, stride=width), :] = rolled


def place(dev_ref):
    return dev_ref[0] & (N_ROW - 1), 1 - 2 * ((dev_ref[0] >> 5) & 1)


def near_slot(col, here):
    hop = ((col >> 1) - here[0]) & (N_ROW - 1)
    slot = jnp.int32(0)
    for k, h in enumerate(HOPS):
        slot = jnp.where(hop == h % N_ROW, k, slot)
    return slot * HALF + (col & 1)


def any_slot(col, here):
    owner = col >> 1
    hop = owner - here[0]
    slot = owner >> 3
    for k, h in enumerate(SHARED + tuple(-h for h in SHARED)):
        slot = jnp.where(((hop * here[1]) & (N_ROW - 1)) == h % N_ROW, N_X + k, slot)
    slot = slot * HALF + (col & 1)
    return jnp.where(col >= N_ROW * HALF, col - N_ROW * HALF + (N_X + 2 * len(SHARED)) * HALF, slot)


def split(x):
    high = x.astype(jnp.bfloat16)
    return high, (x - high.astype(F32)).astype(jnp.bfloat16)


def product(slots_ref, slot, tiles_ref, t):
    high, low = split(slots_ref[slot])
    tile_high, tile_low = split(tiles_ref[t])
    contract = (((1,), (1,)), ((), ()))
    both = lax.dot_general(jnp.concatenate([high, low], axis=0), tile_high, contract, preferred_element_type=F32)
    return both[:Q] + both[Q:] + lax.dot_general(high, tile_low, contract, preferred_element_type=F32)


def spread(slots_ref, k, block):
    for h in range(HALF):
        slots_ref[k * HALF + h] = block[:, h * TILE:(h + 1) * TILE]


def store(acc_ref, out_ref, copies_ref=None):
    for h in range(HALF):
        cols = slice(h * TILE, (h + 1) * TILE)
        out_ref[:, cols] = acc_ref[h]
        if copies_ref is not None:
            for x in range(N_X):
                copies_ref[x, :, cols] = acc_ref[h]


def inner_kernel(dev_ref, row_ref, col_ref, near_ref, tiles_ref, out_ref, slots_ref):
    width = len(HOPS) * QS * HALF
    for k in range(len(HOPS)):
        for h in range(HALF):
            for q in range(QS):
                slots_ref[k * HALF + h, q * N_ROW:(q + 1) * N_ROW, :] = near_ref[
                    pl.ds((k * QS + q) * HALF + h, N_ROW, stride=width), :]
    out_ref[...] = jnp.zeros_like(out_ref)
    for t in range(tiles_ref.shape[0]):
        inside = col_ref[t] < N_ROW * HALF
        slot = jnp.where(inside, near_slot(col_ref[t], place(dev_ref)), 0)
        out_ref[row_ref[t]] += jnp.where(inside, product(slots_ref, slot, tiles_ref, t), 0.0)


def outer_kernel(row_ref, col_ref, inner_ref, low_ref, high_ref, tiles_ref, out_ref, copies_ref, slots_ref, acc_ref):
    spread(slots_ref, 0, low_ref[...])
    spread(slots_ref, 1, high_ref[...])
    acc_ref[...] = inner_ref[...]
    for t in range(tiles_ref.shape[0]):
        @pl.when(col_ref[t] >= N_ROW * HALF)
        def _():
            acc_ref[row_ref[t]] += product(slots_ref, col_ref[t] - N_ROW * HALF, tiles_ref, t)
    store(acc_ref, out_ref, copies_ref)


def pair_kernel(dev_ref, own_ref, low_ref, high_ref, out_ref):
    out_ref[0] = own_ref[...]
    out_ref[1] = jnp.where(place(dev_ref)[1] == 1, high_ref[...], low_ref[...])


def swap_kernel(*refs):
    *got, out_ref = refs
    for k, ref in enumerate(got):
        out_ref[k] = ref[1]


N_BLOCKS = 7


def times_s(dev_ref, row_ref, col_ref, blocks, tiles_ref, slots_ref, acc_ref):
    _, line_ref, a_ref, b_ref, swapped_ref, low_ref, high_ref = blocks
    blocks = [line_ref[x] for x in range(N_X)] + [
        a_ref[0], b_ref[0], swapped_ref[0], swapped_ref[1], low_ref[...], high_ref[...]]
    for k, block in enumerate(blocks):
        spread(slots_ref, k, block)
    acc_ref[...] = jnp.zeros_like(acc_ref)
    for t in range(tiles_ref.shape[0]):
        acc_ref[row_ref[t]] += product(slots_ref, any_slot(col_ref[t], place(dev_ref)), tiles_ref, t)


def next_kernel(dev_ref, row_ref, col_ref, *refs):
    tiles_ref, out_ref, copies_ref, slots_ref, acc_ref = refs[N_BLOCKS:]
    times_s(dev_ref, row_ref, col_ref, refs[:N_BLOCKS], tiles_ref, slots_ref, acc_ref)
    store(acc_ref, out_ref, copies_ref)


def side(col, here):
    hop = ((col >> 1) - here[0]) * here[1]
    kind = jnp.int32(0)
    for sign, value in ((1, 1), (-1, 2)):
        for h in SHARED:
            kind = jnp.where((hop & (N_ROW - 1)) == sign * h % N_ROW, value, kind)
    return jnp.where(col >= N_ROW * HALF, 0, kind)


def half_kernel(dev_ref, row_ref, col_ref, v2_ref, line_ref, low_ref, high_ref, a_ref, b_ref, v0_ref, v1_ref, tiles_ref,
                part_ref, moments_ref, slots_ref, acc_ref):
    blocks = [line_ref[x] for x in range(N_X)] + [a_ref[...], b_ref[...], None, None, low_ref[...], high_ref[...]]
    for k, block in enumerate(blocks):
        if block is not None:
            spread(slots_ref, k, block)
    acc_ref[...] = jnp.zeros_like(acc_ref)
    for t in range(tiles_ref.shape[0]):
        kind = side(col_ref[t], (place(dev_ref)[0], 1))
        slot = jnp.where(kind == 2, 0, any_slot(col_ref[t], (place(dev_ref)[0], 1)))
        acc_ref[kind * HALF + row_ref[t]] += product(slots_ref, slot, tiles_ref, t)
    doubled = []
    for h in range(HALF):
        part_ref[h] = acc_ref[h] + acc_ref[HALF + h]
        doubled.append(acc_ref[h] + 2.0 * acc_ref[HALF + h])
    vs = [v0_ref[...], v1_ref[...], v2_ref[...], jnp.concatenate(doubled, axis=1)]
    lane = lax.broadcasted_iota(jnp.int32, (Q, TILE), 1)
    packed = [jnp.zeros((Q, TILE), F32), jnp.zeros((Q, TILE), F32)]
    for m in range(6):
        prod = vs[m // 2] * vs[(m + 1) // 2]
        total = jnp.sum(prod[:, :TILE] + prod[:, TILE:], axis=1, keepdims=True)
        packed[m % 2] = jnp.where(lane == m // 2, total, packed[m % 2])
    moments_ref[...] = jnp.concatenate(packed, axis=0).T[:4]


def rest_kernel(dev_ref, row_ref, col_ref, part_ref, a_ref, b_ref, tiles_ref, out_ref, slots_ref, acc_ref):
    spread(slots_ref, 0, a_ref[...])
    spread(slots_ref, 1, b_ref[...])
    acc_ref[...] = part_ref[...]
    for t in range(tiles_ref.shape[0]):
        @pl.when(side(col_ref[t], (place(dev_ref)[0], 1)) == 2)
        def _():
            slot = any_slot(col_ref[t], (place(dev_ref)[0], 1)) - (N_X + len(SHARED)) * HALF
            acc_ref[row_ref[t]] += product(slots_ref, slot, tiles_ref, t)
    store(acc_ref, out_ref)


def finish_kernel(moments_ref, v0_ref, v1_ref, v2_ref, v3_ref, diffused_ref, residual_ref):
    parts = [moments_ref[r] for r in range(N_REGION)]
    while len(parts) > 1:
        parts = [a + b for a, b in zip(parts[::2], parts[1::2])]
    square = jnp.concatenate([parts[0], jnp.zeros((TILE - 4, TILE), F32)], axis=0).T
    m = [square[(k % 2) * Q:(k % 2 + 1) * Q, k // 2:k // 2 + 1] for k in range(6)]
    g = [None] + [x / m[0] for x in m[1:]]
    d11 = g[2] - g[1] * g[1]
    d12 = g[3] - g[1] * g[2]
    d22 = g[4] - g[2] * g[2]
    f1 = g[4] - g[1] * g[3]
    f2 = g[5] - g[2] * g[3]
    ratio = d12 / d11
    c2 = -(f2 - ratio * f1) / (d22 - ratio * d12)
    c1 = -(f1 + d12 * c2) / d11
    c0 = -(g[3] + g[1] * c1 + g[2] * c2)
    e1 = TAU + c2
    e0 = e1 * TAU + c1
    scale = 1.0 / (e0 * TAU + c0)
    v0, v1, v2 = v0_ref[...], v1_ref[...], v2_ref[...]
    diffused_ref[...] = (TAU * scale) * (v2 + e1 * v1 + e0 * v0)
    residual_ref[...] = scale * (v3_ref[...] + c2 * v2 + c1 * v1 + c0 * v0)


SMEM = pl.BlockSpec(memory_space=pltpu.SMEM)
VMEM = pl.BlockSpec(memory_space=pltpu.VMEM)
HBM = pl.BlockSpec(memory_space=pltpu.MemorySpace.HBM)
PARAMS = pltpu.CompilerParams(vmem_limit_bytes=32 * 1024 * 1024)


def shape(*dims):
    return jax.ShapeDtypeStruct(dims, F32)


def local(queries, descriptors, candidates, cluster_perm, tile_vals, tile_row, tile_col):
    row_index = lax.axis_index("row").astype(jnp.int32)
    region = lax.axis_index("region").astype(jnp.int32)
    device = (region * N_ROW + row_index)[None]

    index = jax.ShapeDtypeStruct(tile_row.shape, jnp.int32)
    packed, tile_row, tile_col = pl.pallas_call(
        pack_kernel, out_shape=(shape(N_ROW, QS, D + TILE), index, index), in_specs=[HBM] * 4, out_specs=(VMEM, SMEM, SMEM),
        scratch_shapes=[pltpu.VMEM(queries.shape, F32), pltpu.VMEM(cluster_perm.shape, jnp.int32),
                        pltpu.SemaphoreType.DMA((4,))],
        compiler_params=pltpu.CompilerParams(vmem_limit_bytes=64 * 1024 * 1024), name="pack",
    )(queries, cluster_perm, tile_row, tile_col)
    packed = lax.all_to_all(packed, "row", 0, 0, tiled=True).reshape(Q, D + TILE)
    by_query = pl.pallas_call(
        scores_kernel, out_shape=shape(N_ROW * QS * HALF, TILE), in_specs=[SMEM, VMEM, VMEM, VMEM], out_specs=VMEM,
        compiler_params=PARAMS, name="scores",
    )(device, packed, descriptors, candidates)
    table = lax.all_to_all(by_query.reshape(N_ROW, QS * HALF, TILE), "row", 0, 0, tiled=True)
    width = len(HOPS) * QS * HALF
    near = pl.pallas_call(
        permute_kernel, out_shape=shape(N_ROW * width, TILE), in_specs=[VMEM, VMEM], out_specs=VMEM,
        scratch_shapes=[pltpu.VMEM((QS, N_ROW * HALF, TILE), F32)],
        compiler_params=PARAMS, name="permute",
    )(table.reshape(N_ROW * QS * HALF, TILE), packed)
    near = lax.all_to_all(near.reshape(N_ROW, width, TILE), "row", 0, 0, tiled=True)
    v0 = near[:, :QS * HALF].reshape(N_ROW, QS, HALF, TILE).transpose(1, 0, 2, 3).reshape(Q, ROWS)

    def region_pair(v):
        return (lax.ppermute(v, "region", ring(N_REGION, 1)), lax.ppermute(v, "region", ring(N_REGION, -1)))

    def x_line(copies):
        return lax.all_to_all(
            copies, "row", 0, 0, tiled=True,
            axis_index_groups=[[x * N_Y + y for x in range(N_X)] for y in range(N_Y)])

    def fetch(v, copies):
        low, high = region_pair(v)
        line = x_line(copies)
        both = pl.pallas_call(
            pair_kernel, out_shape=shape(2, Q, ROWS), in_specs=[SMEM] + [VMEM] * 3, out_specs=VMEM,
            compiler_params=PARAMS, name="pair",
        )(device, v, low, high)
        got = []
        for hop in SHARED:
            pairs = [(r * N_ROW + i, r * N_ROW + (i - (hop if r % 2 == 0 else -hop)) % N_ROW)
                     for r in range(N_REGION) for i in range(N_ROW)]
            got.append(lax.ppermute(both, ("region", "row"), pairs))
        *got, line = lax.optimization_barrier((*got, line))
        return line, low, high, got

    def swap(got):
        swapped = pl.pallas_call(
            swap_kernel, out_shape=shape(len(got), Q, ROWS), in_specs=[VMEM] * len(got), out_specs=VMEM,
            compiler_params=PARAMS, name="swap",
        )(*got)
        return lax.ppermute(swapped, "region", [(r, r ^ 1) for r in range(N_REGION)])

    slots = pltpu.VMEM((SLOTS * HALF, Q, TILE), F32)
    acc = pltpu.VMEM((HALF, Q, TILE), F32)
    low, high = region_pair(v0)
    inner = pl.pallas_call(
        inner_kernel, out_shape=shape(HALF, Q, TILE), in_specs=[SMEM] * 3 + [VMEM] * 2, out_specs=VMEM,
        scratch_shapes=[pltpu.VMEM((len(HOPS) * HALF, Q, TILE), F32)],
        cost_estimate=pl.CostEstimate(flops=2 * 12 * Q * TILE * TILE, bytes_accessed=2000000, transcendentals=0),
        compiler_params=PARAMS, name="first_inner",
    )(device, tile_row, tile_col, near.reshape(N_ROW * width, TILE), tile_vals)
    with_copies = (shape(Q, ROWS), shape(N_X, Q, ROWS))
    v1, copies = pl.pallas_call(
        outer_kernel, out_shape=with_copies, in_specs=[SMEM] * 2 + [VMEM] * 4, out_specs=(VMEM, VMEM),
        scratch_shapes=[pltpu.VMEM((2 * HALF, Q, TILE), F32), acc], compiler_params=PARAMS, name="first_outer",
    )(tile_row, tile_col, inner, low, high, tile_vals)
    line, low, high, got = fetch(v1, copies)
    v2, copies = pl.pallas_call(
        next_kernel, out_shape=with_copies, in_specs=[SMEM] * 3 + [VMEM] * (N_BLOCKS + 1), out_specs=(VMEM, VMEM),
        scratch_shapes=[slots, acc], compiler_params=PARAMS, name="second",
    )(device, tile_row, tile_col, v1, line, *got, swap(got), low, high, tile_vals)
    low, high = region_pair(v2)
    ahead = [lax.ppermute(v2, "row", ring(N_ROW, -hop)) for hop in SHARED]
    part, moments = pl.pallas_call(
        half_kernel, out_shape=(shape(HALF, Q, TILE), shape(4, TILE)), in_specs=[SMEM] * 3 + [VMEM] * 9,
        out_specs=(VMEM, VMEM), scratch_shapes=[slots, pltpu.VMEM((3 * HALF, Q, TILE), F32)],
        compiler_params=PARAMS, name="half",
    )(device, tile_row, tile_col, v2, x_line(copies), low, high, *ahead, v0, v1, tile_vals)
    later, moments = lax.optimization_barrier((v2, moments))
    behind = [lax.ppermute(later, "row", ring(N_ROW, hop)) for hop in SHARED]
    moments = lax.all_to_all(jnp.broadcast_to(moments[None], (N_ROW, 4, TILE)), "row", 0, 0, tiled=True)
    moments = jnp.sum(moments.reshape(2, 2, 2, 2, 2, 4, TILE).sum(0).sum(0).sum(0).sum(0), axis=0)
    v3 = pl.pallas_call(
        rest_kernel, out_shape=shape(Q, ROWS), in_specs=[SMEM] * 3 + [VMEM] * 4, out_specs=VMEM,
        scratch_shapes=[pltpu.VMEM((2 * HALF, Q, TILE), F32), acc],
        cost_estimate=pl.CostEstimate(flops=2 * 12 * Q * TILE * TILE, bytes_accessed=2000000, transcendentals=0),
        compiler_params=PARAMS, name="rest",
    )(device, tile_row, tile_col, part, *behind, tile_vals)
    moments = lax.all_to_all(jnp.broadcast_to(moments[None], (N_REGION, 4, TILE)), "region", 0, 0, tiled=True)
    diffused, residual = pl.pallas_call(
        finish_kernel, out_shape=(shape(Q, ROWS), shape(Q, ROWS)), in_specs=[VMEM] * 5, out_specs=(VMEM, VMEM),
        compiler_params=PARAMS, name="finish",
    )(moments, v0, v1, v2, v3)
    return (diffused, residual)


def solution(mesh):
    in_specs = (
        P("row", None),
        P(("region", "row"), None),
        P(),
        P("region", "row"),
        P(("region", "row"), None, None),
        P(("region", "row")),
        P(("region", "row")),
    )
    out_specs = (P(None, ("region", "row")), P(None, ("region", "row")))
    return jax.shard_map(local, mesh=mesh, in_specs=in_specs, out_specs=out_specs, check_vma=False)
```

```python
import jax
import jax.numpy as jnp
from jax import lax
from jax.experimental import pallas as pl
from jax.experimental.pallas import tpu as pltpu
from jax.sharding import PartitionSpec as P

Q = 64
D = 512
TILE = 128
HALF = 2
ROWS = TILE * HALF
N_ROW = 32
N_REGION = 16
QS = Q // N_ROW
HOPS = (0, 1, -1, 3, -3, 8, -8, 16)
N_X = 4
N_Y = 8
SHARED = (1, 3)
SLOTS = len(HOPS) + 2
HIGHEST = lax.Precision.HIGHEST
F32 = jnp.float32
TAU = 1.0 / 0.9


def ring(count, hop):
    return [(i, (i + hop) % count) for i in range(count)]


def pack_kernel(queries_hbm, perm_hbm, row_hbm, col_hbm, out_ref, where_ref, queries_ref, perm_ref, row_ref, col_ref, sems):
    pairs = ((queries_hbm, queries_ref), (perm_hbm, perm_ref), (row_hbm, row_ref), (col_hbm, col_ref))
    copies = [pltpu.make_async_copy(src, dst, sems.at[n]) for n, (src, dst) in enumerate(pairs)]
    for copy in copies:
        copy.start()
    for copy in copies:
        copy.wait()
    count = row_ref.shape[0]
    for t in range(count):
        where_ref[t] = row_ref[t]
        where_ref[count + t] = col_ref[t]
    perm = perm_ref[...].astype(F32)
    out_ref[:, :, :D] = jnp.broadcast_to(queries_ref[...][None], (N_ROW, QS, D))
    for h in range(HALF):
        out_ref[:, h:h + 1, D:] = jnp.broadcast_to(perm[:, h * TILE:(h + 1) * TILE][None], (N_ROW, 1, TILE))


def scores_kernel(dev_ref, packed_ref, desc_ref, cand_ref, out_ref):
    scores = lax.dot_general(
        packed_ref[:, :D], desc_ref[...], (((1,), (1,)), ((), ())),
        precision=HIGHEST, preferred_element_type=F32,
    ) * (1.0 / (D ** 0.5))
    stored = jnp.exp(scores)
    cand = cand_ref[...]
    for h in range(HALF):
        hit = jnp.where(cand == dev_ref[0] * HALF + h, 1.0, 0.0)
        member = jnp.max(hit, axis=1, keepdims=True) > 0.5
        kept = jnp.where(member, stored[:, h * TILE:(h + 1) * TILE], 0.0)
        for q in range(QS):
            out_ref[pl.ds(q * HALF + h, N_ROW, stride=QS * HALF), :] = kept[q * N_ROW:(q + 1) * N_ROW]


GROUPS = 2


def permute_kernel(table_ref, packed_ref, out_ref, graph_ref):
    rows = N_ROW * HALF
    perm = packed_ref[:, D:].astype(jnp.int32)
    for first in range(0, rows, 8 * GROUPS):
        spans = [slice(first + 8 * g, first + 8 * g + 8) for g in range(GROUPS)]
        low = [perm[span] & (TILE - 1) for span in spans]
        high = [perm[span] >> 7 for span in spans]
        acc = [[jnp.zeros((8, TILE), F32) for _ in spans] for _ in range(QS)]
        for sender in range(N_ROW):
            for h in range(HALF):
                hits = [x == sender * HALF + h for x in high]
                for q in range(QS):
                    line = table_ref[(sender * QS + q) * HALF + h:(sender * QS + q) * HALF + h + 1, :]
                    line = jnp.broadcast_to(line, (8, TILE))
                    for g in range(GROUPS):
                        acc[q][g] = jnp.where(hits[g], jnp.take_along_axis(line, low[g], axis=1), acc[q][g])
        for q in range(QS):
            for g, span in enumerate(spans):
                graph_ref[q, span, :] = acc[q][g]
    width = len(HOPS) * QS * HALF
    for q in range(QS):
        for h in range(HALF):
            mine = graph_ref[q, pl.ds(h, N_ROW, stride=HALF), :]
            for k, hop in enumerate(HOPS):
                hop = hop % N_ROW
                rolled = mine if hop == 0 else jnp.concatenate([mine[hop:], mine[:hop]], axis=0)
                out_ref[pl.ds((k * QS + q) * HALF + h, N_ROW, stride=width), :] = rolled


def place(dev_ref):
    return dev_ref[0] & (N_ROW - 1), 1 - 2 * ((dev_ref[0] >> 5) & 1)


def near_slot(col, here):
    hop = ((col >> 1) - here[0]) & (N_ROW - 1)
    slot = jnp.int32(0)
    for k, h in enumerate(HOPS):
        slot = jnp.where(hop == h % N_ROW, k, slot)
    return slot * HALF + (col & 1)


def any_slot(col, here):
    owner = col >> 1
    hop = owner - here[0]
    slot = owner >> 3
    for k, h in enumerate(SHARED + tuple(-h for h in SHARED)):
        slot = jnp.where(((hop * here[1]) & (N_ROW - 1)) == h % N_ROW, N_X + k, slot)
    slot = slot * HALF + (col & 1)
    return jnp.where(col >= N_ROW * HALF, col - N_ROW * HALF + (N_X + 2 * len(SHARED)) * HALF, slot)


def split(x):
    high = x.astype(jnp.bfloat16)
    return high, (x - high.astype(F32)).astype(jnp.bfloat16)


def product(slots_ref, slot, tiles_ref, t):
    high, low = split(slots_ref[slot])
    tile_high, tile_low = split(tiles_ref[t])
    contract = (((1,), (1,)), ((), ()))
    both = lax.dot_general(jnp.concatenate([high, low], axis=0), tile_high, contract, preferred_element_type=F32)
    return both[:Q] + both[Q:] + lax.dot_general(high, tile_low, contract, preferred_element_type=F32)


def spread(slots_ref, k, block):
    for h in range(HALF):
        slots_ref[k * HALF + h] = block[:, h * TILE:(h + 1) * TILE]


def store(acc_ref, out_ref, copies_ref=None):
    for h in range(HALF):
        cols = slice(h * TILE, (h + 1) * TILE)
        out_ref[:, cols] = acc_ref[h]
        if copies_ref is not None:
            for x in range(N_X):
                copies_ref[x, :, cols] = acc_ref[h]


def inner_kernel(dev_ref, where_ref, near_ref, tiles_ref, out_ref, slots_ref):
    width = len(HOPS) * QS * HALF
    for k in range(len(HOPS)):
        for h in range(HALF):
            for q in range(QS):
                slots_ref[k * HALF + h, q * N_ROW:(q + 1) * N_ROW, :] = near_ref[
                    pl.ds((k * QS + q) * HALF + h, N_ROW, stride=width), :]
    out_ref[...] = jnp.zeros_like(out_ref)
    for t in range(tiles_ref.shape[0]):
        inside = where_ref[tiles_ref.shape[0] + t] < N_ROW * HALF
        slot = jnp.where(inside, near_slot(where_ref[tiles_ref.shape[0] + t], place(dev_ref)), 0)
        out_ref[where_ref[t]] += jnp.where(inside, product(slots_ref, slot, tiles_ref, t), 0.0)


def outer_kernel(where_ref, inner_ref, low_ref, high_ref, tiles_ref, out_ref, copies_ref, slots_ref, acc_ref):
    spread(slots_ref, 0, low_ref[...])
    spread(slots_ref, 1, high_ref[...])
    acc_ref[...] = inner_ref[...]
    for t in range(tiles_ref.shape[0]):
        @pl.when(where_ref[tiles_ref.shape[0] + t] >= N_ROW * HALF)
        def _():
            acc_ref[where_ref[t]] += product(slots_ref, where_ref[tiles_ref.shape[0] + t] - N_ROW * HALF, tiles_ref, t)
    store(acc_ref, out_ref, copies_ref)


def pair_kernel(dev_ref, own_ref, low_ref, high_ref, out_ref):
    out_ref[0] = own_ref[...]
    out_ref[1] = jnp.where(place(dev_ref)[1] == 1, high_ref[...], low_ref[...])


def swap_kernel(*refs):
    *got, out_ref = refs
    for k, ref in enumerate(got):
        out_ref[k] = ref[1]


N_BLOCKS = 7


def times_s(dev_ref, where_ref, blocks, tiles_ref, slots_ref, acc_ref):
    _, line_ref, a_ref, b_ref, swapped_ref, low_ref, high_ref = blocks
    blocks = [line_ref[x] for x in range(N_X)] + [
        a_ref[0], b_ref[0], swapped_ref[0], swapped_ref[1], low_ref[...], high_ref[...]]
    for k, block in enumerate(blocks):
        spread(slots_ref, k, block)
    acc_ref[...] = jnp.zeros_like(acc_ref)
    for t in range(tiles_ref.shape[0]):
        acc_ref[where_ref[t]] += product(slots_ref, any_slot(where_ref[tiles_ref.shape[0] + t], place(dev_ref)), tiles_ref, t)


def next_kernel(dev_ref, where_ref, *refs):
    tiles_ref, out_ref, copies_ref, slots_ref, acc_ref = refs[N_BLOCKS:]
    times_s(dev_ref, where_ref, refs[:N_BLOCKS], tiles_ref, slots_ref, acc_ref)
    store(acc_ref, out_ref, copies_ref)


def side(col, here):
    hop = ((col >> 1) - here[0]) * here[1]
    kind = jnp.int32(0)
    for sign, value in ((1, 1), (-1, 2)):
        for h in SHARED:
            kind = jnp.where((hop & (N_ROW - 1)) == sign * h % N_ROW, value, kind)
    return jnp.where(col >= N_ROW * HALF, 0, kind)


def half_kernel(dev_ref, where_ref, v2_ref, line_ref, low_ref, high_ref, a_ref, b_ref, v0_ref, v1_ref, tiles_ref,
                part_ref, moments_ref, slots_ref, acc_ref):
    blocks = [line_ref[x] for x in range(N_X)] + [a_ref[...], b_ref[...], None, None, low_ref[...], high_ref[...]]
    for k, block in enumerate(blocks):
        if block is not None:
            spread(slots_ref, k, block)
    acc_ref[...] = jnp.zeros_like(acc_ref)
    for t in range(tiles_ref.shape[0]):
        kind = side(where_ref[tiles_ref.shape[0] + t], (place(dev_ref)[0], 1))
        slot = jnp.where(kind == 2, 0, any_slot(where_ref[tiles_ref.shape[0] + t], (place(dev_ref)[0], 1)))
        acc_ref[kind * HALF + where_ref[t]] += product(slots_ref, slot, tiles_ref, t)
    doubled = []
    for h in range(HALF):
        part_ref[h] = acc_ref[h] + acc_ref[HALF + h]
        doubled.append(acc_ref[h] + 2.0 * acc_ref[HALF + h])
    vs = [v0_ref[...], v1_ref[...], v2_ref[...], jnp.concatenate(doubled, axis=1)]
    lane = lax.broadcasted_iota(jnp.int32, (Q, TILE), 1)
    packed = [jnp.zeros((Q, TILE), F32), jnp.zeros((Q, TILE), F32)]
    for m in range(6):
        prod = vs[m // 2] * vs[(m + 1) // 2]
        total = jnp.sum(prod[:, :TILE] + prod[:, TILE:], axis=1, keepdims=True)
        packed[m % 2] = jnp.where(lane == m // 2, total, packed[m % 2])
    moments_ref[...] = jnp.concatenate(packed, axis=0).T[:4]


def rest_kernel(dev_ref, where_ref, part_ref, a_ref, b_ref, tiles_ref, out_ref, slots_ref, acc_ref):
    spread(slots_ref, 0, a_ref[...])
    spread(slots_ref, 1, b_ref[...])
    acc_ref[...] = part_ref[...]
    for t in range(tiles_ref.shape[0]):
        @pl.when(side(where_ref[tiles_ref.shape[0] + t], (place(dev_ref)[0], 1)) == 2)
        def _():
            slot = any_slot(where_ref[tiles_ref.shape[0] + t], (place(dev_ref)[0], 1)) - (N_X + len(SHARED)) * HALF
            acc_ref[where_ref[t]] += product(slots_ref, slot, tiles_ref, t)
    store(acc_ref, out_ref)


def finish_kernel(moments_ref, v0_ref, v1_ref, v2_ref, v3_ref, diffused_ref, residual_ref):
    parts = [moments_ref[r] for r in range(N_REGION)]
    while len(parts) > 1:
        parts = [a + b for a, b in zip(parts[::2], parts[1::2])]
    square = jnp.concatenate([parts[0], jnp.zeros((TILE - 4, TILE), F32)], axis=0).T
    m = [square[(k % 2) * Q:(k % 2 + 1) * Q, k // 2:k // 2 + 1] for k in range(6)]
    g = [None] + [x / m[0] for x in m[1:]]
    d11 = g[2] - g[1] * g[1]
    d12 = g[3] - g[1] * g[2]
    d22 = g[4] - g[2] * g[2]
    f1 = g[4] - g[1] * g[3]
    f2 = g[5] - g[2] * g[3]
    ratio = d12 / d11
    c2 = -(f2 - ratio * f1) / (d22 - ratio * d12)
    c1 = -(f1 + d12 * c2) / d11
    c0 = -(g[3] + g[1] * c1 + g[2] * c2)
    e1 = TAU + c2
    e0 = e1 * TAU + c1
    scale = 1.0 / (e0 * TAU + c0)
    v0, v1, v2 = v0_ref[...], v1_ref[...], v2_ref[...]
    diffused_ref[...] = (TAU * scale) * (v2 + e1 * v1 + e0 * v0)
    residual_ref[...] = scale * (v3_ref[...] + c2 * v2 + c1 * v1 + c0 * v0)


SMEM = pl.BlockSpec(memory_space=pltpu.SMEM)
VMEM = pl.BlockSpec(memory_space=pltpu.VMEM)
HBM = pl.BlockSpec(memory_space=pltpu.MemorySpace.HBM)
PARAMS = pltpu.CompilerParams(vmem_limit_bytes=32 * 1024 * 1024)


def shape(*dims):
    return jax.ShapeDtypeStruct(dims, F32)


def local(queries, descriptors, candidates, cluster_perm, tile_vals, tile_row, tile_col):
    row_index = lax.axis_index("row").astype(jnp.int32)
    region = lax.axis_index("region").astype(jnp.int32)
    device = (region * N_ROW + row_index)[None]

    index = jax.ShapeDtypeStruct((2 * tile_row.shape[0],), jnp.int32)
    packed, where = pl.pallas_call(
        pack_kernel, out_shape=(shape(N_ROW, QS, D + TILE), index), in_specs=[HBM] * 4, out_specs=(VMEM, SMEM),
        scratch_shapes=[pltpu.VMEM(queries.shape, F32), pltpu.VMEM(cluster_perm.shape, jnp.int32),
                        pltpu.SMEM(tile_row.shape, jnp.int32), pltpu.SMEM(tile_col.shape, jnp.int32),
                        pltpu.SemaphoreType.DMA((4,))],
        compiler_params=pltpu.CompilerParams(vmem_limit_bytes=64 * 1024 * 1024), name="pack",
    )(queries, cluster_perm, tile_row, tile_col)
    packed = lax.all_to_all(packed, "row", 0, 0, tiled=True).reshape(Q, D + TILE)
    by_query = pl.pallas_call(
        scores_kernel, out_shape=shape(N_ROW * QS * HALF, TILE), in_specs=[SMEM, VMEM, VMEM, VMEM], out_specs=VMEM,
        compiler_params=PARAMS, name="scores",
    )(device, packed, descriptors, candidates)
    table = lax.all_to_all(by_query.reshape(N_ROW, QS * HALF, TILE), "row", 0, 0, tiled=True)
    width = len(HOPS) * QS * HALF
    near = pl.pallas_call(
        permute_kernel, out_shape=shape(N_ROW * width, TILE), in_specs=[VMEM, VMEM], out_specs=VMEM,
        scratch_shapes=[pltpu.VMEM((QS, N_ROW * HALF, TILE), F32)],
        compiler_params=PARAMS, name="permute",
    )(table.reshape(N_ROW * QS * HALF, TILE), packed)
    near = lax.all_to_all(near.reshape(N_ROW, width, TILE), "row", 0, 0, tiled=True)
    v0 = near[:, :QS * HALF].reshape(N_ROW, QS, HALF, TILE).transpose(1, 0, 2, 3).reshape(Q, ROWS)

    def region_pair(v):
        return (lax.ppermute(v, "region", ring(N_REGION, 1)), lax.ppermute(v, "region", ring(N_REGION, -1)))

    def x_line(copies):
        return lax.all_to_all(
            copies, "row", 0, 0, tiled=True,
            axis_index_groups=[[x * N_Y + y for x in range(N_X)] for y in range(N_Y)])

    def fetch(v, copies):
        low, high = region_pair(v)
        line = x_line(copies)
        both = pl.pallas_call(
            pair_kernel, out_shape=shape(2, Q, ROWS), in_specs=[SMEM] + [VMEM] * 3, out_specs=VMEM,
            compiler_params=PARAMS, name="pair",
        )(device, v, low, high)
        got = []
        for hop in SHARED:
            pairs = [(r * N_ROW + i, r * N_ROW + (i - (hop if r % 2 == 0 else -hop)) % N_ROW)
                     for r in range(N_REGION) for i in range(N_ROW)]
            got.append(lax.ppermute(both, ("region", "row"), pairs))
        *got, line = lax.optimization_barrier((*got, line))
        return line, low, high, got

    def swap(got):
        swapped = pl.pallas_call(
            swap_kernel, out_shape=shape(len(got), Q, ROWS), in_specs=[VMEM] * len(got), out_specs=VMEM,
            compiler_params=PARAMS, name="swap",
        )(*got)
        return lax.ppermute(swapped, "region", [(r, r ^ 1) for r in range(N_REGION)])

    slots = pltpu.VMEM((SLOTS * HALF, Q, TILE), F32)
    acc = pltpu.VMEM((HALF, Q, TILE), F32)
    low, high = region_pair(v0)
    inner = pl.pallas_call(
        inner_kernel, out_shape=shape(HALF, Q, TILE), in_specs=[SMEM] * 2 + [VMEM] * 2, out_specs=VMEM,
        scratch_shapes=[pltpu.VMEM((len(HOPS) * HALF, Q, TILE), F32)],
        cost_estimate=pl.CostEstimate(flops=2 * 12 * Q * TILE * TILE, bytes_accessed=2000000, transcendentals=0),
        compiler_params=PARAMS, name="first_inner",
    )(device, where, near.reshape(N_ROW * width, TILE), tile_vals)
    with_copies = (shape(Q, ROWS), shape(N_X, Q, ROWS))
    v1, copies = pl.pallas_call(
        outer_kernel, out_shape=with_copies, in_specs=[SMEM] + [VMEM] * 4, out_specs=(VMEM, VMEM),
        scratch_shapes=[pltpu.VMEM((2 * HALF, Q, TILE), F32), acc], compiler_params=PARAMS, name="first_outer",
    )(where, inner, low, high, tile_vals)
    line, low, high, got = fetch(v1, copies)
    v2, copies = pl.pallas_call(
        next_kernel, out_shape=with_copies, in_specs=[SMEM] * 2 + [VMEM] * (N_BLOCKS + 1), out_specs=(VMEM, VMEM),
        scratch_shapes=[slots, acc], compiler_params=PARAMS, name="second",
    )(device, where, v1, line, *got, swap(got), low, high, tile_vals)
    low, high = region_pair(v2)
    ahead = [lax.ppermute(v2, "row", ring(N_ROW, -hop)) for hop in SHARED]
    part, moments = pl.pallas_call(
        half_kernel, out_shape=(shape(HALF, Q, TILE), shape(4, TILE)), in_specs=[SMEM] * 2 + [VMEM] * 9,
        out_specs=(VMEM, VMEM), scratch_shapes=[slots, pltpu.VMEM((3 * HALF, Q, TILE), F32)],
        compiler_params=PARAMS, name="half",
    )(device, where, v2, x_line(copies), low, high, *ahead, v0, v1, tile_vals)
    later, moments = lax.optimization_barrier((v2, moments))
    behind = [lax.ppermute(later, "row", ring(N_ROW, hop)) for hop in SHARED]
    moments = lax.all_to_all(jnp.broadcast_to(moments[None], (N_ROW, 4, TILE)), "row", 0, 0, tiled=True)
    moments = jnp.sum(moments.reshape(2, 2, 2, 2, 2, 4, TILE).sum(0).sum(0).sum(0).sum(0), axis=0)
    v3 = pl.pallas_call(
        rest_kernel, out_shape=shape(Q, ROWS), in_specs=[SMEM] * 2 + [VMEM] * 4, out_specs=VMEM,
        scratch_shapes=[pltpu.VMEM((2 * HALF, Q, TILE), F32), acc],
        cost_estimate=pl.CostEstimate(flops=2 * 12 * Q * TILE * TILE, bytes_accessed=2000000, transcendentals=0),
        compiler_params=PARAMS, name="rest",
    )(device, where, part, *behind, tile_vals)
    moments = lax.all_to_all(jnp.broadcast_to(moments[None], (N_REGION, 4, TILE)), "region", 0, 0, tiled=True)
    diffused, residual = pl.pallas_call(
        finish_kernel, out_shape=(shape(Q, ROWS), shape(Q, ROWS)), in_specs=[VMEM] * 5, out_specs=(VMEM, VMEM),
        compiler_params=PARAMS, name="finish",
    )(moments, v0, v1, v2, v3)
    return (diffused, residual)


def solution(mesh):
    in_specs = (
        P("row", None),
        P(("region", "row"), None),
        P(),
        P("region", "row"),
        P(("region", "row"), None, None),
        P(("region", "row")),
        P(("region", "row")),
    )
    out_specs = (P(None, ("region", "row")), P(None, ("region", "row")))
    return jax.shard_map(local, mesh=mesh, in_specs=in_specs, out_specs=out_specs, check_vma=False)
```
